32 devices in a mesh: dp: 2 (over y), ctx: 4 (over x, core), tensor: 4 (over z).
Axes of the slice: x: 2, y: 2, z: 4, core: 2. Of those that a mesh axis runs over, the one named last changes fastest.
Arguments:
- hidden: bfloat16 [2, 1920, 2048], P('dp', 'ctx'), may hold values from -6 to 6
- cotangent: bfloat16 [2, 1920, 2048], P('dp', 'ctx'), may hold values from -6 to 6
- gain_attn: bfloat16 [2048], P(('dp', 'ctx')), may hold values from 0.5 to 1.5
- query_weight: bfloat16 [2048, 4096], P(('dp', 'ctx'), 'tensor'), may hold values from -0.125 to 0.125
- key_weight: bfloat16 [2048, 512], P(('dp', 'ctx'), 'tensor'), may hold values from -0.125 to 0.125
- value_weight: bfloat16 [2048, 512], P(('dp', 'ctx'), 'tensor'), may hold values from -0.125 to 0.125
- gain_query: bfloat16 [128], P(('dp', 'ctx')), may hold values from 0.25 to 1.75
- gain_key: bfloat16 [128], P(('dp', 'ctx')), may hold values from 0.25 to 1.75
- out_weight: bfloat16 [4096, 2048], P('tensor', ('dp', 'ctx')), may hold values from -0.75 to 0.75
- gain_moe: bfloat16 [2048], P(('dp', 'ctx')), may hold values from 0.5 to 1.5
- router_weight: bfloat16 [2048, 16], P(('dp', 'ctx')), may hold values from -0.0625 to 0.0625
- gate_weight: bfloat16 [16, 2048, 768], P(None, ('dp', 'ctx'), 'tensor'), may hold values from -0.125 to 0.125
- up_weight: bfloat16 [16, 2048, 768], P(None, ('dp', 'ctx'), 'tensor'), may hold values from -0.125 to 0.125
- down_weight: bfloat16 [16, 768, 2048], P(None, 'tensor', ('dp', 'ctx')), may hold values from -0.875 to 0.875
- segment: int32 [2, 1920], P('dp'), may hold values from 0 to 12, as said below
- parent: int32 [2, 13], P('dp'), may hold values from 0 to 12, as said below
- tree_depth: int32 [2, 1920], P('dp', 'ctx'), may hold values from 0 to 1119, as said below
- routes: int32 [2, 1920, 8], P('dp', 'ctx'), may hold values from 0 to 15, all different within a row; in each aligned block of 480 rows (0 to 479, 480 to 959, ..., all dimensions but the last counted through in order) at most 320 rows name the same one
Outputs:
- output: bfloat16 [2, 1920, 2048], P('dp', 'ctx')
- grad_hidden: bfloat16 [2, 1920, 2048], P('dp', 'ctx')
- grad_gain_attn: float32 [2048], P(('dp', 'ctx'))
- grad_query_weight: float32 [2048, 4096], P(('dp', 'ctx'), 'tensor')
- grad_key_weight: float32 [2048, 512], P(('dp', 'ctx'), 'tensor')
- grad_value_weight: float32 [2048, 512], P(('dp', 'ctx'), 'tensor')
- grad_gain_query: float32 [128], P(('dp', 'ctx'))
- grad_gain_key: float32 [128], P(('dp', 'ctx'))
- grad_out_weight: float32 [4096, 2048], P('tensor', ('dp', 'ctx'))
- grad_gain_moe: float32 [2048], P(('dp', 'ctx'))
- grad_router_weight: float32 [2048, 16], P(('dp', 'ctx'))
- grad_gate_weight: float32 [16, 2048, 768], P(None, ('dp', 'ctx'), 'tensor')
- grad_up_weight: float32 [16, 2048, 768], P(None, ('dp', 'ctx'), 'tensor')
- grad_down_weight: float32 [16, 768, 2048], P(None, 'tensor', ('dp', 'ctx'))
The draws below stay inside these ranges and needn't reach their ends.
Inputs may be any that keep to these rules, and one draw needn't show every extreme that they name: Within a tree, tokens of one segment stand together: the trunk first, then each branch followed by its two leaves; a segment's ancestors stand before it. The trunk is its own parent; the four branches have the trunk as parent, and each branch is the parent of two leaves. `tree_depth`: A token's place on the path from its tree's first token: trunk tokens count from 0, a branch continues after the 896 trunk tokens, a leaf after its branch's 128. `routes`: 8 different experts a token; among the 480 tokens of one device's part of a tree, no expert is named by more than 320 rows; in some of these parts of every draw an expert is named exactly 320 times.
All inputs are finite; a program needn't handle non-finite values.
Results may differ from the reference program's by a relative error of at most 0.03.
Values may be sent and summed in bfloat16 or wider, within the bound.
No kernel may reach another device: no remote copies, remote signals or barrier semaphores. Data moves between devices by JAX's collectives and lax.ppermute only.
A program may use at most 448 MiB of HBM per device.

```python
import math
import jax
import jax.numpy as jnp
import numpy as np
from jax import lax

D = 2048
HEADS_Q = 32
HEADS_KV = 4
HEAD = 128
FF = 768
TOP = 8
EXPERTS = 16
TRUNK = 896
BRANCH = 128
LEAF = 64
SEGMENTS = 13
TREE = 1920
TREES = 2
CAPACITY = 320
N_CTX = 4


def tree_layout(key):
    tree_keys = jax.random.split(key, TREES)
    parent_layout = jnp.array(np.array([0, 0, 1, 1, 0, 4, 4, 0, 7, 7, 0, 10, 10], np.int32))
    base_layout = jnp.array([0] + [TRUNK, TRUNK + BRANCH, TRUNK + BRANCH] * 4, jnp.int32)

    def single(tree_key):
        label_key, leaf_key = jax.random.split(tree_key)
        labels = jax.random.permutation(label_key, SEGMENTS).astype(jnp.int32)
        top_label = jnp.int32(SEGMENTS - 1)
        slot_range = jnp.arange(SEGMENTS, dtype=jnp.int32)
        top_slot = jnp.sum(jnp.where(labels == top_label, slot_range, 0)).astype(jnp.int32)
        first_branch = labels[1]
        labels = jnp.where(slot_range == top_slot, first_branch, labels)
        labels = jnp.where(slot_range == 1, top_label, labels).astype(jnp.int32)
        shorter = jax.random.randint(leaf_key, (4,), LEAF // 2, LEAF + LEAF // 2 + 1).astype(jnp.int32)
        shorter = shorter.at[0].set(LEAF // 2)
        triples = jnp.stack([jnp.full((4,), BRANCH, jnp.int32), shorter, 2 * LEAF - shorter], 1).reshape(12)
        lengths = jnp.concatenate([jnp.full((1,), TRUNK, jnp.int32), triples])
        starts = jnp.cumsum(lengths) - lengths
        position = jnp.arange(TREE, dtype=jnp.int32)
        layout_index = jnp.sum((position[:, None] >= starts[None, 1:]).astype(jnp.int32), 1)
        segment_ids = labels[layout_index]
        parent_table = jnp.zeros((SEGMENTS,), jnp.int32).at[labels].set(labels[parent_layout])
        depth_ids = position - starts[layout_index] + base_layout[layout_index]
        return (segment_ids, parent_table, depth_ids.astype(jnp.int32))
    return jax.vmap(single)(tree_keys)


def draw_segment(key, part):
    return tree_layout(key)[0]


def draw_parent(key, part):
    return tree_layout(key)[1]


def draw_tree_depth(key, part):
    return tree_layout(key)[2]


def block_levels(key, shape, cuts, low, largest):
    factor_of = 1.0
    for dim, blocks in cuts:
        heights = jax.random.uniform(jax.random.fold_in(jax.random.fold_in(key, 6), dim), (blocks,), jnp.float32, low / len(cuts), largest / len(cuts))
        factor_of = factor_of * jnp.repeat(jnp.exp(heights), shape[dim] // blocks).reshape((-1,) + (1,) * (len(shape) - 1 - dim))
    return factor_of


def deal_out(rng, own, number, rows, count, top, bound, lean):
    ranking = jax.random.permutation(rng, count)
    heavy_load, ordinary = shares(count, rows * top, bound, lean, True), shares(count, rows * top, bound, lean, False)
    places = jnp.arange(count)

    def named(tallies, rotation):
        used = int((tallies > 0).sum())
        fixed = max(1, used // 4)
        moved = fixed + (places - fixed + rotation * (used - fixed)) % max(1, count - fixed)
        return jnp.zeros((count,), jnp.int32).at[ranking[jnp.where(places < fixed, places, moved)]].set(jnp.asarray(tallies, jnp.int32))

    tallies = jnp.where(number % 4 == 0, named(heavy_load, number // 4), named(ordinary, number - number // 4 - 1))
    mixed = jax.random.permutation(jax.random.fold_in(own, 3), count)
    giver, sink = mixed[0:count // 2 * 2:2], mixed[1:count // 2 * 2:2]
    slack = jnp.minimum(tallies[giver] - 1, bound - tallies[sink]) // 2
    slack = jnp.where((giver == ranking[0]) | (sink == ranking[0]) | (tallies[sink] == 0), 0, jnp.maximum(slack, 0))
    moved = jax.random.randint(jax.random.fold_in(own, 4), (count // 2,), 0, 1 << 20) % (slack + 1)
    tallies = tallies.at[giver].add(-moved).at[sink].add(moved)
    members = jnp.searchsorted(jnp.cumsum(tallies), jnp.arange(rows * top), side="right").astype(jnp.int32)
    listing = members.reshape(top, rows).T
    listing = listing[jax.random.permutation(jax.random.fold_in(own, 1), rows)]
    rotation = jax.random.randint(jax.random.fold_in(own, 2), (rows, 1), 0, top)
    return jnp.take_along_axis(listing, (jnp.arange(top)[None, :] + rotation) % top, axis=1)


def shares(amount, total, bound, lean, full):
    weights = [(1 << 20) // math.isqrt(standing ** lean) + 1 for standing in range(1, amount + 1)]
    largest = bound if full else min(bound, max(-(-total // amount), total * weights[0] // sum(weights)))
    least = 1 if total - largest >= amount - 1 else 0
    counts, spare = [largest] + [least] * (amount - 1), total - largest - least * (amount - 1)
    while spare > 0:
        movable = [i for i in range(1, amount) if counts[i] < largest] or [i for i in range(1, amount) if counts[i] < bound]
        pool, budget = sum([weights[i] for i in movable]), spare
        for i in movable:
            addition = min(bound - counts[i], max(1, budget * weights[i] // pool), spare)
            counts[i] = counts[i] + addition
            spare = spare - addition
    return np.array(counts)


def noise(rng, dims, width, most, cuts=(), kind=jnp.bfloat16):
    values = width * jax.random.normal(rng, dims, jnp.float32)
    if cuts:
        values = values * block_levels(rng, dims, cuts, -0.22, 0.18)
    return jnp.clip(values, -most, most).astype(kind)


def setup_inputs(seed: int = 0) -> dict:
    seeds = jax.random.split(jax.random.key(seed), 19)
    hidden = noise(seeds[0], (TREES, TREE, D), 1.0, 6.0, ((0, 2), (1, 4)))
    cotangent = noise(seeds[1], (TREES, TREE, D), 1.0, 6.0, ((0, 2), (1, 4)))
    gain_attn = jnp.clip(1.0 + 0.1 * jax.random.normal(seeds[2], (D,), jnp.float32), 0.5, 1.5).astype(jnp.bfloat16)
    query_weight = noise(seeds[3], (D, HEADS_Q * HEAD), D ** -0.5, 0.125, ((0, 8), (1, 4)))
    key_weight = noise(seeds[4], (D, HEADS_KV * HEAD), D ** -0.5, 0.125, ((0, 8), (1, 4)))
    value_weight = noise(seeds[5], (D, HEADS_KV * HEAD), D ** -0.5, 0.125, ((0, 8), (1, 4)))
    gain_query = jnp.clip(1.0 + 0.15 * jax.random.normal(seeds[6], (HEAD,), jnp.float32), 0.25, 1.75).astype(jnp.bfloat16)
    gain_key = jnp.clip(1.0 + 0.15 * jax.random.normal(seeds[7], (HEAD,), jnp.float32), 0.25, 1.75).astype(jnp.bfloat16)
    out_weight = noise(seeds[8], (HEADS_Q * HEAD, D), (max(HEADS_Q * HEAD // 64, 1)) ** -0.5, 0.75, ((0, 4), (1, 8)))
    gain_moe = jnp.clip(1.0 + 0.1 * jax.random.normal(seeds[9], (D,), jnp.float32), 0.5, 1.5).astype(jnp.bfloat16)
    router_weight = noise(seeds[10], (D, EXPERTS), (4 * D) ** -0.5, 0.0625, ((0, 8),))
    gate_weight = noise(seeds[11], (EXPERTS, D, FF), D ** -0.5, 0.125, ((1, 8), (2, 4)))
    up_weight = noise(seeds[12], (EXPERTS, D, FF), D ** -0.5, 0.125, ((1, 8), (2, 4)))
    down_weight = noise(seeds[13], (EXPERTS, FF, D), (max(FF // 16, 1)) ** -0.5, 0.875, ((1, 4), (2, 8)))
    segment = draw_segment(jax.random.fold_in(seeds[18], 71), 0)
    parent = draw_parent(jax.random.fold_in(seeds[18], 71), 0)
    tree_depth = draw_tree_depth(jax.random.fold_in(seeds[18], 71), 0)
    routes_keys = jax.random.split(jax.random.fold_in(seeds[17], 1), TREES * TREE // (TREE // N_CTX))
    routes_turns = jax.random.permutation(jax.random.fold_in(seeds[17], 3), TREES * TREE // (TREE // N_CTX))
    routes = jax.vmap(lambda own, number: deal_out(jax.random.fold_in(seeds[17], 2), own, number, TREE // N_CTX, EXPERTS, TOP, CAPACITY, 0))(routes_keys, routes_turns).reshape((TREES, TREE, TOP))
    return {"hidden": hidden, "cotangent": cotangent, "gain_attn": gain_attn, "query_weight": query_weight, "key_weight": key_weight, "value_weight": value_weight, "gain_query": gain_query, "gain_key": gain_key, "out_weight": out_weight, "gain_moe": gain_moe, "router_weight": router_weight, "gate_weight": gate_weight, "up_weight": up_weight, "down_weight": down_weight, "segment": segment, "parent": parent, "tree_depth": tree_depth, "routes": routes}


EPS = 1e-06
THETA = 1000000.0
MASKED = -1e+30
HIGH = lax.Precision.HIGHEST

@jax.custom_vjp
def low(v):
    return lax.optimization_barrier(v.astype(jnp.bfloat16)).astype(jnp.float32)

@jax.custom_vjp
def low_back(v):
    return v

def low_keep(v):
    return (low(v), None)

def low_pass(kept, grad):
    return (grad,)

def back_keep(v):
    return (v, None)

def back_low(kept, grad):
    return (low(grad),)
low.defvjp(low_keep, low_pass)
low_back.defvjp(back_keep, back_low)

def rms_scale(field, gain_vec):
    return field * lax.rsqrt(lax.optimization_barrier(jnp.mean(field * field, axis=-1, keepdims=True)) + EPS) * gain_vec

def angle_tables(positions):
    half_size = HEAD // 2
    frequency = jnp.exp(jnp.arange(half_size, dtype=jnp.float32) * (-2.0 * math.log(THETA) / HEAD))
    angles = positions.astype(jnp.float32)[..., None] * frequency
    angles = jnp.concatenate([angles, angles], -1)
    return (jnp.cos(angles), jnp.sin(angles))

def rotate(field, cosine_table, sine_table):
    half_size = field.shape[-1] // 2
    turned = jnp.concatenate([-field[..., half_size:], field[..., :half_size]], -1)
    return field * cosine_table + turned * sine_table

def tree_forward(tokens_in, gain_attn, query_weight, key_weight, value_weight, gain_query, gain_key, out_weight, gain_moe, router_weight, gate_weight, up_weight, down_weight, segment, parent, tree_depth, routes):
    group_size = HEADS_Q // HEADS_KV
    score_scale = HEAD ** (-0.5)
    block_rows = TREE // N_CTX
    normed = low(rms_scale(tokens_in, gain_attn))
    query_proj = low_back(jnp.dot(normed, query_weight, precision=HIGH))
    key_proj = low_back(jnp.dot(normed, key_weight, precision=HIGH))
    value_proj = low_back(low(jnp.dot(normed, value_weight, precision=HIGH)))
    cosine_table, sine_table = angle_tables(tree_depth)
    query_heads = query_proj.reshape(TREE, HEADS_Q, HEAD).transpose(1, 0, 2)
    key_heads = key_proj.reshape(TREE, HEADS_KV, HEAD).transpose(1, 0, 2)
    value_heads = value_proj.reshape(TREE, HEADS_KV, HEAD).transpose(1, 0, 2)
    query_rot = low(rotate(rms_scale(query_heads, gain_query), cosine_table, sine_table))
    key_rot = low(rotate(rms_scale(key_heads, gain_key), cosine_table, sine_table))
    first_up = jnp.take(parent, segment)
    second_up = jnp.take(parent, first_up)
    key_pos = jnp.arange(TREE, dtype=jnp.int32)

    def attend_block(block_start):
        query_block = lax.dynamic_slice_in_dim(query_rot, block_start, block_rows, 1).reshape(HEADS_KV, group_size, block_rows, HEAD)
        query_pos = block_start + jnp.arange(block_rows, dtype=jnp.int32)
        own_segment = lax.dynamic_slice_in_dim(segment, block_start, block_rows)
        own_first = lax.dynamic_slice_in_dim(first_up, block_start, block_rows)
        own_second = lax.dynamic_slice_in_dim(second_up, block_start, block_rows)
        related = (segment[None, :] == own_segment[:, None]) | (segment[None, :] == own_first[:, None]) | (segment[None, :] == own_second[:, None])
        visible = (key_pos[None, :] <= query_pos[:, None]) & related
        raw_score = low_back(jnp.einsum('hgqd,hkd->hgqk', query_block, key_rot, precision=HIGH))
        scores = jnp.where(visible, raw_score * score_scale, MASKED)
        row_max = lax.optimization_barrier(jnp.max(scores, -1, keepdims=True))
        weight = jnp.exp(scores - row_max)
        probability = weight / lax.optimization_barrier(jnp.sum(weight, -1, keepdims=True))
        return jnp.einsum('hgqk,hkd->hgqd', low(probability), value_heads, precision=HIGH)
    starts = jnp.arange(N_CTX, dtype=jnp.int32) * block_rows
    mixed = lax.map(jax.checkpoint(attend_block), starts)
    attn_out = low_back(low(mixed.transpose(0, 3, 1, 2, 4).reshape(TREE, HEADS_Q * HEAD)))
    attn_add = low_back(jnp.dot(attn_out, out_weight, precision=HIGH))
    resid = tokens_in + attn_add
    moe_in = low(rms_scale(resid, gain_moe))
    logits = low_back(jnp.dot(moe_in, router_weight, precision=HIGH))
    gates = jax.nn.softmax(jnp.take_along_axis(logits, routes, 1), -1)
    flat_routes = routes.reshape(-1).astype(jnp.int32)
    onehot = (flat_routes[:, None] == jnp.arange(EXPERTS, dtype=jnp.int32)[None, :]).astype(jnp.int32)
    slot_index = lax.optimization_barrier(jnp.sum((jnp.cumsum(onehot, 0) - onehot) * onehot, 1)).astype(jnp.int32)
    token_index = (jnp.arange(TREE * TOP, dtype=jnp.int32) // TOP).astype(jnp.int32)
    dispatched = jnp.zeros((EXPERTS, N_CTX * CAPACITY, D), jnp.float32).at[flat_routes, slot_index].set(moe_in[token_index])
    gate_pre = low_back(jnp.einsum('ecd,edf->ecf', dispatched, gate_weight, precision=HIGH))
    up_pre = low_back(jnp.einsum('ecd,edf->ecf', dispatched, up_weight, precision=HIGH))
    activated = low(jax.nn.silu(gate_pre) * up_pre)
    expert_out = low_back(jnp.einsum('ecf,efd->ecd', activated, down_weight, precision=HIGH))
    picked = expert_out[flat_routes, slot_index].reshape(TREE, TOP, D)
    return resid + lax.optimization_barrier(jnp.sum(gates[..., None] * picked, 1))

def reference(hidden, cotangent, gain_attn, query_weight, key_weight, value_weight, gain_query, gain_key, out_weight, gain_moe, router_weight, gate_weight, up_weight, down_weight, segment, parent, tree_depth, routes):
    params = (gain_attn.astype(jnp.float32), query_weight.astype(jnp.float32), key_weight.astype(jnp.float32), value_weight.astype(jnp.float32), gain_query.astype(jnp.float32), gain_key.astype(jnp.float32), out_weight.astype(jnp.float32), gain_moe.astype(jnp.float32), router_weight.astype(jnp.float32), gate_weight.astype(jnp.float32), up_weight.astype(jnp.float32), down_weight.astype(jnp.float32))

    def per_tree(carry, pieces):
        tokens_tree, cot_tree, seg_tree, parent_tree, depth_tree, route_tree = pieces

        def forward(tokens_in, *weights):
            return tree_forward(tokens_in, *weights, seg_tree, parent_tree, depth_tree, route_tree)
        result, pull = jax.vjp(forward, tokens_tree.astype(jnp.float32), *params)
        grads = pull(cot_tree.astype(jnp.float32))
        carry = tuple((total_grad + grad_tree for total_grad, grad_tree in zip(carry, grads[1:])))
        return (carry, (result.astype(jnp.bfloat16), grads[0].astype(jnp.bfloat16)))
    zeros_init = tuple((jnp.zeros(member.shape, jnp.float32) for member in params))
    totals, (outputs, grad_hidden) = lax.scan(per_tree, zeros_init, (hidden, cotangent, segment, parent, tree_depth, routes))
    return (outputs, grad_hidden, totals[0], totals[1], totals[2], totals[3], totals[4], totals[5], totals[6], totals[7], totals[8], totals[9], totals[10], totals[11])
```

```python
import functools
import math

import jax
import jax.numpy as jnp
from jax import lax
from jax.experimental import pallas as pl
from jax.experimental.pallas import tpu as pltpu
from jax.sharding import PartitionSpec as P

HEADS_Q = 32
HEADS_KV = 4
HEAD = 128
TOP = 8
EXPERTS = 16

EPS = 1e-06
THETA = 1000000.0
LOG2E = 1.4426950408889634
HIDE = -1e30

F32 = jnp.float32
BF16 = jnp.bfloat16
VMEM_BYTES = 58 * 1024 * 1024


def rounded(v):
    return v.astype(BF16)


def dot(a, b, contract):
    return lax.dot_general(a, b, ((contract[:1], contract[1:]), ((), ())), preferred_element_type=F32)


def after(value, *others):
    return lax.optimization_barrier((value,) + others)[0]


def to_core(v):
    return lax.ppermute(v, "ctx", [(i, i ^ 1) for i in range(4)])


def to_x(v):
    return lax.ppermute(v, "ctx", [(i, i ^ 2) for i in range(4)])


def to_dp(v):
    return lax.ppermute(v, "dp", [(0, 1), (1, 0)])


def sum_z(v):
    size, step = lax.axis_size("tensor"), 1
    while step < size:
        v = v + lax.ppermute(v, "tensor", [(i, i ^ step) for i in range(size)])
        step *= 2
    return v


def place():
    ctx = lax.axis_index("ctx")
    return lax.axis_index("dp"), ctx // 2, ctx % 2


def flips():
    dp, x, _ = place()
    return x + 2 * dp if lax.axis_size("dp") == 2 else x


def flip(v, axis, bit):
    return jnp.where(bit == 0, v, jnp.flip(v, axis))


def relative(v):
    dp, x, _ = place()
    count = lax.axis_size("dp")
    cut = v.reshape(v.shape[:-1] + (count, 2, v.shape[-1] // (2 * count)))
    cut = flip(cut, cut.ndim - 2, x)
    if count == 2:
        cut = flip(cut, cut.ndim - 3, dp)
    return cut.reshape(v.shape)


def halves(v, axis):
    return jnp.split(v, 2, axis)


class Link:
    def __init__(self, move):
        self.move, self.sent, self.last = move, [], []

    def send(self, v, *gate):
        gate = gate + tuple(self.sent[-2:-1]) + tuple(self.last)
        v = after(v, *gate) if gate else v
        self.last = [v]
        self.sent.append(self.move(v))
        return self.sent[-1]


def scatter_far(blocks, axis, x_link, y_link):
    far_first, far_second = halves(blocks[3], axis)
    return x_link.send(far_first), y_link.send(far_second)


def scatter_near(blocks, got, axis, x_link, y_link):
    y_first, y_second = halves(blocks[2], axis)
    x_first, x_second = halves(blocks[1], axis)
    x_got, y_got = x_link.send(x_first), y_link.send(y_second)
    y_first = rounded(y_first.astype(F32) + got[0].astype(F32))
    x_second = rounded(x_second.astype(F32) + got[1].astype(F32))
    return x_got, y_link.send(y_first), x_link.send(x_second), y_got


def scatter_sum(own, near, axis):
    x_first, y_first, x_second, y_second = (v.astype(F32) for v in near)
    return own.astype(F32) + jnp.concatenate([x_first + y_first, x_second + y_second], axis)


def gather_whole(block, axis):
    pair = jnp.concatenate([block, to_x(block)], axis)
    return lax.all_gather(pair, "dp", axis=axis, tiled=True)


def scatter_whole(blocks):
    kept = jnp.stack(blocks[0::2]).astype(F32) + to_x(jnp.stack(blocks[1::2])).astype(F32)
    return lax.psum_scatter(rounded(kept), "dp", scatter_dimension=0, tiled=False).astype(F32)


def whole(array):
    dims = len(array.shape)
    return pl.BlockSpec(array.shape, lambda *_: (0,) * dims)


SCALARS = pl.BlockSpec(memory_space=pltpu.SMEM)


def kernel_call(body, grid, in_specs, out_specs, out_shape, flops, moved, scratch=()):
    return pl.pallas_call(
        body,
        grid=grid,
        in_specs=in_specs,
        out_specs=out_specs,
        out_shape=out_shape,
        scratch_shapes=list(scratch),
        compiler_params=pltpu.CompilerParams(vmem_limit_bytes=VMEM_BYTES),
        cost_estimate=pl.CostEstimate(flops=int(flops), bytes_accessed=int(moved), transcendentals=0),
    )


def sds(shape, dtype):
    return jax.ShapeDtypeStruct(shape, dtype)


def piece_starts(scal, places, shard):
    core = scal[1]
    shift = {0: 0, 1: core * shard, 2: (1 - core) * shard}
    return [
        (start if kind == 0 else pl.multiple_of(start + shift[kind], length), length)
        for start, length, kind in places
    ]


def kernel_inverse_rms(v):
    return lax.rsqrt(jnp.mean(v * v, axis=-1, keepdims=True) + EPS)


def permute_kernel(scal, in_ref, out_ref):
    out_ref[...] = in_ref[...]


def permute_width(v, scal, blocks):
    rows, width = v.shape
    span = width // blocks
    return pl.pallas_call(
        permute_kernel,
        grid_spec=pltpu.PrefetchScalarGridSpec(
            num_scalar_prefetch=1,
            grid=(blocks,),
            in_specs=[pl.BlockSpec((rows, span), lambda j, s: (0, j ^ s[0]))],
            out_specs=pl.BlockSpec((rows, span), lambda j, s: (0, j)),
        ),
        out_shape=sds(v.shape, v.dtype),
        cost_estimate=pl.CostEstimate(flops=0, bytes_accessed=4 * v.size, transcendentals=0),
    )(scal, v)


def pick_columns(v, scal, shard, other):
    rows, width = v.shape
    count = width // (2 * shard)
    if shard % 128:
        which = 1 - scal[1] if other else scal[1]
        cut = v.reshape(rows, count, 2, shard)
        return lax.dynamic_index_in_dim(cut, which, 2, keepdims=False).reshape(rows, count * shard)
    return pl.pallas_call(
        permute_kernel,
        grid_spec=pltpu.PrefetchScalarGridSpec(
            num_scalar_prefetch=1,
            grid=(count,),
            in_specs=[pl.BlockSpec((rows, shard), lambda j, s: (0, 2 * j + (1 - s[1] if other else s[1])))],
            out_specs=pl.BlockSpec((rows, shard), lambda j, s: (0, j)),
        ),
        out_shape=sds((rows, count * shard), v.dtype),
        cost_estimate=pl.CostEstimate(flops=0, bytes_accessed=2 * v.size, transcendentals=0),
    )(scal, v)


def qkv_kernel(places, shard, blocks, scal, hid, gain, gain_q, gain_k, cos, sin, *refs):
    weights, (normed, hid_rel, raw, rot) = refs[: len(places)], refs[len(places) :]
    step, last = pl.program_id(0), pl.num_programs(0) - 1
    width = hid.shape[1]
    span = width // blocks

    @pl.when(step == 0)
    def _():
        for j in range(blocks):
            source = pl.multiple_of((scal[0] ^ j) * span, span)
            hid_rel[:, j * span : (j + 1) * span] = hid[:, pl.ds(source, span)]
        tokens = hid_rel[...].astype(F32)
        normed[...] = rounded(tokens * kernel_inverse_rms(tokens) * gain[...])

    total = jnp.zeros(raw.shape, F32)
    for (start, length), weight in zip(piece_starts(scal, places, shard), weights):
        total += dot(normed[:, pl.ds(start, length)], weight[...], (1, 0))
    raw[...] = total
    vector = jnp.where(step == last, gain_k[...], gain_q[...])
    for head in range(2):
        cut = total[:, head * HEAD : (head + 1) * HEAD]
        scaled = cut * kernel_inverse_rms(cut) * vector
        turned = scaled * cos[...] + pltpu.roll(scaled, HEAD // 2, 1) * sin[...]
        if head == 1:
            turned = jnp.where(step == last, cut, turned)
        rot[:, head * HEAD : (head + 1) * HEAD] = rounded(turned)


def qkv_call(scal, hid, gain, gain_q, gain_k, cos, sin, pieces, places, shard, blocks, columns):
    rows, width = hid.shape
    pair = 2 * HEAD
    small = (gain, gain_q, gain_k, cos, sin)
    block = pl.BlockSpec((rows, pair), lambda i: (0, i))
    return kernel_call(
        functools.partial(qkv_kernel, places, shard, blocks),
        (columns // pair,),
        [SCALARS, whole(hid)]
        + [whole(v) for v in small]
        + [pl.BlockSpec((p.shape[0], pair), lambda i: (0, i)) for p in pieces],
        [whole(hid), whole(hid), block, block],
        [sds(hid.shape, BF16), sds(hid.shape, BF16), sds((rows, columns), F32), sds((rows, columns), BF16)],
        2 * rows * width * columns,
        2 * width * columns + 12 * rows * width,
    )(scal, hid, *small, *pieces)


def write_bias(bias, key_side, query_side):
    seg = key_side[:, 0:1]
    seen = (seg == query_side[0:1]) | (seg == query_side[1:2]) | (seg == query_side[2:3])
    seen = seen & (key_side[:, 1:2] <= query_side[3:4])
    bias[...] = jnp.where(seen, 0.0, HIDE)


def key_tiles(count):
    tile = next(t for t in (384, 320, 256, 128) if count % t == 0)
    return [(s, tile) for s in range(0, count, tile)]


def attend_kernel(query, keys, values, key_side, query_side, mixed, inverse, bias, values_t):
    @pl.when(pl.program_id(0) == 0)
    def _():
        write_bias(bias, key_side[...], query_side[...])
        values_t[...] = values[...].T

    rows = query.shape[0]
    total = jnp.zeros((HEAD, rows), F32)
    row_sum = jnp.zeros((1, rows), F32)
    factor = LOG2E * HEAD**-0.5
    for start, tile in key_tiles(keys.shape[0]):
        raw = dot(keys[start : start + tile], query[...], (1, 1))
        weight = jnp.exp2(raw * factor + bias[start : start + tile])
        row_sum += jnp.sum(weight, 0, keepdims=True)
        total += dot(values_t[:, start : start + tile], rounded(weight), (1, 0))
    scale = 1.0 / row_sum
    mixed[...] = rounded((total * scale).T)
    inverse[0] = scale


def attend_call(rot, kv_all, key_side, query_side, heads):
    rows, count = rot.shape[0], kv_all.shape[0]
    column = pl.BlockSpec((rows, HEAD), lambda h: (0, h))
    return kernel_call(
        attend_kernel,
        (heads,),
        [
            column,
            pl.BlockSpec((count, HEAD), lambda h: (0, 0)),
            pl.BlockSpec((count, HEAD), lambda h: (0, 1)),
            whole(key_side),
            whole(query_side),
        ],
        [column, pl.BlockSpec((1, 1, rows), lambda h: (h, 0, 0))],
        [sds((rows, heads * HEAD), BF16), sds((heads, 1, rows), F32)],
        4 * heads * rows * count * HEAD,
        4 * rows * heads * HEAD + 4 * count * HEAD,
        [pltpu.VMEM((count, rows), F32), pltpu.VMEM((HEAD, count), BF16)],
    )(rot, kv_all, kv_all, key_side, query_side)


def attend_back_kernel(
    query, keys, values, key_side, query_side, grad, mixed, inverse, raw_query, cos, sin, gain,
    query_back, grad_kv, grad_gain, bias, keys_t,
):
    @pl.when(pl.program_id(0) == 0)
    def _():
        write_bias(bias, key_side[...], query_side[...])
        keys_t[...] = keys[...].T
        grad_kv[...] = jnp.zeros(grad_kv.shape, F32)
        grad_gain[...] = jnp.zeros(grad_gain.shape, F32)

    rows = query.shape[0]
    scale = HEAD**-0.5
    factor = LOG2E * scale
    both = grad[...].astype(F32) * mixed[...].astype(F32)
    mean = jnp.sum(both.T, 0, keepdims=True)
    norm = inverse[0]
    total = jnp.zeros((HEAD, rows), F32)
    for start, tile in key_tiles(keys.shape[0]):
        span = slice(start, start + tile)
        raw = dot(keys[span], query[...], (1, 1))
        prob = jnp.exp2(raw * factor + bias[span]) * norm
        grad_prob = dot(values[span], grad[...], (1, 1))
        grad_raw = rounded(prob * (grad_prob - mean) * scale)
        total += dot(keys_t[:, span], grad_raw, (1, 0))
        grad_kv[span, :HEAD] += dot(grad_raw, query[...], (1, 0))
        grad_kv[span, HEAD:] += dot(rounded(prob), grad[...], (1, 0))
    turned = total.T
    turned = turned * cos[...] - pltpu.roll(turned, HEAD // 2, 1) * sin[...]
    value = raw_query[...]
    shrink = kernel_inverse_rms(value)
    normal = value * shrink
    grad_gain[...] += jnp.sum(turned * normal, 0, keepdims=True)
    scaled = turned * gain[...]
    middle = jnp.mean(scaled * normal, axis=-1, keepdims=True)
    query_back[...] = rounded(shrink * (scaled - normal * middle))


def attend_back_call(rot, kv_all, key_side, query_side, grad, mixed, inverse, raw, cos, sin, gain, heads):
    rows, count = rot.shape[0], kv_all.shape[0]
    column = pl.BlockSpec((rows, HEAD), lambda h: (0, h))
    return kernel_call(
        attend_back_kernel,
        (heads,),
        [
            column,
            pl.BlockSpec((count, HEAD), lambda h: (0, 0)),
            pl.BlockSpec((count, HEAD), lambda h: (0, 1)),
            whole(key_side),
            whole(query_side),
            column,
            column,
            pl.BlockSpec((1, 1, rows), lambda h: (h, 0, 0)),
            column,
            whole(cos),
            whole(sin),
            whole(gain),
        ],
        [
            column,
            pl.BlockSpec((count, 2 * HEAD), lambda h: (0, 0)),
            pl.BlockSpec((1, HEAD), lambda h: (0, 0)),
        ],
        [sds((rows, heads * HEAD), BF16), sds((count, 2 * HEAD), F32), sds((1, HEAD), F32)],
        10 * heads * rows * count * HEAD,
        12 * rows * heads * HEAD + 12 * count * HEAD,
        [pltpu.VMEM((count, rows), F32), pltpu.VMEM((HEAD, count), BF16)],
    )(rot, kv_all, kv_all, key_side, query_side, grad, mixed, inverse, raw, cos, sin, gain)


def project_kernel(places, shard, scal, mixed, *refs):
    out = refs[-1]
    for (start, length), weight in zip(piece_starts(scal, places, shard), refs[:-1]):
        out[:, pl.ds(start, length)] = rounded(dot(mixed[...], weight[...], (1, 0)))


def project_call(scal, mixed, pieces, places, shard, width):
    rows, inner = mixed.shape
    return kernel_call(
        functools.partial(project_kernel, places, shard),
        (1,),
        [SCALARS, whole(mixed)] + [whole(p) for p in pieces],
        pl.BlockSpec((rows, width), lambda i: (0, 0)),
        sds((rows, width), BF16),
        2 * rows * inner * width,
        2 * inner * width + 2 * rows * (inner + width),
    )(scal, mixed, *pieces)


def project_back_kernel(places, shard, scal, grad, *refs):
    out = refs[-1]
    total = jnp.zeros(out.shape, F32)
    for (start, length), weight in zip(piece_starts(scal, places, shard), refs[:-1]):
        total += dot(grad[:, pl.ds(start, length)], weight[...], (1, 1))
    out[...] = rounded(total)


def project_back_call(scal, grad, pieces, places, shard, inner):
    rows, width = grad.shape
    tile = inner // 2
    return kernel_call(
        functools.partial(project_back_kernel, places, shard),
        (2,),
        [SCALARS, whole(grad)] + [pl.BlockSpec((tile, p.shape[1]), lambda i: (i, 0)) for p in pieces],
        pl.BlockSpec((rows, tile), lambda i: (0, i)),
        sds((rows, inner), BF16),
        2 * rows * inner * width,
        2 * inner * width + 2 * rows * (inner + width),
    )(scal, grad, *pieces)


def qkv_back_kernel(places, shard, scal, back, hid, *refs):
    weights, (part, grad_gain) = refs[: len(places)], refs[len(places) :]
    tokens = hid[...].astype(F32)
    shrink = kernel_inverse_rms(tokens)
    for (start, length), weight in zip(piece_starts(scal, places, shard), weights):
        lanes = pl.ds(start, length)
        value = dot(back[...], weight[...], (1, 1))
        part[:, lanes] = rounded(value)
        normal = hid[:, lanes].astype(F32) * shrink
        grad_gain[:, lanes] = jnp.sum(value * normal, 0, keepdims=True)


def qkv_back_call(scal, back, hid, pieces, places, shard):
    rows, width = hid.shape
    columns = back.shape[1]
    return kernel_call(
        functools.partial(qkv_back_kernel, places, shard),
        (1,),
        [SCALARS, whole(back), whole(hid)] + [whole(p) for p in pieces],
        [pl.BlockSpec((rows, width), lambda i: (0, 0)), pl.BlockSpec((1, width), lambda i: (0, 0))],
        [sds((rows, width), BF16), sds((1, width), F32)],
        2 * rows * columns * width,
        2 * columns * width + 2 * rows * (columns + 2 * width),
    )(scal, back, hid, *pieces)


def join_rows(own, other, scratch):
    rows = own.shape[0]

    @pl.when(pl.program_id(0) == 0)
    def _():
        scratch[:rows] = own[...]
        scratch[rows:] = other[...]


def product(weights, rows_ref):
    return dot(jnp.concatenate([w[...] for w in weights], 1), rows_ref[...], (1, 1))


def single(shape):
    dims = len(shape)
    return pl.BlockSpec(shape, lambda *_: (0,) * dims, pipeline_mode=pl.Buffered(1))


def products_kernel(own, other, *refs):
    weights, (out, both) = refs[:-2], refs[-2:]
    join_rows(own, other, both)
    out[...] = product(weights, both)


def products_call(own, other, pieces):
    rows, width = own.shape
    hidden = pieces[0].shape[0]
    tile = hidden // 4
    return kernel_call(
        products_kernel,
        (4,),
        [single(own.shape), single(own.shape)]
        + [pl.BlockSpec((tile, w.shape[1]), lambda i: (i, 0)) for w in pieces],
        pl.BlockSpec((tile, 2 * rows), lambda i: (i, 0)),
        sds((hidden, 2 * rows), F32),
        4 * rows * width * hidden,
        2 * hidden * width + 4 * rows * width + 8 * hidden * rows,
        [pltpu.VMEM((2 * rows, width), BF16)],
    )(own, other, *pieces)


def experts_kernel(places, hid, own, other, gate_ref, grad_act, gates, *refs):
    n = len(places)
    gated, gate_back, up_back, gated_t, gate_back_t, up_back_t, gate_part, both = refs[n:]
    join_rows(own, other, both)
    gate_pre, up_pre = gate_ref[...], product(refs[:n], both)
    sig = 1.0 / (1.0 + jnp.exp(-gate_pre))
    silu = gate_pre * sig
    act = silu * up_pre
    slope = sig * (1.0 + gate_pre * (1.0 - sig))
    count = gates.shape[0]
    for e in range(count):
        rows = slice(e * hid, (e + 1) * hid)
        gate = gates[e]
        raw = grad_act[rows, :]
        back = gate * raw
        gated[rows, :] = rounded(gate * act[rows])
        gate_back[rows, :] = rounded(back * up_pre[rows] * slope[rows])
        up_back[rows, :] = rounded(back * silu[rows])
        gate_part[e] = jnp.sum(act[rows] * raw, 0, keepdims=True)
    gated_t[...] = gated[...].T
    gate_back_t[...] = gate_back[...].T
    up_back_t[...] = up_back[...].T


def experts_call(own, other, gate_pre, grad_act, gates, up_p, places, hid):
    rows, width = own.shape
    both = 2 * rows
    experts = gates.shape[0]
    per = 2
    tile = per * hid
    act = pl.BlockSpec((tile, both), lambda i: (i, 0))
    act_t = pl.BlockSpec((both, tile), lambda i: (0, i))
    gate = pl.BlockSpec((per, 1, both), lambda i: (i, 0, 0))
    weights = list(up_p)
    hidden = experts * hid
    return kernel_call(
        functools.partial(experts_kernel, places, hid),
        (experts // per,),
        [single(own.shape), single(own.shape), act, act, gate]
        + [pl.BlockSpec((tile, w.shape[1]), lambda i: (i, 0)) for w in weights],
        [act, act, act, act_t, act_t, act_t, gate],
        [sds((hidden, both), BF16)] * 3
        + [sds((both, hidden), BF16)] * 3
        + [sds((experts, 1, both), F32)],
        2 * both * width * hidden,
        2 * hidden * width + 20 * hidden * both + 2 * both * width,
        [pltpu.VMEM((both, width), BF16)],
    )(own, other, gate_pre, grad_act, gates, *weights)


def backward_tiles(places, tile):
    return [(p, k) for p, (_, length, _) in enumerate(places) for k in range(length // tile)]


def spread_kernel(tiles, terms, *refs):
    acts = refs[:terms]
    n = (len(refs) - terms - 2) // terms
    own_ref, other_ref = refs[-2:]
    step = pl.program_id(0)
    rows = own_ref.shape[0]
    for p in range(n):
        steps = [t for t, (q, _) in enumerate(tiles) if q == p]

        @pl.when((step >= steps[0]) & (step <= steps[-1]))
        def _():
            value = sum(dot(acts[k][...], refs[terms + k * n + p][...], (1, 0)) for k in range(terms))
            own_ref[...] = value[:rows]
            other_ref[...] = rounded(value[rows:])


def spread_call(acts, weights, places):
    both, hidden = acts[0].shape
    rows = both // 2
    width = sum(length for _, length, _ in places)
    tile = 256
    tiles = backward_tiles(places, tile)
    assert [s for s, _, _ in places] == sorted(s for s, _, _ in places)

    def spec(p):
        steps = [t for t, (q, _) in enumerate(tiles) if q == p]
        first, last = steps[0], steps[-1]
        return pl.BlockSpec((hidden, tile), lambda t: (0, jnp.clip(t, first, last) - first))

    out = pl.BlockSpec((rows, tile), lambda t: (0, t))
    return kernel_call(
        functools.partial(spread_kernel, tiles, len(acts)),
        (len(tiles),),
        [single(a.shape) for a in acts] + [spec(p) for _ in acts for p in range(len(places))],
        [out, out],
        [sds((rows, width), F32), sds((rows, width), BF16)],
        2 * both * width * hidden * len(acts),
        2 * hidden * (width + both) * len(acts) + 6 * rows * width,
    )(*acts, *[w for pieces in weights for w in pieces])


def route_kernel(top_count, hid, attn_add, gain, router_t, routes, resid, moe_low, gates):
    value = hid[...].astype(F32) + attn_add[...].astype(F32)
    resid[...] = value
    moe_low[...] = rounded(value * kernel_inverse_rms(value) * gain[...])
    logits = dot(moe_low[...], router_t[...], (1, 1))
    numbers = lax.broadcasted_iota(jnp.int32, logits.shape, 1)
    chosen = routes[:, 0:1] == numbers
    for k in range(1, top_count):
        chosen = chosen | (routes[:, k : k + 1] == numbers)
    top = jnp.max(jnp.where(chosen, logits, HIDE), -1, keepdims=True)
    lift = jnp.where(chosen, jnp.exp(jnp.where(chosen, logits, top) - top), 0.0)
    gates[...] = lift / jnp.sum(lift, -1, keepdims=True)


def row_specs(arrays, rows, tile):
    return [
        pl.BlockSpec((tile, a.shape[1]), lambda i: (i, 0)) if a.shape[0] == rows else whole(a) for a in arrays
    ]


def route_call(hid, attn_add, gain, router_t, routes):
    rows, width = hid.shape
    tile = rows // 3
    arrays = (hid, attn_add, gain, router_t, routes)
    outs = [sds((rows, width), F32), sds((rows, width), BF16), sds((rows, router_t.shape[0]), F32)]
    return kernel_call(
        functools.partial(route_kernel, routes.shape[1]),
        (3,),
        row_specs(arrays, rows, tile),
        row_specs(outs, rows, tile),
        outs,
        40 * rows * width,
        10 * rows * width,
    )(*arrays)


def route_back_kernel(
    grad_moe, gate_grads, gates, resid, cot, router_t, gain, grad_resid, resid_low, grad_logits, grad_gain
):
    chosen = gates[...]
    part = gate_grads[...]
    middle = jnp.sum(chosen * part, -1, keepdims=True)
    grad_logits[...] = rounded(chosen * (part - middle))
    total = grad_moe[...].astype(F32) + dot(grad_logits[...], router_t[...], (1, 0))
    value = resid[...]
    shrink = kernel_inverse_rms(value)
    normal = value * shrink

    @pl.when(pl.program_id(0) == 0)
    def _():
        grad_gain[...] = jnp.zeros(grad_gain.shape, F32)

    grad_gain[...] += jnp.sum(total * normal, 0, keepdims=True)
    scaled = total * gain[...]
    mean = jnp.mean(scaled * normal, axis=-1, keepdims=True)
    out = cot[...].astype(F32) + shrink * (scaled - normal * mean)
    grad_resid[...] = out
    resid_low[...] = rounded(out)


def route_back_call(grad_moe, gate_grads, gates, resid, cot, router_t, gain):
    rows, width = resid.shape
    tile = rows // 3
    arrays = (grad_moe, gate_grads, gates, resid, cot, router_t, gain)
    outs = [
        sds((rows, width), F32),
        sds((rows, width), BF16),
        sds(gates.shape, BF16),
        sds((1, width), F32),
    ]
    return kernel_call(
        route_back_kernel,
        (3,),
        row_specs(arrays, rows, tile),
        row_specs(outs, rows, tile),
        outs,
        50 * rows * width,
        14 * rows * width,
    )(*arrays)


def to_whole_order(scal, blocks, value, out):
    span = value.shape[1] // blocks
    for j in range(blocks):
        target = pl.multiple_of((scal[0] ^ j) * span, span)
        out[:, pl.ds(target, span)] = value[:, j * span : (j + 1) * span]


def add_kernel(blocks, scal, first, second, out):
    value = rounded(first[...] + second[...].astype(F32))
    to_whole_order(scal, blocks, value, out)


def last_kernel(blocks, scal, hid, grad_resid, grad_normed, gain, out):
    tokens = hid[...].astype(F32)
    shrink = kernel_inverse_rms(tokens)
    normal = tokens * shrink
    scaled = grad_normed[...].astype(F32) * gain[...]
    middle = jnp.mean(scaled * normal, axis=-1, keepdims=True)
    value = rounded(grad_resid[...] + shrink * (scaled - normal * middle))
    to_whole_order(scal, blocks, value, out)


def by_rows(body, scal, arrays, blocks, steps):
    rows, width = arrays[0].shape
    tile = rows // steps
    spec = pl.BlockSpec((tile, width), lambda i: (i, 0))
    return kernel_call(
        functools.partial(body, blocks),
        (steps,),
        [SCALARS] + [spec if a.shape[0] == rows else whole(a) for a in arrays],
        spec,
        sds((rows, width), BF16),
        10 * rows * width,
        8 * rows * width,
    )(scal, *arrays)


def inverse_rms(v):
    return lax.rsqrt(jnp.mean(v * v, axis=-1, keepdims=True) + EPS)


def angle_tables(positions):
    half_size = HEAD // 2
    frequency = jnp.exp(jnp.arange(half_size, dtype=F32) * (-2.0 * math.log(THETA) / HEAD))
    angles = positions.astype(F32)[..., None] * frequency
    sine = jnp.sin(angles)
    cosine = jnp.cos(angles)
    return jnp.concatenate([cosine, cosine], -1), jnp.concatenate([-sine, sine], -1)


def rotate_back(field, cosine, signed_sine):
    half_size = field.shape[-1] // 2
    turned = jnp.concatenate([field[..., half_size:], field[..., :half_size]], -1)
    return field * cosine - turned * signed_sine


def norm_back(scaled, scale, normal):
    return scale * (scaled - normal * jnp.mean(scaled * normal, axis=-1, keepdims=True))


def lookup_parent(segment_ids, parent):
    seg_table = jnp.arange(parent.shape[-1], dtype=jnp.int32)
    return jnp.sum(jnp.where(segment_ids[..., None] == seg_table, parent, 0), -1)


def shards(
    hidden,
    cotangent,
    gain_attn,
    query_weight,
    key_weight,
    value_weight,
    gain_query,
    gain_key,
    out_weight,
    gain_moe,
    router_weight,
    gate_weight,
    up_weight,
    down_weight,
    segment,
    parent,
    tree_depth,
    routes,
):
    _, rows, width = hidden.shape
    dp, x, core = place()
    ctx = lax.axis_index("ctx")
    count = lax.axis_size("dp")
    paired = count == 2
    chips = 2 * count
    tensor = lax.axis_size("tensor")
    heads = HEADS_Q // tensor
    shard = query_weight.shape[0]
    span = 2 * shard
    inner = heads * HEAD
    columns = inner + 2 * HEAD
    half = EXPERTS // 2
    hid = down_weight.shape[1]
    scal = jnp.stack([flips(), core]).astype(jnp.int32)

    def by_core(own, other, axis):
        return jnp.where(core == 0, jnp.stack([own, other], axis), jnp.stack([other, own], axis))

    x_link, y_link = Link(to_x), Link(to_dp)

    def near_pieces(block):
        return x_link.send(block), y_link.send(block)

    def far_pieces(block, near, axis):
        x_block, y_block = near
        far_first = y_link.send(halves(x_block, axis)[0])
        far_second = x_link.send(halves(y_block, axis)[1])
        size = block.shape[axis]
        arrays = [block, x_block, y_block, far_first, far_second]
        starts = [0, span, 2 * span, 3 * span, 3 * span + size // 2]
        return arrays, [(s, a.shape[axis], 0) for s, a in zip(starts, arrays)]

    def whole_piece(block, axis):
        own = gather_whole(block, axis)
        cut = own.shape[:axis] + (chips, shard) + own.shape[axis + 1 :]
        full = by_core(own.reshape(cut), to_core(own).reshape(cut), axis + 1)
        return [full.reshape(own.shape[:axis] + (width,) + own.shape[axis + 1 :])], [(0, width, 0)]

    per = gain_query.shape[0]
    gain_row = jnp.concatenate([gain_query, gain_key])
    small = jnp.concatenate(
        [
            gain_attn[None],
            gain_moe[None],
            router_weight.T,
            jnp.pad(gain_row, (0, shard - 2 * per))[None],
            jnp.zeros((13, shard), BF16),
        ]
    )
    qkv_shard = jnp.concatenate([query_weight, key_weight, value_weight], 1)
    if paired:
        qkv_near = near_pieces(qkv_shard)
        small_x, small_y = near_pieces(small)
        qkv_own, places = far_pieces(qkv_shard, qkv_near, 0)
        small_own = jnp.stack([small, small_x, small_y, y_link.send(small_x)], 1)
        qkv_pieces = qkv_own + [to_core(a) for a in qkv_own]
        qkv_places = [(s, n, kind) for kind in (1, 2) for s, n, _ in places]
    else:
        small_own = gather_whole(small, 1).reshape(32, chips, shard)
        qkv_pieces, qkv_places = whole_piece(qkv_shard, 0)
    small_all = by_core(small_own, to_core(small_own), 2).reshape(32, width)
    gain_one = small_all[0:1].astype(F32)
    gain_two = small_all[1:2].astype(F32)
    router_t = small_all[2 : 2 + EXPERTS]
    gain_heads = relative(small_all[2 + EXPERTS])
    gain_heads = gain_heads.reshape(2 * chips, shard)[:, : 2 * per].astype(F32)
    gain_q = gain_heads[:, :per].reshape(1, HEAD)
    gain_k = gain_heads[:, per:].reshape(1, HEAD)

    if paired:
        out_own, places = far_pieces(out_weight, near_pieces(out_weight), 1)
        out_pieces = out_own + [to_core(a) for a in out_own]
        out_places = [(s, n, kind) for kind in (1, 2) for s, n, _ in places]
    else:
        out_pieces, out_places = whole_piece(out_weight, 1)

    def expert_block(weight):
        own = lax.dynamic_slice_in_dim(weight, core * half, half, 0)
        sent = lax.dynamic_slice_in_dim(weight, (1 - core) * half, half, 0)
        return by_core(own, to_core(sent), 2).reshape(half * hid, span)

    expert_blocks = [
        expert_block(after(w, qkv_pieces[1 % len(qkv_pieces)]))
        for w in (down_weight, gate_weight.transpose(0, 2, 1), up_weight.transpose(0, 2, 1))
    ]

    cosine, sine = angle_tables(tree_depth[0])
    normed, tokens_low, raw, rot = qkv_call(
        scal, hidden[0], gain_one, gain_q, gain_k, cosine, sine, qkv_pieces, qkv_places, shard, chips, columns
    )
    key_value = rot[:, inner:]
    kv_x = x_link.send(key_value)
    kv_other = to_core(key_value)
    kv_all = jnp.concatenate([key_value, kv_other, kv_x, to_core(kv_x)])
    if paired:
        down_near = near_pieces(expert_blocks[0])
        gate_near = near_pieces(expert_blocks[1])
        down_pieces, expert_places = far_pieces(expert_blocks[0], down_near, 1)
        up_near = near_pieces(expert_blocks[2])
        gate_pieces, _ = far_pieces(expert_blocks[1], gate_near, 1)
        up_pieces, _ = far_pieces(expert_blocks[2], up_near, 1)
    else:
        down_pieces, gate_pieces, up_pieces = ([gather_whole(b, 1)] for b in expert_blocks)
        expert_places = [(0, width, 0)]

    seg = segment[0].reshape(2, 2, rows)
    seg_rel = flip(flip(seg, 0, x), 1, core).reshape(4 * rows)
    position = jnp.arange(4 * rows, dtype=jnp.int32).reshape(2, 2, rows)
    key_pos = flip(flip(position, 0, x), 1, core).reshape(4 * rows)
    first_up = lookup_parent(seg_rel[:rows], parent[0])
    second_up = lookup_parent(first_up, parent[0])
    key_side = jnp.stack([seg_rel, key_pos], 1)
    query_side = jnp.stack([seg_rel[:rows], first_up, second_up, key_pos[:rows]])

    mixed_low, inverse = attend_call(rot, kv_all, key_side, query_side, heads)
    attn_part = project_call(scal, mixed_low, out_pieces, out_places, shard, width)
    attn_add = lax.psum(attn_part, "tensor")

    cot = permute_width(cotangent[0], scal, chips)
    cot_other = to_core(cot)
    grad_act = products_call(cot, cot_other, down_pieces)
    attn_add = after(attn_add, grad_act, *gate_pieces[1:3])
    resid, moe_low, gates = route_call(tokens_low, attn_add, gain_two, router_t, routes[0])
    moe_other = to_core(moe_low)
    gate_pre = products_call(moe_low, moe_other, gate_pieces)
    gates_t = gates.T
    gates_own = lax.dynamic_slice_in_dim(gates_t, core * half, half, 0)
    gates_sent = lax.dynamic_slice_in_dim(gates_t, (1 - core) * half, half, 0)
    gate_pair = jnp.concatenate([gates_own, to_core(gates_sent)], 1)[:, None, :]

    gated_act, gate_back, up_back, gated_t, gate_back_t, up_back_t, gate_part = experts_call(
        moe_low, moe_other, gate_pre, grad_act, gate_pair, up_pieces, expert_places, hid
    )
    part_own, part_other = spread_call([gate_back_t, up_back_t], [gate_pieces, up_pieces], expert_places)
    moe_sum = rounded(part_own + to_core(part_other).astype(F32))
    grad_moe_in = lax.psum(moe_sum, "tensor")
    gate_part = gate_part[:, 0]
    gate_other = to_core(gate_part[:, rows:])
    gate_grads = sum_z(by_core(gate_part[:, :rows], gate_other, 0).reshape(EXPERTS, rows)).T
    pair_x = jnp.concatenate([moe_low, moe_other])
    pair_dy = jnp.concatenate([cot, cot_other])

    def expert_blocks_of(left, right):
        left = after(left, moe_sum)
        return [rounded(dot(left, right[:, r * span : (r + 1) * span], (1, 0))) for r in range(chips)]

    grad_blocks = [
        expert_blocks_of(gated_act, pair_dy),
        expert_blocks_of(gate_back, pair_x),
        expert_blocks_of(up_back, pair_x),
    ]
    if paired:
        down_far = scatter_far(grad_blocks[0], 1, x_link, y_link)
        gate_far = scatter_far(grad_blocks[1], 1, x_link, y_link)
        down_got = scatter_near(grad_blocks[0], down_far, 1, x_link, y_link)
        up_far = scatter_far(grad_blocks[2], 1, x_link, y_link)
        gate_got = scatter_near(grad_blocks[1], gate_far, 1, x_link, y_link)

    out_own, out_other = spread_call([after(gated_t, moe_sum)], [down_pieces], expert_places)
    out_sum = rounded(out_own + to_core(out_other).astype(F32))
    quarter = rows // tensor
    first_row = lax.axis_index("tensor") * quarter
    out_sum = after(out_sum, grad_moe_in)
    moe_add = lax.psum_scatter(out_sum, "tensor", scatter_dimension=0, tiled=True)
    moe_add = by_rows(add_kernel, scal, [lax.dynamic_slice_in_dim(resid, first_row, quarter, 0), moe_add], chips, 1)
    output = lax.all_gather(moe_add, "tensor", axis=0, tiled=True)[None]

    grad_resid, resid_low, grad_logits, grad_gain_two = route_back_call(
        grad_moe_in, gate_grads, gates, resid, cot, router_t, gain_two
    )

    grad_mixed = project_back_call(scal, after(resid_low, out_sum), out_pieces, out_places, shard, inner)
    query_back, grad_kv, grad_gain_q = attend_back_call(
        rot, kv_all, key_side, query_side, grad_mixed, mixed_low, inverse, raw, cosine, sine, gain_q, heads
    )
    grad_kv = after(grad_kv, moe_add).reshape(4, rows, 2 * HEAD)
    kv_got = to_core(rounded(jnp.stack([grad_kv[1], grad_kv[3]]))).astype(F32)
    kv_far = x_link.send(rounded(grad_kv[2] + kv_got[1])).astype(F32)
    kv_sum = grad_kv[0] + kv_got[0] + kv_far
    value_back = rounded(kv_sum[:, HEAD:])
    grad_key_n = rotate_back(kv_sum[:, :HEAD], cosine, sine)
    raw_key = raw[:, inner : inner + HEAD]
    scale_k = inverse_rms(raw_key)
    normal_k = raw_key * scale_k
    grad_gain_k = jnp.sum(grad_key_n * normal_k, 0)
    key_back = rounded(norm_back(grad_key_n * gain_k, scale_k, normal_k))
    qkv_back = jnp.concatenate([query_back, key_back, value_back], 1)

    back_part, grad_gain_one = qkv_back_call(scal, qkv_back, tokens_low, qkv_pieces, qkv_places, shard)
    grad_normed = lax.psum(back_part, "tensor")
    grad_hidden = by_rows(last_kernel, scal, [tokens_low, grad_resid, grad_normed, gain_one], chips, 3)[None]

    late_resid, late_mixed, late_normed, late_moe = lax.optimization_barrier(
        (resid_low, mixed_low, normed, moe_low, back_part)
    )[:4]
    grad_router_t = dot(grad_logits, late_moe, (0, 0))
    normed_sent, normed_own = (pick_columns(late_normed, scal, shard, other) for other in (True, False))
    qkv_sent = to_core(rounded(dot(normed_sent, qkv_back, (0, 0))))
    qkv_sum = dot(normed_own, qkv_back, (0, 0)) + qkv_sent.astype(F32)
    qkv_sum = rounded(qkv_sum)
    resid_sent, resid_own = (pick_columns(late_resid, scal, shard, other) for other in (True, False))
    out_sent = to_core(rounded(dot(late_mixed, resid_sent, (0, 0))))
    out_sum = dot(late_mixed, resid_own, (0, 0)) + out_sent.astype(F32)
    out_sum = rounded(out_sum)
    qkv_blocks = [qkv_sum[r * shard : (r + 1) * shard] for r in range(chips)]
    out_blocks = [out_sum[:, r * shard : (r + 1) * shard] for r in range(chips)]
    if paired:
        up_got = scatter_near(grad_blocks[2], after(up_far, query_back), 1, x_link, y_link)
        qkv_far = scatter_far(qkv_blocks, 0, x_link, y_link)
        out_far = scatter_far(out_blocks, 0, x_link, y_link)
        qkv_got = scatter_near(qkv_blocks, qkv_far, 0, x_link, y_link)
        out_got = scatter_near(out_blocks, out_far, 0, x_link, y_link)
        expert_sums = [
            scatter_sum(grad_blocks[0][0], after(down_got, query_back), 1),
            scatter_sum(grad_blocks[1][0], after(gate_got, back_part), 1),
            scatter_sum(grad_blocks[2][0], up_got, 1),
        ]
        grad_qkv = scatter_sum(qkv_blocks[0], qkv_got, 0)
        grad_out_weight = scatter_sum(out_blocks[0], out_got, 0)
    else:
        expert_sums = [scatter_whole(b) for b in grad_blocks]
        grad_qkv, grad_out_weight = scatter_whole(qkv_blocks), scatter_whole(out_blocks)

    def expert_grad(total):
        total = total.reshape(half, hid, span)
        own = lax.dynamic_slice_in_dim(total, core * shard, shard, 2)
        sent = lax.dynamic_slice_in_dim(total, (1 - core) * shard, shard, 2)
        other = to_core(rounded(sent)).astype(F32)
        return by_core(own, other, 0).reshape(EXPERTS, hid, shard)

    grad_down, grad_gate, grad_up = (expert_grad(v) for v in expert_sums)
    grad_gate, grad_up = grad_gate.transpose(0, 2, 1), grad_up.transpose(0, 2, 1)

    share = 1.0 / tensor
    head_rows = jnp.concatenate(
        [grad_gain_q.reshape(2 * chips, per), grad_gain_k.reshape(2 * chips, per)], 1
    )
    head_rows = relative(jnp.pad(head_rows, ((0, 0), (0, shard - 2 * per))).reshape(width))
    table = jnp.concatenate(
        [
            grad_gain_one,
            grad_gain_two * share,
            grad_router_t * share,
            head_rows[None],
            jnp.zeros((5, width), F32),
        ]
    ).reshape(24, chips, 2, shard)
    table_own = lax.dynamic_index_in_dim(table, core, 2, keepdims=False)
    table_sent = lax.dynamic_index_in_dim(table, 1 - core, 2, keepdims=False)
    table = table_own + to_core(table_sent)
    table = table.reshape(24, count, 2, shard)
    table = table[:, :, 0] + to_x(table[:, :, 1])
    if paired:
        table = table[:, 0] + to_dp(table[:, 1])
    else:
        table = lax.psum_scatter(table, "dp", scatter_dimension=1, tiled=False)
    mine = sum_z(table)
    gains = mine[2 + EXPERTS, : 2 * per]

    return (
        output,
        grad_hidden,
        mine[0],
        grad_qkv[:, :inner],
        grad_qkv[:, inner : inner + HEAD],
        grad_qkv[:, inner + HEAD :],
        gains[:per],
        gains[per:],
        grad_out_weight,
        mine[1],
        mine[2 : 2 + EXPERTS].T,
        grad_gate,
        grad_up,
        grad_down,
    )


def solution(mesh):
    plane = ("dp", "ctx")
    in_specs = (
        P("dp", "ctx", None),
        P("dp", "ctx", None),
        P(plane),
        P(plane, "tensor"),
        P(plane, "tensor"),
        P(plane, "tensor"),
        P(plane),
        P(plane),
        P("tensor", plane),
        P(plane),
        P(plane, None),
        P(None, plane, "tensor"),
        P(None, plane, "tensor"),
        P(None, "tensor", plane),
        P("dp", None),
        P("dp", None),
        P("dp", "ctx"),
        P("dp", "ctx", None),
    )
    out_specs = (
        P("dp", "ctx", None),
        P("dp", "ctx", None),
        P(plane),
        P(plane, "tensor"),
        P(plane, "tensor"),
        P(plane, "tensor"),
        P(plane),
        P(plane),
        P("tensor", plane),
        P(plane),
        P(plane, None),
        P(None, plane, "tensor"),
        P(None, plane, "tensor"),
        P(None, "tensor", plane),
    )
    return jax.shard_map(shards, mesh=mesh, in_specs=in_specs, out_specs=out_specs, check_vma=False)
```

```python
import functools
import math

import jax
import jax.numpy as jnp
from jax import lax
from jax.experimental import pallas as pl
from jax.experimental.pallas import tpu as pltpu
from jax.sharding import PartitionSpec as P

HEADS_Q = 32
HEADS_KV = 4
HEAD = 128
TOP = 8
EXPERTS = 16

EPS = 1e-06
THETA = 1000000.0
LOG2E = 1.4426950408889634
HIDE = -1e30

F32 = jnp.float32
BF16 = jnp.bfloat16
VMEM_BYTES = 58 * 1024 * 1024


def rounded(v):
    return v.astype(BF16)


def dot(a, b, contract):
    return lax.dot_general(a, b, ((contract[:1], contract[1:]), ((), ())), preferred_element_type=F32)


def after(value, *others):
    return lax.optimization_barrier((value,) + others)[0]


def to_core(v):
    return lax.ppermute(v, "ctx", [(i, i ^ 1) for i in range(4)])


def to_x(v):
    return lax.ppermute(v, "ctx", [(i, i ^ 2) for i in range(4)])


def to_dp(v):
    return lax.ppermute(v, "dp", [(0, 1), (1, 0)])


def exchange(x_value, y_value, *gate):
    x_value, y_value = after((x_value, y_value), *gate) if gate else lax.optimization_barrier((x_value, y_value))
    return lax.optimization_barrier((to_x(x_value), to_dp(y_value)))


def sum_z(v):
    size = lax.axis_size("tensor")
    one, two, three = (lax.ppermute(v, "tensor", [(i, i ^ k) for i in range(size)]) for k in (1, 2, 3))
    return (v + one) + (two + three)


def place():
    ctx = lax.axis_index("ctx")
    return lax.axis_index("dp"), ctx // 2, ctx % 2


def flips():
    dp, x, _ = place()
    return x + 2 * dp if lax.axis_size("dp") == 2 else x


def flip(v, axis, bit):
    return jnp.where(bit == 0, v, jnp.flip(v, axis))


def relative(v):
    dp, x, _ = place()
    count = lax.axis_size("dp")
    cut = v.reshape(v.shape[:-1] + (count, 2, v.shape[-1] // (2 * count)))
    cut = flip(cut, cut.ndim - 2, x)
    if count == 2:
        cut = flip(cut, cut.ndim - 3, dp)
    return cut.reshape(v.shape)


def halves(v, axis):
    return jnp.split(v, 2, axis)


def gather_whole(block, axis):
    pair = jnp.concatenate([block, to_x(block)], axis)
    return lax.all_gather(pair, "dp", axis=axis, tiled=True)


def scatter_whole(blocks):
    kept = jnp.stack(blocks[0::2]).astype(F32) + to_x(jnp.stack(blocks[1::2])).astype(F32)
    return lax.psum_scatter(rounded(kept), "dp", scatter_dimension=0, tiled=False).astype(F32)


def whole(array):
    dims = len(array.shape)
    return pl.BlockSpec(array.shape, lambda *_: (0,) * dims)


SCALARS = pl.BlockSpec(memory_space=pltpu.SMEM)


TIMES = {
    "permute_kernel": 4.6, "half_kernel": 4, "block_kernel": 6, "qkv_kernel": 11.7,
    "attend_kernel": 16.3, "attend_back_kernel": 30, "project_kernel": 6.6, "project_back_kernel": 6.5,
    "kv_pass_kernel": 2, "qkv_back_kernel": 9.8, "products_kernel": 11.8, "experts_kernel": 20,
    "spread_kernel": 10, "join_kernel": 4.6, "weight_grad_kernel": 50, "met_kernel": 0.5, "total_kernel": 0.5,
    "lay_kernel": 0.5, "pair_grad_kernel": 0.5, "columns_grad_kernel": 0.5, "cut_kernel": 0.3, "end_kernel": 0.3,
    "route_kernel": 6.3, "route_back_kernel": 8.6, "add_kernel": 2.2, "last_kernel": 6.2,
}


def cost(body):
    name = getattr(body, "func", body).__name__
    return pl.CostEstimate(flops=int(TIMES.get(name, 0.3) * 1e9), bytes_accessed=0, transcendentals=0)


def kernel_call(body, grid, in_specs, out_specs, out_shape, flops, moved, scratch=()):
    return pl.pallas_call(
        body,
        grid=grid,
        in_specs=in_specs,
        out_specs=out_specs,
        out_shape=out_shape,
        scratch_shapes=list(scratch),
        compiler_params=pltpu.CompilerParams(vmem_limit_bytes=VMEM_BYTES),
        cost_estimate=cost(body),
    )


def sds(shape, dtype):
    return jax.ShapeDtypeStruct(shape, dtype)


def piece_starts(scal, places, shard):
    core = scal[1]
    shift = {0: 0, 1: core * shard, 2: (1 - core) * shard}
    return [
        (start if kind == 0 else pl.multiple_of(start + shift[kind], length), length)
        for start, length, kind in places
    ]


def kernel_inverse_rms(v):
    return lax.rsqrt(jnp.mean(v * v, axis=-1, keepdims=True) + EPS)


def permute_kernel(scal, in_ref, out_ref):
    out_ref[...] = in_ref[...]


def permute_width(v, scal, blocks):
    rows, width = v.shape
    span = width // blocks
    return pl.pallas_call(
        permute_kernel,
        grid_spec=pltpu.PrefetchScalarGridSpec(
            num_scalar_prefetch=1,
            grid=(blocks,),
            in_specs=[pl.BlockSpec((rows, span), lambda j, s: (0, j ^ s[0]))],
            out_specs=pl.BlockSpec((rows, span), lambda j, s: (0, j)),
        ),
        out_shape=sds(v.shape, v.dtype),
        cost_estimate=cost(permute_kernel),
    )(scal, v)


def pick_columns(v, scal, shard, other):
    rows, width = v.shape
    count = width // (2 * shard)
    which = 1 - scal[1] if other else scal[1]
    cut = v.reshape(rows, count, 2, shard)
    return lax.dynamic_index_in_dim(cut, which, 2, keepdims=False).reshape(rows, count * shard)


def prefetch_call(body, scal, grid, in_specs, out_specs, out_shape, arrays, scratch=()):
    return pl.pallas_call(
        body,
        grid_spec=pltpu.PrefetchScalarGridSpec(
            num_scalar_prefetch=1,
            grid=grid,
            in_specs=in_specs,
            out_specs=out_specs,
            scratch_shapes=list(scratch),
        ),
        out_shape=out_shape,
        compiler_params=pltpu.CompilerParams(vmem_limit_bytes=VMEM_BYTES),
        cost_estimate=cost(body),
    )(scal, *arrays)


def half_kernel(scal, *refs):
    ins, out = refs[:3], refs[3]
    for m in range(3):

        @pl.when(pl.program_id(0) == m)
        def _():
            out[0] = ins[m][...]


def other_half_call(scal, weights):
    experts, hid, shard = weights[0].shape
    half = experts // 2
    return prefetch_call(
        half_kernel,
        scal,
        (3,),
        [pl.BlockSpec((half, hid, shard), lambda m, s: (1 - s[1], 0, 0))] * 3,
        pl.BlockSpec((1, half, hid, shard), lambda m, s: (m, 0, 0, 0)),
        sds((3, half, hid, shard), BF16),
        weights,
    )


def block_kernel(scal, *refs):
    ins, got, out = refs[:3], refs[3], refs[4]
    shard = got.shape[3]
    rows = out.shape[0]
    other = pl.ds(pl.multiple_of((1 - scal[1]) * shard, shard), shard)
    out[:, other] = got[0].reshape(rows, shard)
    for m in range(3):

        @pl.when(pl.program_id(0) == m)
        def _():
            out[:, pl.ds(pl.multiple_of(scal[1] * shard, shard), shard)] = ins[m][...].reshape(rows, shard)


def block_call(scal, weights, got):
    experts, hid, shard = weights[0].shape
    half = experts // 2
    return prefetch_call(
        block_kernel,
        scal,
        (3,),
        [pl.BlockSpec((half, hid, shard), lambda m, s: (s[1], 0, 0))] * 3
        + [pl.BlockSpec((1, half, hid, shard), lambda m, s: (m, 0, 0, 0))],
        pl.BlockSpec((half * hid, 2 * shard), lambda m, s: (m, 0)),
        sds((3 * half * hid, 2 * shard), BF16),
        [*weights, got],
    )


def read_small(places, shard, per, scal, pieces, gain_one, gain_two, router_t, gain_q, gain_k):
    gain_q[...] = jnp.zeros(gain_q.shape, F32)
    gain_k[...] = jnp.zeros(gain_k.shape, F32)
    lane = lax.broadcasted_iota(jnp.int32, (shard // 2, HEAD), 0)
    target = lax.broadcasted_iota(jnp.int32, (shard // 2, HEAD), 1)
    for (start, length), (fixed, _, kind), ref in zip(piece_starts(scal, places, shard), places, pieces):
        value = ref[...].astype(F32).T
        lanes = pl.ds(start, length)
        router_t[:, lanes] = rounded(value[:EXPERTS])
        gain_one[:, lanes] = value[EXPERTS : EXPERTS + 1]
        gain_two[:, lanes] = value[EXPERTS + 1 : EXPERTS + 2]
        if fixed % shard:
            continue
        half = scal[1] if kind == 1 else 1 - scal[1]
        heads = rounded(value[EXPERTS + 2 : EXPERTS + 3, : shard // 2])
        first = (2 * ((fixed // (2 * shard)) ^ scal[0]) + half) * per
        in_q = (target == first + lane) & (lane < per)
        in_k = (target == first + lane - per) & (lane >= per) & (lane < 2 * per)
        gain_q[...] += dot(heads, jnp.where(in_q, 1.0, 0.0).astype(BF16), (1, 0))
        gain_k[...] += dot(heads, jnp.where(in_k, 1.0, 0.0).astype(BF16), (1, 0))


def qkv_kernel(places, shard, per, blocks, given, scal, hid, cos, sin, *refs):
    n = len(places)
    weights, refs = refs[:n], refs[n:]
    if given:
        gain, gain_q, gain_k, normed, hid_rel, raw, rot = refs
    else:
        smalls, (gain, gain_two, router_t, gain_q, gain_k, normed, hid_rel, raw, rot) = refs[:n], refs[n:]
    step, last = pl.program_id(0), pl.num_programs(0) - 1
    width = hid.shape[1]
    span = width // blocks

    @pl.when(step == 0)
    def _():
        if not given:
            read_small(places, shard, per, scal, smalls, gain, gain_two, router_t, gain_q, gain_k)
        for j in range(blocks):
            source = pl.multiple_of((scal[0] ^ j) * span, span)
            hid_rel[:, j * span : (j + 1) * span] = hid[:, pl.ds(source, span)]
        tokens = hid_rel[...].astype(F32)
        normed[...] = rounded(tokens * kernel_inverse_rms(tokens) * gain[...])

    total = jnp.zeros(raw.shape, F32)
    for (start, length), weight in zip(piece_starts(scal, places, shard), weights):
        total += dot(normed[:, pl.ds(start, length)], weight[...], (1, 0))
    raw[...] = total
    vector = jnp.where(step == last, gain_k[...], gain_q[...])
    for head in range(2):
        cut = total[:, head * HEAD : (head + 1) * HEAD]
        scaled = cut * kernel_inverse_rms(cut) * vector
        turned = scaled * cos[...] + pltpu.roll(scaled, HEAD // 2, 1) * sin[...]
        if head == 1:
            turned = jnp.where(step == last, cut, turned)
        rot[:, head * HEAD : (head + 1) * HEAD] = rounded(turned)


def qkv_call(scal, hid, gains, cos, sin, pieces, places, shard, per, blocks, columns):
    rows, width = hid.shape
    pair = 2 * HEAD
    block = pl.BlockSpec((rows, pair), lambda i: (0, i))
    weights = [pl.BlockSpec((p.shape[0], pair), lambda i: (0, i)) for p in pieces]
    outs = [sds(hid.shape, BF16), sds(hid.shape, BF16), sds((rows, columns), F32), sds((rows, columns), BF16)]
    specs = [whole(hid), whole(hid), block, block]
    if gains:
        more, more_specs = list(gains), [whole(g) for g in gains]
    else:
        more = pieces
        more_specs = [pl.BlockSpec((p.shape[0], HEAD), lambda i: (0, columns // HEAD)) for p in pieces]
        found = [
            sds((1, width), F32),
            sds((1, width), F32),
            sds((EXPERTS, width), BF16),
            sds((1, HEAD), F32),
            sds((1, HEAD), F32),
        ]
        outs, specs = found + outs, [whole(v) for v in found] + specs
    return kernel_call(
        functools.partial(qkv_kernel, places, shard, per, blocks, bool(gains)),
        (columns // pair,),
        [SCALARS, whole(hid), whole(cos), whole(sin)] + weights + more_specs,
        specs,
        outs,
        0,
        0,
    )(scal, hid, cos, sin, *pieces, *more)


def write_bias(bias, key_side, query_side):
    seg = key_side[:, 0:1]
    seen = (seg == query_side[0:1]) | (seg == query_side[1:2]) | (seg == query_side[2:3])
    seen = seen & (key_side[:, 1:2] <= query_side[3:4])
    bias[...] = jnp.where(seen, 0.0, HIDE)


def key_tiles(count):
    tile = next(t for t in (384, 320, 256, 128) if count % t == 0)
    return [(s, tile) for s in range(0, count, tile)]


def attend_kernel(query, keys, values, key_side, query_side, mixed, inverse, bias, values_t):
    @pl.when(pl.program_id(0) == 0)
    def _():
        write_bias(bias, key_side[...], query_side[...])
        values_t[...] = values[...].T

    rows = query.shape[0]
    total = jnp.zeros((HEAD, rows), F32)
    row_sum = jnp.zeros((1, rows), F32)
    factor = LOG2E * HEAD**-0.5
    for start, tile in key_tiles(keys.shape[0]):
        raw = dot(keys[start : start + tile], query[...], (1, 1))
        weight = jnp.exp2(raw * factor + bias[start : start + tile])
        row_sum += jnp.sum(weight, 0, keepdims=True)
        total += dot(values_t[:, start : start + tile], rounded(weight), (1, 0))
    scale = 1.0 / row_sum
    mixed[...] = rounded((total * scale).T)
    inverse[0] = scale


def attend_call(rot, kv_all, key_side, query_side, heads):
    rows, count = rot.shape[0], kv_all.shape[0]
    column = pl.BlockSpec((rows, HEAD), lambda h: (0, h))
    return kernel_call(
        attend_kernel,
        (heads,),
        [
            column,
            pl.BlockSpec((count, HEAD), lambda h: (0, 0)),
            pl.BlockSpec((count, HEAD), lambda h: (0, 1)),
            whole(key_side),
            whole(query_side),
        ],
        [column, pl.BlockSpec((1, 1, rows), lambda h: (h, 0, 0))],
        [sds((rows, heads * HEAD), BF16), sds((heads, 1, rows), F32)],
        4 * heads * rows * count * HEAD,
        4 * rows * heads * HEAD + 4 * count * HEAD,
        [pltpu.VMEM((count, rows), F32), pltpu.VMEM((HEAD, count), BF16)],
    )(rot, kv_all, kv_all, key_side, query_side)


def attend_back_kernel(
    query, keys, values, key_side, query_side, grad, mixed, inverse, raw_query, cos, sin, gain,
    query_back, kv_own, kv_sent, kv_mid, grad_gain, bias, keys_t, grad_kv,
):
    @pl.when(pl.program_id(0) == 0)
    def _():
        write_bias(bias, key_side[...], query_side[...])
        keys_t[...] = keys[...].T
        grad_kv[...] = jnp.zeros(grad_kv.shape, F32)
        grad_gain[...] = jnp.zeros(grad_gain.shape, F32)

    rows = query.shape[0]
    scale = HEAD**-0.5
    factor = LOG2E * scale
    both = grad[...].astype(F32) * mixed[...].astype(F32)
    mean = jnp.sum(both.T, 0, keepdims=True)
    norm = inverse[0]
    total = jnp.zeros((HEAD, rows), F32)
    for start, tile in key_tiles(keys.shape[0]):
        span = slice(start, start + tile)
        raw = dot(keys[span], query[...], (1, 1))
        prob = jnp.exp2(raw * factor + bias[span]) * norm
        grad_prob = dot(values[span], grad[...], (1, 1))
        grad_raw = rounded(prob * (grad_prob - mean) * scale)
        total += dot(keys_t[:, span], grad_raw, (1, 0))
        grad_kv[span, :HEAD] += dot(grad_raw, query[...], (1, 0))
        grad_kv[span, HEAD:] += dot(rounded(prob), grad[...], (1, 0))
    turned = total.T
    turned = turned * cos[...] - pltpu.roll(turned, HEAD // 2, 1) * sin[...]
    value = raw_query[...]
    shrink = kernel_inverse_rms(value)
    normal = value * shrink
    grad_gain[...] += jnp.sum(turned * normal, 0, keepdims=True)
    scaled = turned * gain[...]
    middle = jnp.mean(scaled * normal, axis=-1, keepdims=True)
    query_back[...] = rounded(shrink * (scaled - normal * middle))

    @pl.when(pl.program_id(0) == pl.num_programs(0) - 1)
    def _():
        kv_own[...] = grad_kv[:rows]
        kv_sent[:rows] = rounded(grad_kv[rows : 2 * rows])
        kv_mid[...] = grad_kv[2 * rows : 3 * rows]
        kv_sent[rows:] = rounded(grad_kv[3 * rows :])


def attend_back_call(rot, kv_all, key_side, query_side, grad, mixed, inverse, raw, cos, sin, gain, heads):
    rows, count = rot.shape[0], kv_all.shape[0]
    column = pl.BlockSpec((rows, HEAD), lambda h: (0, h))
    return kernel_call(
        attend_back_kernel,
        (heads,),
        [
            column,
            pl.BlockSpec((count, HEAD), lambda h: (0, 0)),
            pl.BlockSpec((count, HEAD), lambda h: (0, 1)),
            whole(key_side),
            whole(query_side),
            column,
            column,
            pl.BlockSpec((1, 1, rows), lambda h: (h, 0, 0)),
            column,
            whole(cos),
            whole(sin),
            whole(gain),
        ],
        [
            column,
            pl.BlockSpec((rows, 2 * HEAD), lambda h: (0, 0)),
            pl.BlockSpec((2 * rows, 2 * HEAD), lambda h: (0, 0)),
            pl.BlockSpec((rows, 2 * HEAD), lambda h: (0, 0)),
            pl.BlockSpec((1, HEAD), lambda h: (0, 0)),
        ],
        [
            sds((rows, heads * HEAD), BF16),
            sds((rows, 2 * HEAD), F32),
            sds((2 * rows, 2 * HEAD), BF16),
            sds((rows, 2 * HEAD), F32),
            sds((1, HEAD), F32),
        ],
        10 * heads * rows * count * HEAD,
        12 * rows * heads * HEAD + 12 * count * HEAD,
        [
            pltpu.VMEM((count, rows), F32),
            pltpu.VMEM((HEAD, count), BF16),
            pltpu.VMEM((count, 2 * HEAD), F32),
        ],
    )(rot, kv_all, kv_all, key_side, query_side, grad, mixed, inverse, raw, cos, sin, gain)


def project_kernel(places, shard, scal, mixed, *refs):
    out = refs[-1]
    for (start, length), weight in zip(piece_starts(scal, places, shard), refs[:-1]):
        out[:, pl.ds(start, length)] = rounded(dot(mixed[...], weight[...], (1, 0)))


def project_call(scal, mixed, pieces, places, shard, width):
    rows, inner = mixed.shape
    return kernel_call(
        functools.partial(project_kernel, places, shard),
        (1,),
        [SCALARS, whole(mixed)] + [whole(p) for p in pieces],
        pl.BlockSpec((rows, width), lambda i: (0, 0)),
        sds((rows, width), BF16),
        2 * rows * inner * width,
        2 * inner * width + 2 * rows * (inner + width),
    )(scal, mixed, *pieces)


def project_back_kernel(places, shard, scal, grad, *refs):
    out = refs[-1]
    total = jnp.zeros(out.shape, F32)
    for (start, length), weight in zip(piece_starts(scal, places, shard), refs[:-1]):
        total += dot(grad[:, pl.ds(start, length)], weight[...], (1, 1))
    out[...] = rounded(total)


def project_back_call(scal, grad, pieces, places, shard, inner):
    rows, width = grad.shape
    tile = inner // 2
    return kernel_call(
        functools.partial(project_back_kernel, places, shard),
        (2,),
        [SCALARS, whole(grad)] + [pl.BlockSpec((tile, p.shape[1]), lambda i: (i, 0)) for p in pieces],
        pl.BlockSpec((rows, tile), lambda i: (0, i)),
        sds((rows, inner), BF16),
        2 * rows * inner * width,
        2 * inner * width + 2 * rows * (inner + width),
    )(scal, grad, *pieces)


def kv_pass_kernel(own, mid, got, part, sent):
    rows = own.shape[0]
    part[...] = own[...] + got[:rows].astype(F32)
    sent[...] = rounded(mid[...] + got[rows:].astype(F32))


def kv_pass_call(own, mid, got):
    return kernel_call(
        kv_pass_kernel,
        (1,),
        [whole(own), whole(mid), whole(got)],
        [whole(own), whole(own)],
        [sds(own.shape, F32), sds(own.shape, BF16)],
        0,
        0,
    )(own, mid, got)


def qkv_back_kernel(
    places, shard, scal, query_back, kv_part, kv_far, raw_key, cos, sin, gain_k, hid, *refs
):
    weights, (part, grad_gain, kv_back, grad_gain_k) = refs[: len(places)], refs[len(places) :]
    inner = query_back.shape[1]
    total = kv_part[...] + kv_far[...].astype(F32)
    turned = total[:, :HEAD]
    turned = turned * cos[...] - pltpu.roll(turned, HEAD // 2, 1) * sin[...]
    value = raw_key[...]
    shrink = kernel_inverse_rms(value)
    normal = value * shrink
    grad_gain_k[...] = jnp.sum(turned * normal, 0, keepdims=True)
    scaled = turned * gain_k[...]
    middle = jnp.mean(scaled * normal, axis=-1, keepdims=True)
    kv_back[:, :HEAD] = rounded(shrink * (scaled - normal * middle))
    kv_back[:, HEAD:] = rounded(total[:, HEAD:])

    tokens = hid[...].astype(F32)
    shrink = kernel_inverse_rms(tokens)
    for (start, length), weight in zip(piece_starts(scal, places, shard), weights):
        lanes = pl.ds(start, length)
        value = dot(query_back[...], weight[:, :inner], (1, 1))
        value += dot(kv_back[...], weight[:, inner : inner + 2 * HEAD], (1, 1))
        part[:, lanes] = rounded(value)
        normal = hid[:, lanes].astype(F32) * shrink
        grad_gain[:, lanes] = jnp.sum(value * normal, 0, keepdims=True)


def qkv_back_call(scal, query_back, kv_part, kv_far, raw, cos, sin, gain_k, hid, pieces, places, shard):
    rows, width = hid.shape
    inner = query_back.shape[1]
    arrays = (cos, sin, gain_k, hid)
    outs = [sds((rows, width), BF16), sds((1, width), F32), sds((rows, 2 * HEAD), BF16), sds((1, HEAD), F32)]
    return kernel_call(
        functools.partial(qkv_back_kernel, places, shard),
        (1,),
        [SCALARS, whole(query_back), whole(kv_part), whole(kv_far)]
        + [pl.BlockSpec((rows, HEAD), lambda i: (0, inner // HEAD))]
        + [whole(a) for a in arrays]
        + [whole(p) for p in pieces],
        [whole(o) for o in outs],
        outs,
        0,
        0,
    )(scal, query_back, kv_part, kv_far, raw, *arrays, *pieces)


def join_rows(own, other, scratch):
    rows = own.shape[0]

    @pl.when(pl.program_id(0) == 0)
    def _():
        scratch[:rows] = own[...]
        scratch[rows:] = other[...]


def product(weights, rows_ref):
    return dot(jnp.concatenate([w[...] for w in weights], 1), rows_ref[...], (1, 1))


def single(shape):
    dims = len(shape)
    return pl.BlockSpec(shape, lambda *_: (0,) * dims, pipeline_mode=pl.Buffered(1))


def products_kernel(own, other, *refs):
    weights, (out, both, pair) = refs[:-3], refs[-3:]
    join_rows(own, other, both)
    out[...] = product(weights, both)

    @pl.when(pl.program_id(0) == 0)
    def _():
        pair[...] = both[...]


def row_pieces(pieces, tile, hidden):
    step = hidden // tile
    return [pl.BlockSpec((tile, a.shape[1]), lambda i, m=m: (i + m * step, 0)) for a, m in pieces]


def products_call(own, other, pieces, hidden):
    rows, width = own.shape
    tile = hidden // 4
    return kernel_call(
        products_kernel,
        (4,),
        [single(own.shape), single(own.shape)] + row_pieces(pieces, tile, hidden),
        [pl.BlockSpec((tile, 2 * rows), lambda i: (i, 0)), single((2 * rows, width))],
        [sds((hidden, 2 * rows), F32), sds((2 * rows, width), BF16)],
        0,
        0,
        [pltpu.VMEM((2 * rows, width), BF16)],
    )(own, other, *[a for a, _ in pieces])


def experts_kernel(hid, both, gate_ref, grad_act, gates, *refs):
    weights, (acts, acts_t, gate_part) = refs[:-3], refs[-3:]
    gate_pre, up_pre = gate_ref[...], product(weights, both)
    sig = 1.0 / (1.0 + jnp.exp(-gate_pre))
    silu = gate_pre * sig
    act = silu * up_pre
    slope = sig * (1.0 + gate_pre * (1.0 - sig))
    count = gates.shape[0]
    for e in range(count):
        rows = slice(e * hid, (e + 1) * hid)
        gate = gates[e]
        raw = grad_act[rows, :]
        back = gate * raw
        acts[0, rows, :] = rounded(gate * act[rows])
        acts[1, rows, :] = rounded(back * up_pre[rows] * slope[rows])
        acts[2, rows, :] = rounded(back * silu[rows])
        gate_part[e] = jnp.sum(act[rows] * raw, 0, keepdims=True)
    for k in range(3):
        acts_t[k] = acts[k].T


def experts_call(pair, gate_pre, grad_act, gates, pieces, hid):
    both, width = pair.shape
    experts = gates.shape[0]
    per = 2
    tile = per * hid
    hidden = experts * hid
    act = pl.BlockSpec((tile, both), lambda i: (i, 0))
    gate = pl.BlockSpec((per, 1, both), lambda i: (i, 0, 0))
    return kernel_call(
        functools.partial(experts_kernel, hid),
        (experts // per,),
        [single(pair.shape), act, act, gate] + row_pieces(pieces, tile, hidden),
        [
            pl.BlockSpec((3, tile, both), lambda i: (0, i, 0)),
            pl.BlockSpec((3, both, tile), lambda i: (0, 0, i)),
            gate,
        ],
        [sds((3, hidden, both), BF16), sds((3, both, hidden), BF16), sds((experts, 1, both), F32)],
        0,
        0,
    )(pair, gate_pre, grad_act, gates, *[a for a, _ in pieces])


def gate_sum_kernel(first, second, third, fourth, own, sent):
    rows = own.shape[1]
    for e in range(own.shape[0]):
        total = (first[e] + second[e]) + (third[e] + fourth[e])
        own[e : e + 1] = total[:, :rows]
        sent[e : e + 1] = total[:, rows:]


def gate_sum_call(part):
    size = lax.axis_size("tensor")
    there = [lax.ppermute(part, "tensor", [(i, i ^ k) for i in range(size)]) for k in (1, 2, 3)]
    out = sds((part.shape[0], part.shape[2] // 2), F32)
    own, sent = kernel_call(
        gate_sum_kernel, (1,), [whole(part)] * 4, [whole(out)] * 2, [out, out], 0, 0
    )(part, *there)
    return own, to_core(sent)


def gate_join_kernel(scal, own, got, out):
    first = jnp.where(scal[1] == 0, own[...], got[...])
    second = jnp.where(scal[1] == 0, got[...], own[...])
    out[...] = jnp.concatenate([first, second]).T


def gate_join_call(scal, own, got):
    out = sds((own.shape[1], 2 * own.shape[0]), F32)
    return kernel_call(gate_join_kernel, (1,), [SCALARS, whole(own), whole(got)], whole(out), out, 0, 0)(
        scal, own, got
    )


def backward_tiles(places, tile):
    return [(p, k) for p, (_, length, _) in enumerate(places) for k in range(length // tile)]


def spread_kernel(tiles, terms, joined, *refs):
    acts, out = refs[:terms], refs[-1]
    weights = refs[terms + joined : -1]
    n = len(weights) // terms
    step = pl.program_id(0)
    for p in range(n):
        steps = [t for t, (q, _) in enumerate(tiles) if q == p]

        @pl.when((step >= steps[0]) & (step <= steps[-1]))
        def _():
            value = sum(dot(acts[k][0], weights[k * n + p][...], (1, 0)) for k in range(terms))
            if joined:
                value += refs[terms][...].astype(F32)
            out[...] = rounded(value)


def spread_call(acts_t, which, tokens, weights, places, got=None):
    _, both, hidden = acts_t.shape
    rows = both // 2
    width = sum(length for _, length, _ in places)
    tile = 256
    tiles = backward_tiles(places, tile)

    def spec(p, m):
        steps = [t for t, (q, _) in enumerate(tiles) if q == p]
        first, last = steps[0], steps[-1]
        return pl.BlockSpec((hidden, tile), lambda t: (m, jnp.clip(t, first, last) - first))

    out = pl.BlockSpec((rows, tile), lambda t: (0, t))
    return kernel_call(
        functools.partial(spread_kernel, tiles, len(which), got is not None),
        (len(tiles),),
        [
            pl.BlockSpec((1, rows, hidden), lambda t, k=k: (k, tokens, 0), pipeline_mode=pl.Buffered(1))
            for k in which
        ]
        + ([] if got is None else [out])
        + [spec(p, m) for pieces in weights for p, (_, m) in enumerate(pieces)],
        out,
        sds((rows, width), BF16),
        0,
        0,
    )(*[acts_t] * len(which), *([] if got is None else [got]), *[a for pieces in weights for a, _ in pieces])


def weight_grad_kernel(left, first, second, *outs):
    def write(right):
        value = dot(left[0], right[...], (1, 0))
        start = 0
        for out in outs:
            length = out.shape[1]
            out[...] = rounded(value[:, start : start + length])
            start += length

    pl.when(pl.program_id(0) == 0)(lambda: write(first))
    pl.when(pl.program_id(0) > 0)(lambda: write(second))


def weight_grad_call(acts, first, second, lengths):
    _, hidden, both = acts.shape
    tile = hidden // 4
    return kernel_call(
        weight_grad_kernel,
        (3, 4),
        [pl.BlockSpec((1, tile, both), lambda m, i: (m, i, 0)), single(first.shape), single(second.shape)],
        [pl.BlockSpec((tile, n), lambda m, i: (4 * m + i, 0)) for n in lengths],
        [sds((3 * hidden, n), BF16) for n in lengths],
        0,
        0,
    )(acts, first, second)


def met_kernel(a, b, c, d, first, second):
    first[...] = rounded(a[...].astype(F32) + b[...].astype(F32))
    second[...] = rounded(c[...].astype(F32) + d[...].astype(F32))


def met_call(a, b, c, d):
    steps = 6 if a.shape[0] % 96 == 0 else 1
    left = pl.BlockSpec((a.shape[0] // steps, a.shape[1]), lambda i: (i, 0))
    return kernel_call(
        met_kernel, (steps,), [left] * 4, [left] * 2, [sds(a.shape, BF16)] * 2, 0, 0
    )(a, b, c, d)


def total_kernel(scal, own, x_first, y_first, x_second, y_second, mine, sent):
    shard = mine.shape[1]
    first = own[:, :shard].astype(F32) + x_first[...].astype(F32) + y_first[...].astype(F32)
    second = own[:, shard:].astype(F32) + x_second[...].astype(F32) + y_second[...].astype(F32)
    core = scal[1]
    mine[...] = jnp.where(core == 0, first, second)
    sent[...] = rounded(jnp.where(core == 0, second, first))


def total_call(scal, own, near):
    rows, span = own.shape
    tile = rows // 12
    half = pl.BlockSpec((tile, span // 2), lambda i: (i, 0))
    return kernel_call(
        total_kernel,
        (12,),
        [SCALARS, pl.BlockSpec((tile, span), lambda i: (i, 0))] + [half] * 4,
        [half] * 2,
        [sds((rows, span // 2), F32), sds((rows, span // 2), BF16)],
        0,
        0,
    )(scal, own, *near)


def lay_kernel(scal, *refs):
    mine, got, outs = refs[:3], refs[3:6], refs[6:]

    @pl.when(pl.program_id(0) == 0)
    def _():
        for m in range(3):
            outs[m][...] = mine[m][...]

    @pl.when(pl.program_id(0) == 1)
    def _():
        for m in range(3):
            outs[m][...] = got[m][...].astype(F32)


def lay_call(scal, mine, got):
    rows, shard = mine.shape
    part = rows // 3
    return prefetch_call(
        lay_kernel,
        scal,
        (2,),
        [pl.BlockSpec((part, shard), lambda i, s, m=m: (m, 0)) for m in range(3)] * 2,
        [pl.BlockSpec((part, shard), lambda i, s: (jnp.where(i == 0, s[1], 1 - s[1]), 0))] * 3,
        [sds((2 * part, shard), F32)] * 3,
        [mine] * 3 + [got] * 3,
    )


def pair_grad_kernel(scal, left_own, left_sent, first, second, own, sent):
    inner = first.shape[1]
    own[:, :inner] = dot(left_own[...], first[...], (0, 0))
    own[:, inner:] = dot(left_own[...], second[...], (0, 0))
    sent[:, :inner] = rounded(dot(left_sent[...], first[...], (0, 0)))
    sent[:, inner:] = rounded(dot(left_sent[...], second[...], (0, 0)))


def rows_grad_call(scal, left, first, second, shard):
    rows, width = left.shape
    columns = first.shape[1] + second.shape[1]
    count = width // (2 * shard)
    return prefetch_call(
        pair_grad_kernel,
        scal,
        (count,),
        [
            pl.BlockSpec((rows, shard), lambda r, s: (0, 2 * r + s[1])),
            pl.BlockSpec((rows, shard), lambda r, s: (0, 2 * r + 1 - s[1])),
            pl.BlockSpec(first.shape, lambda r, s: (0, 0)),
            pl.BlockSpec(second.shape, lambda r, s: (0, 0)),
        ],
        [pl.BlockSpec((shard, columns), lambda r, s: (r, 0))] * 2,
        [sds((count * shard, columns), F32), sds((count * shard, columns), BF16)],
        [left, left, first, second],
    )


def columns_grad_kernel(scal, left, right_own, right_sent, own, sent, left_t):
    @pl.when(pl.program_id(0) == 0)
    def _():
        left_t[...] = left[...].T

    own[...] = dot(left_t[...], right_own[...], (1, 0))
    sent[...] = rounded(dot(left_t[...], right_sent[...], (1, 0)))


def columns_grad_call(scal, left, right, shard):
    rows, inner = left.shape
    count = right.shape[1] // (2 * shard)
    return pl.pallas_call(
        columns_grad_kernel,
        grid_spec=pltpu.PrefetchScalarGridSpec(
            num_scalar_prefetch=1,
            grid=(count,),
            in_specs=[
                pl.BlockSpec((rows, inner), lambda r, s: (0, 0)),
                pl.BlockSpec((rows, shard), lambda r, s: (0, 2 * r + s[1])),
                pl.BlockSpec((rows, shard), lambda r, s: (0, 2 * r + 1 - s[1])),
            ],
            out_specs=[pl.BlockSpec((inner, shard), lambda r, s: (0, r))] * 2,
            scratch_shapes=[pltpu.VMEM((inner, rows), BF16)],
        ),
        out_shape=[sds((inner, count * shard), F32), sds((inner, count * shard), BF16)],
        compiler_params=pltpu.CompilerParams(vmem_limit_bytes=VMEM_BYTES),
        cost_estimate=cost(columns_grad_kernel),
    )(scal, left, right, right)


def cut_kernel(axis, mine, got, *outs):
    value = rounded(mine[...] + got[...].astype(F32))
    start = 0
    for out in outs:
        length = out.shape[axis]
        out[...] = lax.slice_in_dim(value, start, start + length, axis=axis)
        start += length


def cut_call(mine, got, axis):
    eighth = mine.shape[axis] // 8
    shapes = []
    for length in [2 * eighth] + [eighth] * 6:
        shape = list(mine.shape)
        shape[axis] = length
        shapes.append(sds(tuple(shape), BF16))
    return kernel_call(
        functools.partial(cut_kernel, axis),
        (1,),
        [whole(mine), whole(got)],
        [whole(v) for v in shapes],
        shapes,
        0,
        0,
    )(mine, got)


def end_kernel(axis, own, x_first, y_first, x_second, y_second, *outs):
    value = own[...].astype(F32)
    size = x_first.shape[axis]
    first = lax.slice_in_dim(value, 0, size, axis=axis) + x_first[...].astype(F32) + y_first[...].astype(F32)
    second = lax.slice_in_dim(value, size, 2 * size, axis=axis)
    second = second + x_second[...].astype(F32) + y_second[...].astype(F32)
    value = jnp.concatenate([first, second], axis)
    start = 0
    for out in outs:
        length = out.shape[1]
        out[...] = value[:, start : start + length]
        start += length


def end_call(own, near, axis, lengths):
    outs = [sds((own.shape[0], n), F32) for n in lengths]
    return kernel_call(
        functools.partial(end_kernel, axis),
        (1,),
        [whole(own)] + [whole(v) for v in near],
        [whole(v) for v in outs],
        outs,
        0,
        0,
    )(own, *near)


def route_kernel(top_count, hid, attn_add, gain, router_t, routes, resid, moe_low, gates):
    value = hid[...].astype(F32) + attn_add[...].astype(F32)
    resid[...] = value
    moe_low[...] = rounded(value * kernel_inverse_rms(value) * gain[...])
    logits = dot(moe_low[...], router_t[...], (1, 1))
    numbers = lax.broadcasted_iota(jnp.int32, logits.shape, 1)
    chosen = routes[:, 0:1] == numbers
    for k in range(1, top_count):
        chosen = chosen | (routes[:, k : k + 1] == numbers)
    top = jnp.max(jnp.where(chosen, logits, HIDE), -1, keepdims=True)
    lift = jnp.where(chosen, jnp.exp(jnp.where(chosen, logits, top) - top), 0.0)
    gates[...] = lift / jnp.sum(lift, -1, keepdims=True)


def row_specs(arrays, rows, tile):
    return [
        pl.BlockSpec((tile, a.shape[1]), lambda i: (i, 0)) if a.shape[0] == rows else whole(a) for a in arrays
    ]


def route_call(hid, attn_add, gain, router_t, routes):
    rows, width = hid.shape
    tile = rows // 3
    arrays = (hid, attn_add, gain, router_t, routes)
    outs = [sds((rows, width), F32), sds((rows, width), BF16), sds((rows, router_t.shape[0]), F32)]
    return kernel_call(
        functools.partial(route_kernel, routes.shape[1]),
        (3,),
        row_specs(arrays, rows, tile),
        row_specs(outs, rows, tile),
        outs,
        40 * rows * width,
        10 * rows * width,
    )(*arrays)


def route_back_kernel(
    grad_moe, gate_grads, gates, resid, cot, router_t, gain, grad_resid, resid_low, grad_logits, grad_gain
):
    chosen = gates[...]
    part = gate_grads[...]
    middle = jnp.sum(chosen * part, -1, keepdims=True)
    grad_logits[...] = rounded(chosen * (part - middle))
    total = grad_moe[...].astype(F32) + dot(grad_logits[...], router_t[...], (1, 0))
    value = resid[...]
    shrink = kernel_inverse_rms(value)
    normal = value * shrink

    @pl.when(pl.program_id(0) == 0)
    def _():
        grad_gain[...] = jnp.zeros(grad_gain.shape, F32)

    grad_gain[...] += jnp.sum(total * normal, 0, keepdims=True)
    scaled = total * gain[...]
    mean = jnp.mean(scaled * normal, axis=-1, keepdims=True)
    out = cot[...].astype(F32) + shrink * (scaled - normal * mean)
    grad_resid[...] = out
    resid_low[...] = rounded(out)


def route_back_call(grad_moe, gate_grads, gates, resid, cot, router_t, gain):
    rows, width = resid.shape
    tile = rows // 3
    arrays = (grad_moe, gate_grads, gates, resid, cot, router_t, gain)
    outs = [
        sds((rows, width), F32),
        sds((rows, width), BF16),
        sds(gates.shape, BF16),
        sds((1, width), F32),
    ]
    return kernel_call(
        route_back_kernel,
        (3,),
        row_specs(arrays, rows, tile),
        row_specs(outs, rows, tile),
        outs,
        50 * rows * width,
        14 * rows * width,
    )(*arrays)


def to_whole_order(scal, blocks, value, out):
    span = value.shape[1] // blocks
    for j in range(blocks):
        target = pl.multiple_of((scal[0] ^ j) * span, span)
        out[:, pl.ds(target, span)] = value[:, j * span : (j + 1) * span]


def add_kernel(blocks, scal, first, second, out):
    value = rounded(first[...] + second[...].astype(F32))
    to_whole_order(scal, blocks, value, out)


def add_call(scal, resid, part, blocks):
    rows, width = part.shape
    return prefetch_call(
        functools.partial(add_kernel, blocks),
        scal,
        (1,),
        [pl.BlockSpec((rows, width), lambda i, s: (s[2], 0)), pl.BlockSpec((rows, width), lambda i, s: (0, 0))],
        pl.BlockSpec((rows, width), lambda i, s: (0, 0)),
        sds((rows, width), BF16),
        [resid, part],
    )


def last_kernel(blocks, scal, hid, grad_resid, grad_normed, gain, out, wide):
    wide[...] = hid[...].astype(F32)
    rows = out.shape[0]
    tokens = wide[pl.ds(pl.multiple_of(scal[2] * rows, 8), rows)]
    shrink = kernel_inverse_rms(tokens)
    normal = tokens * shrink
    scaled = grad_normed[...].astype(F32) * gain[...]
    middle = jnp.mean(scaled * normal, axis=-1, keepdims=True)
    value = rounded(grad_resid[...] + shrink * (scaled - normal * middle))
    to_whole_order(scal, blocks, value, out)


def last_call(scal, hid, grad_resid, grad_normed, gain, blocks):
    rows, width = grad_normed.shape
    part = pl.BlockSpec((rows, width), lambda i, s: (0, 0))
    return prefetch_call(
        functools.partial(last_kernel, blocks),
        scal,
        (1,),
        [whole(hid), pl.BlockSpec((rows, width), lambda i, s: (s[2], 0)), part, whole(gain)],
        part,
        sds((rows, width), BF16),
        [hid, grad_resid, grad_normed, gain],
        [pltpu.VMEM(hid.shape, F32)],
    )


def angle_tables(positions):
    half_size = HEAD // 2
    frequency = jnp.exp(jnp.arange(half_size, dtype=F32) * (-2.0 * math.log(THETA) / HEAD))
    angles = positions.astype(F32)[..., None] * frequency
    sine = jnp.sin(angles)
    cosine = jnp.cos(angles)
    return jnp.concatenate([cosine, cosine], -1), jnp.concatenate([-sine, sine], -1)


def lookup_parent(segment_ids, parent):
    seg_table = jnp.arange(parent.shape[-1], dtype=jnp.int32)
    return jnp.sum(jnp.where(segment_ids[..., None] == seg_table, parent, 0), -1)


def shards(
    hidden,
    cotangent,
    gain_attn,
    query_weight,
    key_weight,
    value_weight,
    gain_query,
    gain_key,
    out_weight,
    gain_moe,
    router_weight,
    gate_weight,
    up_weight,
    down_weight,
    segment,
    parent,
    tree_depth,
    routes,
):
    _, rows, width = hidden.shape
    dp, x, core = place()
    ctx = lax.axis_index("ctx")
    count = lax.axis_size("dp")
    paired = count == 2
    chips = 2 * count
    tensor = lax.axis_size("tensor")
    heads = HEADS_Q // tensor
    shard = query_weight.shape[0]
    span = 2 * shard
    inner = heads * HEAD
    columns = inner + 2 * HEAD
    half = EXPERTS // 2
    hid = down_weight.shape[1]
    scal = jnp.stack([flips(), core, lax.axis_index("tensor")]).astype(jnp.int32)
    hidden_rows = half * hid

    def by_core(own, other, axis):
        return jnp.where(core == 0, jnp.stack([own, other], axis), jnp.stack([other, own], axis))

    def five_places(size):
        starts = [0, span, 2 * span, 3 * span, 3 * span + size // 2]
        return list(zip(starts, [size, size, size, size // 2, size // 2], [0] * 5))

    def both_cores(own, size):
        return own + [to_core(a) for a in own], [(s, n, k) for k in (1, 2) for s, n, _ in five_places(size)]

    def whole_piece(block, axis):
        own = gather_whole(block, axis)
        cut = own.shape[:axis] + (chips, shard) + own.shape[axis + 1 :]
        full = by_core(own.reshape(cut), to_core(own).reshape(cut), axis + 1)
        return [full.reshape(own.shape[:axis] + (width,) + own.shape[axis + 1 :])], [(0, width, 0)]

    per = gain_query.shape[0]
    heads_column = jnp.pad(jnp.concatenate([gain_query, gain_key]), (0, shard - 2 * per))
    small = [router_weight, gain_attn[:, None], gain_moe[:, None], heads_column[:, None]]
    small.append(jnp.zeros((shard, HEAD - EXPERTS - 3), BF16))
    qkv_shard = jnp.concatenate([query_weight, key_weight, value_weight] + small, 1)
    expert_weights = [down_weight, gate_weight.transpose(0, 2, 1), up_weight.transpose(0, 2, 1)]
    if paired:
        qkv_x, qkv_y = exchange(qkv_shard, qkv_shard)
        expert_block = block_call(scal, expert_weights, to_core(other_half_call(scal, expert_weights)))
        far_second, far_first = exchange(halves(qkv_y, 0)[1], halves(qkv_x, 0)[0], expert_block)
        qkv_pieces, qkv_places = both_cores([qkv_shard, qkv_x, qkv_y, far_first, far_second], shard)
        out_x, out_y = exchange(out_weight, out_weight, far_first, far_second)
        out_far_second, out_far_first = exchange(halves(out_y, 1)[1], halves(out_x, 1)[0])
        out_pieces, out_places = both_cores([out_weight, out_x, out_y, out_far_first, out_far_second], shard)
        gains = ()
    else:
        qkv_pieces, qkv_places = whole_piece(qkv_shard, 0)
        small_t = qkv_pieces[0][:, columns:].T
        router_t = small_t[:EXPERTS]
        gain_one, gain_two = (small_t[EXPERTS + i][None].astype(F32) for i in range(2))
        gain_heads = relative(small_t[EXPERTS + 2]).reshape(2 * chips, shard).astype(F32)
        gain_q = gain_heads[:, :per].reshape(1, HEAD)
        gain_k = gain_heads[:, per : 2 * per].reshape(1, HEAD)
        gains = (gain_one, gain_q, gain_k)
        out_pieces, out_places = whole_piece(out_weight, 1)
        sent = [lax.dynamic_slice_in_dim(w, (1 - core) * half, half, 0) for w in expert_weights]
        own = [lax.dynamic_slice_in_dim(w, core * half, half, 0) for w in expert_weights]
        expert_block = by_core(jnp.stack(own), to_core(jnp.stack(sent)), 3).reshape(3 * hidden_rows, span)

    cosine, sine = angle_tables(tree_depth[0])
    *found, normed, tokens_low, raw, rot = qkv_call(
        scal, hidden[0], gains, cosine, sine, qkv_pieces, qkv_places, shard, per, chips, columns
    )
    if found:
        gain_one, gain_two, router_t, gain_q, gain_k = found
    key_value = rot[:, inner:]
    kv_x = to_x(key_value)
    kv_other = to_core(key_value)
    kv_all = jnp.concatenate([key_value, kv_other, kv_x, to_core(kv_x)])
    if paired:
        near_x, near_y = exchange(expert_block, expert_block, kv_x, out_far_first)
        forwarded, expert_pieces = [], []
        gate = ()
        for m in range(3):
            rows_of = slice(m * hidden_rows, (m + 1) * hidden_rows)
            forwarded.append((near_y[rows_of, shard:], near_x[rows_of, :shard]))
            far_second, far_first = exchange(*forwarded[-1], *gate)
            gate = (far_first, far_second)
            expert_pieces.append([(expert_block, m), (near_x, m), (near_y, m), (far_first, 0), (far_second, 0)])
        expert_places = five_places(span)
    else:
        gathered = gather_whole(expert_block, 1)
        expert_pieces = [[(gathered, m)] for m in range(3)]
        expert_places = [(0, width, 0)]
    down_pieces, gate_pieces, up_pieces = expert_pieces

    seg = segment[0].reshape(2, 2, rows)
    seg_rel = flip(flip(seg, 0, x), 1, core).reshape(4 * rows)
    position = jnp.arange(4 * rows, dtype=jnp.int32).reshape(2, 2, rows)
    key_pos = flip(flip(position, 0, x), 1, core).reshape(4 * rows)
    first_up = lookup_parent(seg_rel[:rows], parent[0])
    second_up = lookup_parent(first_up, parent[0])
    key_side = jnp.stack([seg_rel, key_pos], 1)
    query_side = jnp.stack([seg_rel[:rows], first_up, second_up, key_pos[:rows]])

    mixed_low, inverse = attend_call(rot, kv_all, key_side, query_side, heads)
    attn_part = project_call(scal, mixed_low, out_pieces, out_places, shard, width)
    attn_add = lax.psum(attn_part, "tensor")

    cot = permute_width(cotangent[0], scal, chips)
    cot_other = to_core(cot)
    grad_act, pair_dy = products_call(cot, cot_other, down_pieces, hidden_rows)
    if paired:
        attn_add = after(attn_add, down_pieces[3][0], down_pieces[4][0])
    resid, moe_low, gates = route_call(tokens_low, attn_add, gain_two, router_t, routes[0])
    moe_other = to_core(moe_low)
    gate_pre, pair_x = products_call(moe_low, moe_other, gate_pieces, hidden_rows)
    gates_t = gates.T
    gates_own = lax.dynamic_slice_in_dim(gates_t, core * half, half, 0)
    gates_sent = lax.dynamic_slice_in_dim(gates_t, (1 - core) * half, half, 0)
    gate_pair = jnp.concatenate([gates_own, to_core(gates_sent)], 1)[:, None, :]

    acts, acts_t, gate_part = experts_call(pair_x, gate_pre, grad_act, gate_pair, up_pieces, hid)
    weights = [gate_pieces, up_pieces]
    part_other = to_core(spread_call(acts_t, (1, 2), 1, weights, expert_places))
    moe_sum = spread_call(acts_t, (1, 2), 0, weights, expert_places, part_other)
    grad_moe_in = lax.psum(moe_sum, "tensor")
    acts, acts_t, gate_part = lax.optimization_barrier((acts, acts_t, gate_part, moe_sum))[:3]
    gate_grads = gate_join_call(scal, *gate_sum_call(gate_part))

    lengths = [span] + [shard] * 6 if paired else [span] * chips
    grad_blocks = weight_grad_call(acts, pair_dy, pair_x, lengths)
    acts_t = after(acts_t, grad_blocks[0])
    grad_moe_in = after(grad_moe_in, grad_blocks[0])
    if paired:
        own_grads, x_first, x_second, y_first, y_second, far_first, far_second = grad_blocks
        far_x, far_y = exchange(far_first, far_second)
        x_first, y_second = exchange(x_first, y_second)
        grad_moe_in = after(grad_moe_in, far_x, far_y)
    out_other = to_core(spread_call(acts_t, (0,), 1, [down_pieces], expert_places))
    out_sum = spread_call(acts_t, (0,), 0, [down_pieces], expert_places, out_other)
    grad_moe_in = after(grad_moe_in, out_sum)
    out_sum = after(out_sum, grad_moe_in, gate_grads)
    moe_add = lax.psum_scatter(out_sum, "tensor", scatter_dimension=0, tiled=True)
    output_rows = add_call(scal, resid, moe_add, chips)
    output = lax.all_gather(output_rows, "tensor", axis=0, tiled=True)[None]

    grad_resid, resid_low, grad_logits, grad_gain_two = route_back_call(
        grad_moe_in, gate_grads, gates, resid, cot, router_t, gain_two
    )

    grad_mixed = project_back_call(scal, after(resid_low, out_sum), out_pieces, out_places, shard, inner)
    query_back, kv_own, kv_sent, kv_mid, grad_gain_q = attend_back_call(
        rot, kv_all, key_side, query_side, grad_mixed, mixed_low, inverse, raw, cosine, sine, gain_q, heads
    )
    if paired:
        kv_mid = after(kv_mid, x_first, y_second)
    kv_part, kv_on = kv_pass_call(kv_own, after(kv_mid, output_rows), to_core(kv_sent))
    kv_far = to_x(kv_on)
    if paired:
        x_second, y_first = met_call(after(x_second, kv_far), far_y, y_first, far_x)
        x_second, y_first = exchange(x_second, y_first)
        near_grads = (x_first, y_first, x_second, y_second)
    back_part, grad_gain_one, kv_back, grad_gain_k = qkv_back_call(
        scal, query_back, kv_part, kv_far, raw, cosine, sine, gain_k, tokens_low, qkv_pieces, qkv_places, shard
    )
    grad_normed = lax.psum_scatter(back_part, "tensor", scatter_dimension=0, tiled=True)
    hidden_rows_out = last_call(scal, tokens_low, grad_resid, grad_normed, gain_one, chips)
    grad_hidden = lax.all_gather(hidden_rows_out, "tensor", axis=0, tiled=True)[None]

    late_resid, late_mixed, late_normed, late_moe = lax.optimization_barrier(
        (resid_low, mixed_low, normed, moe_low, back_part)
    )[:4]
    grad_router_t = dot(grad_logits, late_moe, (0, 0))
    if paired:
        qkv_mine, qkv_sent = rows_grad_call(scal, late_normed, query_back, kv_back, shard)
        out_mine, out_sent = columns_grad_call(scal, late_mixed, late_resid, shard)
        qkv_blocks = cut_call(qkv_mine, to_core(qkv_sent), 0)
        out_blocks = cut_call(out_mine, to_core(out_sent), 1)

        def plane_sum(blocks, axis, lengths):
            own, x_first, x_second, y_first, y_second, far_first, far_second = blocks
            far_x, far_y = exchange(far_first, far_second)
            x_first, y_second = exchange(x_first, y_second)
            x_second, y_first = exchange(*met_call(x_second, far_y, y_first, far_x))
            near = (x_first, y_first, x_second, y_second)
            return end_call(own, near, axis, lengths)

        grad_query, grad_key, grad_value = plane_sum(qkv_blocks, 0, [inner, HEAD, HEAD])
        (grad_out_weight,) = plane_sum(out_blocks, 1, [shard])
        own_grads = after(own_grads, qkv_blocks[0], out_blocks[0])
        mine, sent = total_call(scal, own_grads, near_grads)
    else:
        qkv_back = jnp.concatenate([query_back, kv_back], 1)
        sides = [
            (pick_columns(late_normed, scal, shard, o), pick_columns(late_resid, scal, shard, o))
            for o in (False, True)
        ]
        qkv_mine, qkv_sent = (dot(n, qkv_back, (0, 0)) for n, _ in sides)
        out_mine, out_sent = (dot(late_mixed, r, (0, 0)) for _, r in sides)
        qkv_sum = rounded(qkv_mine + to_core(rounded(qkv_sent)).astype(F32))
        out_sum = rounded(out_mine + to_core(rounded(out_sent)).astype(F32))
        grad_qkv = scatter_whole([qkv_sum[r * shard : (r + 1) * shard] for r in range(chips)])
        grad_query, grad_key, grad_value = jnp.split(grad_qkv, [inner, inner + HEAD], 1)
        grad_out_weight = scatter_whole([out_sum[:, r * shard : (r + 1) * shard] for r in range(chips)])
        total = scatter_whole(grad_blocks)
        mine = lax.dynamic_slice_in_dim(total, core * shard, shard, 1)
        sent = rounded(lax.dynamic_slice_in_dim(total, (1 - core) * shard, shard, 1))
    grad_down, grad_gate, grad_up = (
        v.reshape(EXPERTS, hid, shard) for v in lay_call(scal, mine, to_core(sent))
    )
    grad_gate, grad_up = grad_gate.transpose(0, 2, 1), grad_up.transpose(0, 2, 1)

    share = 1.0 / tensor
    head_rows = jnp.concatenate(
        [grad_gain_q.reshape(2 * chips, per), grad_gain_k.reshape(2 * chips, per)], 1
    )
    head_rows = relative(jnp.pad(head_rows, ((0, 0), (0, shard - 2 * per))).reshape(width))
    table = jnp.concatenate(
        [
            grad_gain_one,
            grad_gain_two * share,
            grad_router_t * share,
            head_rows[None],
            jnp.zeros((5, width), F32),
        ]
    ).reshape(24, chips, 2, shard)
    table_own = lax.dynamic_index_in_dim(table, core, 2, keepdims=False)
    table_sent = lax.dynamic_index_in_dim(table, 1 - core, 2, keepdims=False)
    table = table_own + to_core(table_sent)
    table = table.reshape(24, count, 2, shard)
    table = table[:, :, 0] + to_x(table[:, :, 1])
    if paired:
        table = table[:, 0] + to_dp(table[:, 1])
    else:
        table = lax.psum_scatter(table, "dp", scatter_dimension=1, tiled=False)
    mine = sum_z(table)
    gains = mine[2 + EXPERTS, : 2 * per]

    return (
        output,
        grad_hidden,
        mine[0],
        grad_query,
        grad_key,
        grad_value,
        gains[:per],
        gains[per:],
        grad_out_weight,
        mine[1],
        mine[2 : 2 + EXPERTS].T,
        grad_gate,
        grad_up,
        grad_down,
    )


def solution(mesh):
    plane = ("dp", "ctx")
    in_specs = (
        P("dp", "ctx", None),
        P("dp", "ctx", None),
        P(plane),
        P(plane, "tensor"),
        P(plane, "tensor"),
        P(plane, "tensor"),
        P(plane),
        P(plane),
        P("tensor", plane),
        P(plane),
        P(plane, None),
        P(None, plane, "tensor"),
        P(None, plane, "tensor"),
        P(None, "tensor", plane),
        P("dp", None),
        P("dp", None),
        P("dp", "ctx"),
        P("dp", "ctx", None),
    )
    out_specs = (
        P("dp", "ctx", None),
        P("dp", "ctx", None),
        P(plane),
        P(plane, "tensor"),
        P(plane, "tensor"),
        P(plane, "tensor"),
        P(plane),
        P(plane),
        P("tensor", plane),
        P(plane),
        P(plane, None),
        P(None, plane, "tensor"),
        P(None, plane, "tensor"),
        P(None, "tensor", plane),
    )
    return jax.shard_map(shards, mesh=mesh, in_specs=in_specs, out_specs=out_specs, check_vma=False)
```

```python
import functools
import math

import jax
import jax.numpy as jnp
from jax import lax
from jax.experimental import pallas as pl
from jax.experimental.pallas import tpu as pltpu
from jax.sharding import PartitionSpec as P

HEADS_Q = 32
HEADS_KV = 4
HEAD = 128
TOP = 8
EXPERTS = 16

EPS = 1e-06
THETA = 1000000.0
LOG2E = 1.4426950408889634
HIDE = -1e30

F32 = jnp.float32
BF16 = jnp.bfloat16
VMEM_BYTES = 58 * 1024 * 1024


def rounded(v):
    return v.astype(BF16)


def dot(a, b, contract):
    return lax.dot_general(a, b, ((contract[:1], contract[1:]), ((), ())), preferred_element_type=F32)


def after(value, *others):
    return lax.optimization_barrier((value,) + others)[0]


def to_core(v):
    return lax.ppermute(v, "ctx", [(i, i ^ 1) for i in range(4)])


def to_x(v):
    return lax.ppermute(v, "ctx", [(i, i ^ 2) for i in range(4)])


def to_dp(v):
    return lax.ppermute(v, "dp", [(0, 1), (1, 0)])


def exchange(x_value, y_value, *gate):
    x_value, y_value = after((x_value, y_value), *gate) if gate else lax.optimization_barrier((x_value, y_value))
    return lax.optimization_barrier((to_x(x_value), to_dp(y_value)))


def sum_z(v):
    size = lax.axis_size("tensor")
    one, two, three = (lax.ppermute(v, "tensor", [(i, i ^ k) for i in range(size)]) for k in (1, 2, 3))
    return (v + one) + (two + three)


def place():
    ctx = lax.axis_index("ctx")
    return lax.axis_index("dp"), ctx // 2, ctx % 2


def flips():
    dp, x, _ = place()
    return x + 2 * dp if lax.axis_size("dp") == 2 else x


def flip(v, axis, bit):
    return jnp.where(bit == 0, v, jnp.flip(v, axis))


def relative(v):
    dp, x, _ = place()
    count = lax.axis_size("dp")
    cut = v.reshape(v.shape[:-1] + (count, 2, v.shape[-1] // (2 * count)))
    cut = flip(cut, cut.ndim - 2, x)
    if count == 2:
        cut = flip(cut, cut.ndim - 3, dp)
    return cut.reshape(v.shape)


def halves(v, axis):
    return jnp.split(v, 2, axis)


def gather_whole(block, axis):
    pair = jnp.concatenate([block, to_x(block)], axis)
    return lax.all_gather(pair, "dp", axis=axis, tiled=True)


def scatter_whole(blocks):
    kept = jnp.stack(blocks[0::2]).astype(F32) + to_x(jnp.stack(blocks[1::2])).astype(F32)
    return lax.psum_scatter(rounded(kept), "dp", scatter_dimension=0, tiled=False).astype(F32)


def whole(array):
    dims = len(array.shape)
    return pl.BlockSpec(array.shape, lambda *_: (0,) * dims)


SCALARS = pl.BlockSpec(memory_space=pltpu.SMEM)


TIMES = {
    "permute_kernel": 4.6, "half_kernel": 4, "block_kernel": 6, "qkv_kernel": 11.7,
    "attend_kernel": 16.3, "attend_back_kernel": 30, "project_kernel": 6.6, "project_back_kernel": 6.5,
    "kv_pass_kernel": 2, "qkv_back_kernel": 9.8, "products_kernel": 11.8, "experts_kernel": 20,
    "spread_kernel": 10, "join_kernel": 1, "weight_grad_kernel": 50, "met_kernel": 0.5, "total_kernel": 0.5,
    "lay_kernel": 0.5, "pair_grad_kernel": 0.5, "columns_grad_kernel": 0.5, "cut_kernel": 0.3, "end_kernel": 0.3,
    "route_kernel": 6.3, "route_back_kernel": 8.6, "add_kernel": 2.2, "last_kernel": 6.2,
}


def cost(body):
    name = getattr(body, "func", body).__name__
    return pl.CostEstimate(flops=int(TIMES.get(name, 0.3) * 1e9), bytes_accessed=0, transcendentals=0)


def kernel_call(body, grid, in_specs, out_specs, out_shape, flops, moved, scratch=()):
    return pl.pallas_call(
        body,
        grid=grid,
        in_specs=in_specs,
        out_specs=out_specs,
        out_shape=out_shape,
        scratch_shapes=list(scratch),
        compiler_params=pltpu.CompilerParams(vmem_limit_bytes=VMEM_BYTES),
        cost_estimate=cost(body),
    )


def sds(shape, dtype):
    return jax.ShapeDtypeStruct(shape, dtype)


def piece_starts(scal, places, shard):
    core = scal[1]
    shift = {0: 0, 1: core * shard, 2: (1 - core) * shard}
    return [
        (start if kind == 0 else pl.multiple_of(start + shift[kind], length), length)
        for start, length, kind in places
    ]


def kernel_inverse_rms(v):
    return lax.rsqrt(jnp.mean(v * v, axis=-1, keepdims=True) + EPS)


def permute_kernel(scal, in_ref, out_ref):
    out_ref[...] = in_ref[...]


def permute_width(v, scal, blocks):
    rows, width = v.shape
    span = width // blocks
    return pl.pallas_call(
        permute_kernel,
        grid_spec=pltpu.PrefetchScalarGridSpec(
            num_scalar_prefetch=1,
            grid=(blocks,),
            in_specs=[pl.BlockSpec((rows, span), lambda j, s: (0, j ^ s[0]))],
            out_specs=pl.BlockSpec((rows, span), lambda j, s: (0, j)),
        ),
        out_shape=sds(v.shape, v.dtype),
        cost_estimate=cost(permute_kernel),
    )(scal, v)


def pick_columns(v, scal, shard, other):
    rows, width = v.shape
    count = width // (2 * shard)
    which = 1 - scal[1] if other else scal[1]
    cut = v.reshape(rows, count, 2, shard)
    return lax.dynamic_index_in_dim(cut, which, 2, keepdims=False).reshape(rows, count * shard)


def prefetch_call(body, scal, grid, in_specs, out_specs, out_shape, arrays, scratch=()):
    return pl.pallas_call(
        body,
        grid_spec=pltpu.PrefetchScalarGridSpec(
            num_scalar_prefetch=1,
            grid=grid,
            in_specs=in_specs,
            out_specs=out_specs,
            scratch_shapes=list(scratch),
        ),
        out_shape=out_shape,
        compiler_params=pltpu.CompilerParams(vmem_limit_bytes=VMEM_BYTES),
        cost_estimate=cost(body),
    )(scal, *arrays)


def half_kernel(scal, *refs):
    ins, out = refs[:3], refs[3]
    for m in range(3):

        @pl.when(pl.program_id(0) == m)
        def _():
            out[0] = ins[m][...]


def other_half_call(scal, weights):
    experts, hid, shard = weights[0].shape
    half = experts // 2
    return prefetch_call(
        half_kernel,
        scal,
        (3,),
        [pl.BlockSpec((half, hid, shard), lambda m, s: (1 - s[1], 0, 0))] * 3,
        pl.BlockSpec((1, half, hid, shard), lambda m, s: (m, 0, 0, 0)),
        sds((3, half, hid, shard), BF16),
        weights,
    )


def block_kernel(scal, *refs):
    ins, got, out = refs[:3], refs[3], refs[4]
    shard = got.shape[3]
    rows = out.shape[0]
    other = pl.ds(pl.multiple_of((1 - scal[1]) * shard, shard), shard)
    out[:, other] = got[0].reshape(rows, shard)
    for m in range(3):

        @pl.when(pl.program_id(0) == m)
        def _():
            out[:, pl.ds(pl.multiple_of(scal[1] * shard, shard), shard)] = ins[m][...].reshape(rows, shard)


def block_call(scal, weights, got):
    experts, hid, shard = weights[0].shape
    half = experts // 2
    return prefetch_call(
        block_kernel,
        scal,
        (3,),
        [pl.BlockSpec((half, hid, shard), lambda m, s: (s[1], 0, 0))] * 3
        + [pl.BlockSpec((1, half, hid, shard), lambda m, s: (m, 0, 0, 0))],
        pl.BlockSpec((half * hid, 2 * shard), lambda m, s: (m, 0)),
        sds((3 * half * hid, 2 * shard), BF16),
        [*weights, got],
    )


def read_small(places, shard, per, scal, pieces, gain_one, gain_two, router_t, gain_q, gain_k):
    gain_q[...] = jnp.zeros(gain_q.shape, F32)
    gain_k[...] = jnp.zeros(gain_k.shape, F32)
    lane = lax.broadcasted_iota(jnp.int32, (shard // 2, HEAD), 0)
    target = lax.broadcasted_iota(jnp.int32, (shard // 2, HEAD), 1)
    for (start, length), (fixed, _, kind), ref in zip(piece_starts(scal, places, shard), places, pieces):
        value = ref[...].astype(F32).T
        lanes = pl.ds(start, length)
        router_t[:, lanes] = rounded(value[:EXPERTS])
        gain_one[:, lanes] = value[EXPERTS : EXPERTS + 1]
        gain_two[:, lanes] = value[EXPERTS + 1 : EXPERTS + 2]
        if fixed % shard:
            continue
        half = scal[1] if kind == 1 else 1 - scal[1]
        heads = rounded(value[EXPERTS + 2 : EXPERTS + 3, : shard // 2])
        first = (2 * ((fixed // (2 * shard)) ^ scal[0]) + half) * per
        in_q = (target == first + lane) & (lane < per)
        in_k = (target == first + lane - per) & (lane >= per) & (lane < 2 * per)
        gain_q[...] += dot(heads, jnp.where(in_q, 1.0, 0.0).astype(BF16), (1, 0))
        gain_k[...] += dot(heads, jnp.where(in_k, 1.0, 0.0).astype(BF16), (1, 0))


def qkv_kernel(places, shard, per, blocks, given, scal, hid, cos, sin, *refs):
    n = len(places)
    weights, refs = refs[:n], refs[n:]
    if given:
        gain, gain_q, gain_k, normed, hid_rel, raw, rot = refs
    else:
        smalls, (gain, gain_two, router_t, gain_q, gain_k, normed, hid_rel, raw, rot) = refs[:n], refs[n:]
    step, last = pl.program_id(0), pl.num_programs(0) - 1
    width = hid.shape[1]
    span = width // blocks

    @pl.when(step == 0)
    def _():
        if not given:
            read_small(places, shard, per, scal, smalls, gain, gain_two, router_t, gain_q, gain_k)
        for j in range(blocks):
            source = pl.multiple_of((scal[0] ^ j) * span, span)
            hid_rel[:, j * span : (j + 1) * span] = hid[:, pl.ds(source, span)]
        tokens = hid_rel[...].astype(F32)
        normed[...] = rounded(tokens * kernel_inverse_rms(tokens) * gain[...])

    total = jnp.zeros(raw.shape, F32)
    for (start, length), weight in zip(piece_starts(scal, places, shard), weights):
        total += dot(normed[:, pl.ds(start, length)], weight[...], (1, 0))
    raw[...] = total
    vector = jnp.where(step == last, gain_k[...], gain_q[...])
    for head in range(2):
        cut = total[:, head * HEAD : (head + 1) * HEAD]
        scaled = cut * kernel_inverse_rms(cut) * vector
        turned = scaled * cos[...] + pltpu.roll(scaled, HEAD // 2, 1) * sin[...]
        if head == 1:
            turned = jnp.where(step == last, cut, turned)
        rot[:, head * HEAD : (head + 1) * HEAD] = rounded(turned)


def qkv_call(scal, hid, gains, cos, sin, pieces, places, shard, per, blocks, columns):
    rows, width = hid.shape
    pair = 2 * HEAD
    block = pl.BlockSpec((rows, pair), lambda i: (0, i))
    weights = [pl.BlockSpec((p.shape[0], pair), lambda i: (0, i)) for p in pieces]
    outs = [sds(hid.shape, BF16), sds(hid.shape, BF16), sds((rows, columns), F32), sds((rows, columns), BF16)]
    specs = [whole(hid), whole(hid), block, block]
    if gains:
        more, more_specs = list(gains), [whole(g) for g in gains]
    else:
        more = pieces
        more_specs = [pl.BlockSpec((p.shape[0], HEAD), lambda i: (0, columns // HEAD)) for p in pieces]
        found = [
            sds((1, width), F32),
            sds((1, width), F32),
            sds((EXPERTS, width), BF16),
            sds((1, HEAD), F32),
            sds((1, HEAD), F32),
        ]
        outs, specs = found + outs, [whole(v) for v in found] + specs
    return kernel_call(
        functools.partial(qkv_kernel, places, shard, per, blocks, bool(gains)),
        (columns // pair,),
        [SCALARS, whole(hid), whole(cos), whole(sin)] + weights + more_specs,
        specs,
        outs,
        0,
        0,
    )(scal, hid, cos, sin, *pieces, *more)


def write_bias(bias, key_side, query_side):
    seg = key_side[:, 0:1]
    seen = (seg == query_side[0:1]) | (seg == query_side[1:2]) | (seg == query_side[2:3])
    seen = seen & (key_side[:, 1:2] <= query_side[3:4])
    bias[...] = jnp.where(seen, 0.0, HIDE)


def key_tiles(count):
    tile = next(t for t in (384, 320, 256, 128) if count % t == 0)
    return [(s, tile) for s in range(0, count, tile)]


def attend_kernel(query, keys, values, key_side, query_side, mixed, inverse, bias, values_t):
    @pl.when(pl.program_id(0) == 0)
    def _():
        write_bias(bias, key_side[...], query_side[...])
        values_t[...] = values[...].T

    rows = query.shape[0]
    total = jnp.zeros((HEAD, rows), F32)
    row_sum = jnp.zeros((1, rows), F32)
    factor = LOG2E * HEAD**-0.5
    for start, tile in key_tiles(keys.shape[0]):
        raw = dot(keys[start : start + tile], query[...], (1, 1))
        weight = jnp.exp2(raw * factor + bias[start : start + tile])
        row_sum += jnp.sum(weight, 0, keepdims=True)
        total += dot(values_t[:, start : start + tile], rounded(weight), (1, 0))
    scale = 1.0 / row_sum
    mixed[...] = rounded((total * scale).T)
    inverse[0] = scale


def attend_call(rot, kv_all, key_side, query_side, heads):
    rows, count = rot.shape[0], kv_all.shape[0]
    column = pl.BlockSpec((rows, HEAD), lambda h: (0, h))
    return kernel_call(
        attend_kernel,
        (heads,),
        [
            column,
            pl.BlockSpec((count, HEAD), lambda h: (0, 0)),
            pl.BlockSpec((count, HEAD), lambda h: (0, 1)),
            whole(key_side),
            whole(query_side),
        ],
        [column, pl.BlockSpec((1, 1, rows), lambda h: (h, 0, 0))],
        [sds((rows, heads * HEAD), BF16), sds((heads, 1, rows), F32)],
        4 * heads * rows * count * HEAD,
        4 * rows * heads * HEAD + 4 * count * HEAD,
        [pltpu.VMEM((count, rows), F32), pltpu.VMEM((HEAD, count), BF16)],
    )(rot, kv_all, kv_all, key_side, query_side)


def attend_back_kernel(
    query, keys, values, key_side, query_side, grad, mixed, inverse, raw_query, cos, sin, gain,
    query_back, kv_own, kv_sent, kv_mid, grad_gain, bias, keys_t, grad_kv,
):
    @pl.when(pl.program_id(0) == 0)
    def _():
        write_bias(bias, key_side[...], query_side[...])
        keys_t[...] = keys[...].T
        grad_kv[...] = jnp.zeros(grad_kv.shape, F32)
        grad_gain[...] = jnp.zeros(grad_gain.shape, F32)

    rows = query.shape[0]
    scale = HEAD**-0.5
    factor = LOG2E * scale
    both = grad[...].astype(F32) * mixed[...].astype(F32)
    mean = jnp.sum(both.T, 0, keepdims=True)
    norm = inverse[0]
    total = jnp.zeros((HEAD, rows), F32)
    for start, tile in key_tiles(keys.shape[0]):
        span = slice(start, start + tile)
        raw = dot(keys[span], query[...], (1, 1))
        prob = jnp.exp2(raw * factor + bias[span]) * norm
        grad_prob = dot(values[span], grad[...], (1, 1))
        grad_raw = rounded(prob * (grad_prob - mean) * scale)
        total += dot(keys_t[:, span], grad_raw, (1, 0))
        grad_kv[span, :HEAD] += dot(grad_raw, query[...], (1, 0))
        grad_kv[span, HEAD:] += dot(rounded(prob), grad[...], (1, 0))
    turned = total.T
    turned = turned * cos[...] - pltpu.roll(turned, HEAD // 2, 1) * sin[...]
    value = raw_query[...]
    shrink = kernel_inverse_rms(value)
    normal = value * shrink
    grad_gain[...] += jnp.sum(turned * normal, 0, keepdims=True)
    scaled = turned * gain[...]
    middle = jnp.mean(scaled * normal, axis=-1, keepdims=True)
    query_back[...] = rounded(shrink * (scaled - normal * middle))

    @pl.when(pl.program_id(0) == pl.num_programs(0) - 1)
    def _():
        kv_own[...] = grad_kv[:rows]
        kv_sent[:rows] = rounded(grad_kv[rows : 2 * rows])
        kv_mid[...] = grad_kv[2 * rows : 3 * rows]
        kv_sent[rows:] = rounded(grad_kv[3 * rows :])


def attend_back_call(rot, kv_all, key_side, query_side, grad, mixed, inverse, raw, cos, sin, gain, heads):
    rows, count = rot.shape[0], kv_all.shape[0]
    column = pl.BlockSpec((rows, HEAD), lambda h: (0, h))
    return kernel_call(
        attend_back_kernel,
        (heads,),
        [
            column,
            pl.BlockSpec((count, HEAD), lambda h: (0, 0)),
            pl.BlockSpec((count, HEAD), lambda h: (0, 1)),
            whole(key_side),
            whole(query_side),
            column,
            column,
            pl.BlockSpec((1, 1, rows), lambda h: (h, 0, 0)),
            column,
            whole(cos),
            whole(sin),
            whole(gain),
        ],
        [
            column,
            pl.BlockSpec((rows, 2 * HEAD), lambda h: (0, 0)),
            pl.BlockSpec((2 * rows, 2 * HEAD), lambda h: (0, 0)),
            pl.BlockSpec((rows, 2 * HEAD), lambda h: (0, 0)),
            pl.BlockSpec((1, HEAD), lambda h: (0, 0)),
        ],
        [
            sds((rows, heads * HEAD), BF16),
            sds((rows, 2 * HEAD), F32),
            sds((2 * rows, 2 * HEAD), BF16),
            sds((rows, 2 * HEAD), F32),
            sds((1, HEAD), F32),
        ],
        10 * heads * rows * count * HEAD,
        12 * rows * heads * HEAD + 12 * count * HEAD,
        [
            pltpu.VMEM((count, rows), F32),
            pltpu.VMEM((HEAD, count), BF16),
            pltpu.VMEM((count, 2 * HEAD), F32),
        ],
    )(rot, kv_all, kv_all, key_side, query_side, grad, mixed, inverse, raw, cos, sin, gain)


def project_kernel(places, shard, scal, mixed, *refs):
    out = refs[-1]
    for (start, length), weight in zip(piece_starts(scal, places, shard), refs[:-1]):
        out[:, pl.ds(start, length)] = rounded(dot(mixed[...], weight[...], (1, 0)))


def project_call(scal, mixed, pieces, places, shard, width):
    rows, inner = mixed.shape
    return kernel_call(
        functools.partial(project_kernel, places, shard),
        (1,),
        [SCALARS, whole(mixed)] + [whole(p) for p in pieces],
        pl.BlockSpec((rows, width), lambda i: (0, 0)),
        sds((rows, width), BF16),
        2 * rows * inner * width,
        2 * inner * width + 2 * rows * (inner + width),
    )(scal, mixed, *pieces)


def project_back_kernel(places, shard, scal, grad, *refs):
    out = refs[-1]
    total = jnp.zeros(out.shape, F32)
    for (start, length), weight in zip(piece_starts(scal, places, shard), refs[:-1]):
        total += dot(grad[:, pl.ds(start, length)], weight[...], (1, 1))
    out[...] = rounded(total)


def project_back_call(scal, grad, pieces, places, shard, inner):
    rows, width = grad.shape
    tile = inner // 2
    return kernel_call(
        functools.partial(project_back_kernel, places, shard),
        (2,),
        [SCALARS, whole(grad)] + [pl.BlockSpec((tile, p.shape[1]), lambda i: (i, 0)) for p in pieces],
        pl.BlockSpec((rows, tile), lambda i: (0, i)),
        sds((rows, inner), BF16),
        2 * rows * inner * width,
        2 * inner * width + 2 * rows * (inner + width),
    )(scal, grad, *pieces)


def kv_pass_kernel(own, mid, got, part, sent):
    rows = own.shape[0]
    part[...] = own[...] + got[:rows].astype(F32)
    sent[...] = rounded(mid[...] + got[rows:].astype(F32))


def kv_pass_call(own, mid, got):
    return kernel_call(
        kv_pass_kernel,
        (1,),
        [whole(own), whole(mid), whole(got)],
        [whole(own), whole(own)],
        [sds(own.shape, F32), sds(own.shape, BF16)],
        0,
        0,
    )(own, mid, got)


def qkv_back_kernel(
    places, shard, scal, query_back, kv_part, kv_far, raw_key, cos, sin, gain_k, hid, *refs
):
    weights, (part, grad_gain, kv_back, grad_gain_k) = refs[: len(places)], refs[len(places) :]
    inner = query_back.shape[1]
    total = kv_part[...] + kv_far[...].astype(F32)
    turned = total[:, :HEAD]
    turned = turned * cos[...] - pltpu.roll(turned, HEAD // 2, 1) * sin[...]
    value = raw_key[...]
    shrink = kernel_inverse_rms(value)
    normal = value * shrink
    grad_gain_k[...] = jnp.sum(turned * normal, 0, keepdims=True)
    scaled = turned * gain_k[...]
    middle = jnp.mean(scaled * normal, axis=-1, keepdims=True)
    kv_back[:, :HEAD] = rounded(shrink * (scaled - normal * middle))
    kv_back[:, HEAD:] = rounded(total[:, HEAD:])

    tokens = hid[...].astype(F32)
    shrink = kernel_inverse_rms(tokens)
    for (start, length), weight in zip(piece_starts(scal, places, shard), weights):
        lanes = pl.ds(start, length)
        value = dot(query_back[...], weight[:, :inner], (1, 1))
        value += dot(kv_back[...], weight[:, inner : inner + 2 * HEAD], (1, 1))
        part[:, lanes] = rounded(value)
        normal = hid[:, lanes].astype(F32) * shrink
        grad_gain[:, lanes] = jnp.sum(value * normal, 0, keepdims=True)


def qkv_back_call(scal, query_back, kv_part, kv_far, raw, cos, sin, gain_k, hid, pieces, places, shard):
    rows, width = hid.shape
    inner = query_back.shape[1]
    arrays = (cos, sin, gain_k, hid)
    outs = [sds((rows, width), BF16), sds((1, width), F32), sds((rows, 2 * HEAD), BF16), sds((1, HEAD), F32)]
    return kernel_call(
        functools.partial(qkv_back_kernel, places, shard),
        (1,),
        [SCALARS, whole(query_back), whole(kv_part), whole(kv_far)]
        + [pl.BlockSpec((rows, HEAD), lambda i: (0, inner // HEAD))]
        + [whole(a) for a in arrays]
        + [whole(p) for p in pieces],
        [whole(o) for o in outs],
        outs,
        0,
        0,
    )(scal, query_back, kv_part, kv_far, raw, *arrays, *pieces)


def join_rows(own, other, scratch):
    rows = own.shape[0]

    @pl.when(pl.program_id(0) == 0)
    def _():
        scratch[:rows] = own[...]
        scratch[rows:] = other[...]


def product(weights, rows_ref):
    return dot(jnp.concatenate([w[...] for w in weights], 1), rows_ref[...], (1, 1))


def single(shape):
    dims = len(shape)
    return pl.BlockSpec(shape, lambda *_: (0,) * dims, pipeline_mode=pl.Buffered(1))


def products_kernel(own, other, *refs):
    weights, (out, both, pair) = refs[:-3], refs[-3:]
    join_rows(own, other, both)
    out[...] = product(weights, both)

    @pl.when(pl.program_id(0) == 0)
    def _():
        pair[...] = both[...]


def row_pieces(pieces, tile, hidden):
    step = hidden // tile
    return [pl.BlockSpec((tile, a.shape[1]), lambda i, m=m: (i + m * step, 0)) for a, m in pieces]


def products_call(own, other, pieces, hidden):
    rows, width = own.shape
    tile = hidden // 4
    return kernel_call(
        products_kernel,
        (4,),
        [single(own.shape), single(own.shape)] + row_pieces(pieces, tile, hidden),
        [pl.BlockSpec((tile, 2 * rows), lambda i: (i, 0)), single((2 * rows, width))],
        [sds((hidden, 2 * rows), F32), sds((2 * rows, width), BF16)],
        0,
        0,
        [pltpu.VMEM((2 * rows, width), BF16)],
    )(own, other, *[a for a, _ in pieces])


def experts_kernel(hid, both, gate_ref, grad_act, gates, *refs):
    weights, (acts, acts_t, gate_part) = refs[:-3], refs[-3:]
    gate_pre, up_pre = gate_ref[...], product(weights, both)
    sig = 1.0 / (1.0 + jnp.exp(-gate_pre))
    silu = gate_pre * sig
    act = silu * up_pre
    slope = sig * (1.0 + gate_pre * (1.0 - sig))
    count = gates.shape[0]
    for e in range(count):
        rows = slice(e * hid, (e + 1) * hid)
        gate = gates[e]
        raw = grad_act[rows, :]
        back = gate * raw
        acts[0, rows, :] = rounded(gate * act[rows])
        acts[1, rows, :] = rounded(back * up_pre[rows] * slope[rows])
        acts[2, rows, :] = rounded(back * silu[rows])
        gate_part[e] = jnp.sum(act[rows] * raw, 0, keepdims=True)
    for k in range(3):
        acts_t[k] = acts[k].T


def experts_call(pair, gate_pre, grad_act, gates, pieces, hid):
    both, width = pair.shape
    experts = gates.shape[0]
    per = 2
    tile = per * hid
    hidden = experts * hid
    act = pl.BlockSpec((tile, both), lambda i: (i, 0))
    gate = pl.BlockSpec((per, 1, both), lambda i: (i, 0, 0))
    return kernel_call(
        functools.partial(experts_kernel, hid),
        (experts // per,),
        [single(pair.shape), act, act, gate] + row_pieces(pieces, tile, hidden),
        [
            pl.BlockSpec((3, tile, both), lambda i: (0, i, 0)),
            pl.BlockSpec((3, both, tile), lambda i: (0, 0, i)),
            gate,
        ],
        [sds((3, hidden, both), BF16), sds((3, both, hidden), BF16), sds((experts, 1, both), F32)],
        0,
        0,
    )(pair, gate_pre, grad_act, gates, *[a for a, _ in pieces])


def gate_sum_kernel(first, second, third, fourth, own, sent):
    rows = own.shape[1]
    for e in range(own.shape[0]):
        total = (first[e] + second[e]) + (third[e] + fourth[e])
        own[e : e + 1] = total[:, :rows]
        sent[e : e + 1] = total[:, rows:]


def gate_sum_call(part):
    size = lax.axis_size("tensor")
    there = [lax.ppermute(part, "tensor", [(i, i ^ k) for i in range(size)]) for k in (1, 2, 3)]
    out = sds((part.shape[0], part.shape[2] // 2), F32)
    own, sent = kernel_call(
        gate_sum_kernel, (1,), [whole(part)] * 4, [whole(out)] * 2, [out, out], 0, 0
    )(part, *there)
    return own, to_core(sent)


def gate_join_kernel(scal, own, got, out):
    first = jnp.where(scal[1] == 0, own[...], got[...])
    second = jnp.where(scal[1] == 0, got[...], own[...])
    out[...] = jnp.concatenate([first, second]).T


def gate_join_call(scal, own, got):
    out = sds((own.shape[1], 2 * own.shape[0]), F32)
    return kernel_call(gate_join_kernel, (1,), [SCALARS, whole(own), whole(got)], whole(out), out, 0, 0)(
        scal, own, got
    )


def backward_tiles(places, tile):
    return [(p, k) for p, (_, length, _) in enumerate(places) for k in range(length // tile)]


def spread_kernel(tiles, terms, joined, *refs):
    acts, out = refs[:terms], refs[-1]
    weights = refs[terms + joined : -1]
    n = len(weights) // terms
    step = pl.program_id(0)
    for p in range(n):
        steps = [t for t, (q, _) in enumerate(tiles) if q == p]

        @pl.when((step >= steps[0]) & (step <= steps[-1]))
        def _():
            value = sum(dot(acts[k][0], weights[k * n + p][...], (1, 0)) for k in range(terms))
            if joined:
                value += refs[terms][...].astype(F32)
            out[...] = rounded(value)


def spread_call(acts_t, which, tokens, weights, places, got=None):
    _, both, hidden = acts_t.shape
    rows = both // 2
    width = sum(length for _, length, _ in places)
    tile = 256
    tiles = backward_tiles(places, tile)

    def spec(p, m):
        steps = [t for t, (q, _) in enumerate(tiles) if q == p]
        first, last = steps[0], steps[-1]
        return pl.BlockSpec((hidden, tile), lambda t: (m, jnp.clip(t, first, last) - first))

    out = pl.BlockSpec((rows, tile), lambda t: (0, t))
    return kernel_call(
        functools.partial(spread_kernel, tiles, len(which), got is not None),
        (len(tiles),),
        [
            pl.BlockSpec((1, rows, hidden), lambda t, k=k: (k, tokens, 0), pipeline_mode=pl.Buffered(1))
            for k in which
        ]
        + ([] if got is None else [out])
        + [spec(p, m) for pieces in weights for p, (_, m) in enumerate(pieces)],
        out,
        sds((rows, width), BF16),
        0,
        0,
    )(*[acts_t] * len(which), *([] if got is None else [got]), *[a for pieces in weights for a, _ in pieces])


def join_kernel(own, other, out):
    out[...] = rounded(own[...].astype(F32) + other[...].astype(F32))


def join_call(own, other):
    rows, width = own.shape
    spec = pl.BlockSpec((rows // 3, width), lambda i: (i, 0))
    return kernel_call(join_kernel, (3,), [spec, spec], spec, sds(own.shape, BF16), 0, 0)(own, other)


def weight_grad_kernel(left, first, second, *outs):
    def write(right):
        value = dot(left[0], right[...], (1, 0))
        start = 0
        for out in outs:
            length = out.shape[1]
            out[...] = rounded(value[:, start : start + length])
            start += length

    pl.when(pl.program_id(0) == 0)(lambda: write(first))
    pl.when(pl.program_id(0) > 0)(lambda: write(second))


def weight_grad_call(acts, first, second, lengths):
    _, hidden, both = acts.shape
    tile = hidden // 4
    return kernel_call(
        weight_grad_kernel,
        (3, 4),
        [pl.BlockSpec((1, tile, both), lambda m, i: (m, i, 0)), single(first.shape), single(second.shape)],
        [pl.BlockSpec((tile, n), lambda m, i: (4 * m + i, 0)) for n in lengths],
        [sds((3 * hidden, n), BF16) for n in lengths],
        0,
        0,
    )(acts, first, second)


def met_kernel(a, b, c, d, first, second):
    first[...] = rounded(a[...].astype(F32) + b[...].astype(F32))
    second[...] = rounded(c[...].astype(F32) + d[...].astype(F32))


def met_call(a, b, c, d):
    steps = 6 if a.shape[0] % 96 == 0 else 1
    left = pl.BlockSpec((a.shape[0] // steps, a.shape[1]), lambda i: (i, 0))
    return kernel_call(
        met_kernel,
        (steps,),
        [left] * 4,
        [left] * 2,
        [sds(a.shape, BF16)] * 2,
        0,
        0,
    )(a, b, c, d)


def total_kernel(scal, own, x_first, y_first, x_second, y_second, mine, sent):
    shard = mine.shape[1]
    first = own[:, :shard].astype(F32) + x_first[...].astype(F32) + y_first[...].astype(F32)
    second = own[:, shard:].astype(F32) + x_second[...].astype(F32) + y_second[...].astype(F32)
    core = scal[1]
    mine[...] = jnp.where(core == 0, first, second)
    sent[...] = rounded(jnp.where(core == 0, second, first))


def total_call(scal, own, near):
    rows, span = own.shape
    tile = rows // 12
    half = pl.BlockSpec((tile, span // 2), lambda i: (i, 0))
    return kernel_call(
        total_kernel,
        (12,),
        [SCALARS, pl.BlockSpec((tile, span), lambda i: (i, 0))] + [half] * 4,
        [half] * 2,
        [sds((rows, span // 2), F32), sds((rows, span // 2), BF16)],
        0,
        0,
    )(scal, own, *near)


def lay_kernel(scal, *refs):
    mine, got, outs = refs[:3], refs[3:6], refs[6:]

    @pl.when(pl.program_id(0) == 0)
    def _():
        for m in range(3):
            outs[m][...] = mine[m][...]

    @pl.when(pl.program_id(0) == 1)
    def _():
        for m in range(3):
            outs[m][...] = got[m][...].astype(F32)


def lay_call(scal, mine, got):
    rows, shard = mine.shape
    part = rows // 3
    return prefetch_call(
        lay_kernel,
        scal,
        (2,),
        [pl.BlockSpec((part, shard), lambda i, s, m=m: (m, 0)) for m in range(3)] * 2,
        [pl.BlockSpec((part, shard), lambda i, s: (jnp.where(i == 0, s[1], 1 - s[1]), 0))] * 3,
        [sds((2 * part, shard), F32)] * 3,
        [mine] * 3 + [got] * 3,
    )


def pair_grad_kernel(scal, left_own, left_sent, first, second, own, sent):
    inner = first.shape[1]
    own[:, :inner] = dot(left_own[...], first[...], (0, 0))
    own[:, inner:] = dot(left_own[...], second[...], (0, 0))
    sent[:, :inner] = rounded(dot(left_sent[...], first[...], (0, 0)))
    sent[:, inner:] = rounded(dot(left_sent[...], second[...], (0, 0)))


def rows_grad_call(scal, left, first, second, shard):
    rows, width = left.shape
    columns = first.shape[1] + second.shape[1]
    count = width // (2 * shard)
    return prefetch_call(
        pair_grad_kernel,
        scal,
        (count,),
        [
            pl.BlockSpec((rows, shard), lambda r, s: (0, 2 * r + s[1])),
            pl.BlockSpec((rows, shard), lambda r, s: (0, 2 * r + 1 - s[1])),
            pl.BlockSpec(first.shape, lambda r, s: (0, 0)),
            pl.BlockSpec(second.shape, lambda r, s: (0, 0)),
        ],
        [pl.BlockSpec((shard, columns), lambda r, s: (r, 0))] * 2,
        [sds((count * shard, columns), F32), sds((count * shard, columns), BF16)],
        [left, left, first, second],
    )


def columns_grad_kernel(scal, left, right_own, right_sent, own, sent, left_t):
    @pl.when(pl.program_id(0) == 0)
    def _():
        left_t[...] = left[...].T

    own[...] = dot(left_t[...], right_own[...], (1, 0))
    sent[...] = rounded(dot(left_t[...], right_sent[...], (1, 0)))


def columns_grad_call(scal, left, right, shard):
    rows, inner = left.shape
    count = right.shape[1] // (2 * shard)
    return pl.pallas_call(
        columns_grad_kernel,
        grid_spec=pltpu.PrefetchScalarGridSpec(
            num_scalar_prefetch=1,
            grid=(count,),
            in_specs=[
                pl.BlockSpec((rows, inner), lambda r, s: (0, 0)),
                pl.BlockSpec((rows, shard), lambda r, s: (0, 2 * r + s[1])),
                pl.BlockSpec((rows, shard), lambda r, s: (0, 2 * r + 1 - s[1])),
            ],
            out_specs=[pl.BlockSpec((inner, shard), lambda r, s: (0, r))] * 2,
            scratch_shapes=[pltpu.VMEM((inner, rows), BF16)],
        ),
        out_shape=[sds((inner, count * shard), F32), sds((inner, count * shard), BF16)],
        compiler_params=pltpu.CompilerParams(vmem_limit_bytes=VMEM_BYTES),
        cost_estimate=cost(columns_grad_kernel),
    )(scal, left, right, right)


def cut_kernel(axis, mine, got, *outs):
    value = rounded(mine[...] + got[...].astype(F32))
    start = 0
    for out in outs:
        length = out.shape[axis]
        out[...] = lax.slice_in_dim(value, start, start + length, axis=axis)
        start += length


def cut_call(mine, got, axis):
    eighth = mine.shape[axis] // 8
    shapes = []
    for length in [2 * eighth] + [eighth] * 6:
        shape = list(mine.shape)
        shape[axis] = length
        shapes.append(sds(tuple(shape), BF16))
    return kernel_call(
        functools.partial(cut_kernel, axis),
        (1,),
        [whole(mine), whole(got)],
        [whole(v) for v in shapes],
        shapes,
        0,
        0,
    )(mine, got)


def end_kernel(axis, own, x_first, y_first, x_second, y_second, *outs):
    value = own[...].astype(F32)
    size = x_first.shape[axis]
    first = lax.slice_in_dim(value, 0, size, axis=axis) + x_first[...].astype(F32) + y_first[...].astype(F32)
    second = lax.slice_in_dim(value, size, 2 * size, axis=axis)
    second = second + x_second[...].astype(F32) + y_second[...].astype(F32)
    value = jnp.concatenate([first, second], axis)
    start = 0
    for out in outs:
        length = out.shape[1]
        out[...] = value[:, start : start + length]
        start += length


def end_call(own, near, axis, lengths):
    outs = [sds((own.shape[0], n), F32) for n in lengths]
    return kernel_call(
        functools.partial(end_kernel, axis),
        (1,),
        [whole(own)] + [whole(v) for v in near],
        [whole(v) for v in outs],
        outs,
        0,
        0,
    )(own, *near)


def route_kernel(top_count, hid, attn_add, gain, router_t, routes, resid, moe_low, gates):
    value = hid[...].astype(F32) + attn_add[...].astype(F32)
    resid[...] = value
    moe_low[...] = rounded(value * kernel_inverse_rms(value) * gain[...])
    logits = dot(moe_low[...], router_t[...], (1, 1))
    numbers = lax.broadcasted_iota(jnp.int32, logits.shape, 1)
    chosen = routes[:, 0:1] == numbers
    for k in range(1, top_count):
        chosen = chosen | (routes[:, k : k + 1] == numbers)
    top = jnp.max(jnp.where(chosen, logits, HIDE), -1, keepdims=True)
    lift = jnp.where(chosen, jnp.exp(jnp.where(chosen, logits, top) - top), 0.0)
    gates[...] = lift / jnp.sum(lift, -1, keepdims=True)


def row_specs(arrays, rows, tile):
    return [
        pl.BlockSpec((tile, a.shape[1]), lambda i: (i, 0)) if a.shape[0] == rows else whole(a) for a in arrays
    ]


def route_call(hid, attn_add, gain, router_t, routes):
    rows, width = hid.shape
    tile = rows // 3
    arrays = (hid, attn_add, gain, router_t, routes)
    outs = [sds((rows, width), F32), sds((rows, width), BF16), sds((rows, router_t.shape[0]), F32)]
    return kernel_call(
        functools.partial(route_kernel, routes.shape[1]),
        (3,),
        row_specs(arrays, rows, tile),
        row_specs(outs, rows, tile),
        outs,
        40 * rows * width,
        10 * rows * width,
    )(*arrays)


def route_back_kernel(
    grad_moe, gate_grads, gates, resid, cot, router_t, gain, grad_resid, resid_low, grad_logits, grad_gain
):
    chosen = gates[...]
    part = gate_grads[...]
    middle = jnp.sum(chosen * part, -1, keepdims=True)
    grad_logits[...] = rounded(chosen * (part - middle))
    total = grad_moe[...].astype(F32) + dot(grad_logits[...], router_t[...], (1, 0))
    value = resid[...]
    shrink = kernel_inverse_rms(value)
    normal = value * shrink

    @pl.when(pl.program_id(0) == 0)
    def _():
        grad_gain[...] = jnp.zeros(grad_gain.shape, F32)

    grad_gain[...] += jnp.sum(total * normal, 0, keepdims=True)
    scaled = total * gain[...]
    mean = jnp.mean(scaled * normal, axis=-1, keepdims=True)
    out = cot[...].astype(F32) + shrink * (scaled - normal * mean)
    grad_resid[...] = out
    resid_low[...] = rounded(out)


def route_back_call(grad_moe, gate_grads, gates, resid, cot, router_t, gain):
    rows, width = resid.shape
    tile = rows // 3
    arrays = (grad_moe, gate_grads, gates, resid, cot, router_t, gain)
    outs = [
        sds((rows, width), F32),
        sds((rows, width), BF16),
        sds(gates.shape, BF16),
        sds((1, width), F32),
    ]
    return kernel_call(
        route_back_kernel,
        (3,),
        row_specs(arrays, rows, tile),
        row_specs(outs, rows, tile),
        outs,
        50 * rows * width,
        14 * rows * width,
    )(*arrays)


def to_whole_order(scal, blocks, value, out):
    span = value.shape[1] // blocks
    for j in range(blocks):
        target = pl.multiple_of((scal[0] ^ j) * span, span)
        out[:, pl.ds(target, span)] = value[:, j * span : (j + 1) * span]


def add_kernel(blocks, scal, first, second, out):
    value = rounded(first[...] + second[...].astype(F32))
    to_whole_order(scal, blocks, value, out)


def add_call(scal, resid, part, blocks):
    rows, width = part.shape
    return prefetch_call(
        functools.partial(add_kernel, blocks),
        scal,
        (1,),
        [pl.BlockSpec((rows, width), lambda i, s: (s[2], 0)), pl.BlockSpec((rows, width), lambda i, s: (0, 0))],
        pl.BlockSpec((rows, width), lambda i, s: (0, 0)),
        sds((rows, width), BF16),
        [resid, part],
    )


def last_kernel(blocks, scal, hid, grad_resid, grad_normed, gain, out, wide):
    wide[...] = hid[...].astype(F32)
    rows = out.shape[0]
    tokens = wide[pl.ds(pl.multiple_of(scal[2] * rows, 8), rows)]
    shrink = kernel_inverse_rms(tokens)
    normal = tokens * shrink
    scaled = grad_normed[...].astype(F32) * gain[...]
    middle = jnp.mean(scaled * normal, axis=-1, keepdims=True)
    value = rounded(grad_resid[...] + shrink * (scaled - normal * middle))
    to_whole_order(scal, blocks, value, out)


def last_call(scal, hid, grad_resid, grad_normed, gain, blocks):
    rows, width = grad_normed.shape
    part = pl.BlockSpec((rows, width), lambda i, s: (0, 0))
    return prefetch_call(
        functools.partial(last_kernel, blocks),
        scal,
        (1,),
        [whole(hid), pl.BlockSpec((rows, width), lambda i, s: (s[2], 0)), part, whole(gain)],
        part,
        sds((rows, width), BF16),
        [hid, grad_resid, grad_normed, gain],
        [pltpu.VMEM(hid.shape, F32)],
    )


def angle_tables(positions):
    half_size = HEAD // 2
    frequency = jnp.exp(jnp.arange(half_size, dtype=F32) * (-2.0 * math.log(THETA) / HEAD))
    angles = positions.astype(F32)[..., None] * frequency
    sine = jnp.sin(angles)
    cosine = jnp.cos(angles)
    return jnp.concatenate([cosine, cosine], -1), jnp.concatenate([-sine, sine], -1)


def lookup_parent(segment_ids, parent):
    seg_table = jnp.arange(parent.shape[-1], dtype=jnp.int32)
    return jnp.sum(jnp.where(segment_ids[..., None] == seg_table, parent, 0), -1)


def shards(
    hidden,
    cotangent,
    gain_attn,
    query_weight,
    key_weight,
    value_weight,
    gain_query,
    gain_key,
    out_weight,
    gain_moe,
    router_weight,
    gate_weight,
    up_weight,
    down_weight,
    segment,
    parent,
    tree_depth,
    routes,
):
    _, rows, width = hidden.shape
    dp, x, core = place()
    ctx = lax.axis_index("ctx")
    count = lax.axis_size("dp")
    paired = count == 2
    chips = 2 * count
    tensor = lax.axis_size("tensor")
    heads = HEADS_Q // tensor
    shard = query_weight.shape[0]
    span = 2 * shard
    inner = heads * HEAD
    columns = inner + 2 * HEAD
    half = EXPERTS // 2
    hid = down_weight.shape[1]
    scal = jnp.stack([flips(), core, lax.axis_index("tensor")]).astype(jnp.int32)
    hidden_rows = half * hid

    def by_core(own, other, axis):
        return jnp.where(core == 0, jnp.stack([own, other], axis), jnp.stack([other, own], axis))

    def five_places(size):
        starts = [0, span, 2 * span, 3 * span, 3 * span + size // 2]
        return list(zip(starts, [size, size, size, size // 2, size // 2], [0] * 5))

    def both_cores(own, size):
        return own + [to_core(a) for a in own], [(s, n, k) for k in (1, 2) for s, n, _ in five_places(size)]

    def whole_piece(block, axis):
        own = gather_whole(block, axis)
        cut = own.shape[:axis] + (chips, shard) + own.shape[axis + 1 :]
        full = by_core(own.reshape(cut), to_core(own).reshape(cut), axis + 1)
        return [full.reshape(own.shape[:axis] + (width,) + own.shape[axis + 1 :])], [(0, width, 0)]

    per = gain_query.shape[0]
    heads_column = jnp.pad(jnp.concatenate([gain_query, gain_key]), (0, shard - 2 * per))
    small = [router_weight, gain_attn[:, None], gain_moe[:, None], heads_column[:, None]]
    small.append(jnp.zeros((shard, HEAD - EXPERTS - 3), BF16))
    qkv_shard = jnp.concatenate([query_weight, key_weight, value_weight] + small, 1)
    expert_weights = [down_weight, gate_weight.transpose(0, 2, 1), up_weight.transpose(0, 2, 1)]
    if paired:
        qkv_x, qkv_y = exchange(qkv_shard, qkv_shard)
        far_second, far_first = exchange(halves(qkv_y, 0)[1], halves(qkv_x, 0)[0])
        expert_got = to_core(other_half_call(after(scal, qkv_x), expert_weights))
        expert_block = block_call(scal, expert_weights, expert_got)
        qkv_pieces, qkv_places = both_cores([qkv_shard, qkv_x, qkv_y, far_first, far_second], shard)
        out_x, out_y = exchange(out_weight, out_weight, far_first, far_second)
        out_far_second, out_far_first = exchange(halves(out_y, 1)[1], halves(out_x, 1)[0])
        out_pieces, out_places = both_cores([out_weight, out_x, out_y, out_far_first, out_far_second], shard)
        gains = ()
    else:
        qkv_pieces, qkv_places = whole_piece(qkv_shard, 0)
        small_t = qkv_pieces[0][:, columns:].T
        router_t = small_t[:EXPERTS]
        gain_one, gain_two = (small_t[EXPERTS + i][None].astype(F32) for i in range(2))
        gain_heads = relative(small_t[EXPERTS + 2]).reshape(2 * chips, shard).astype(F32)
        gain_q = gain_heads[:, :per].reshape(1, HEAD)
        gain_k = gain_heads[:, per : 2 * per].reshape(1, HEAD)
        gains = (gain_one, gain_q, gain_k)
        out_pieces, out_places = whole_piece(out_weight, 1)
        sent = [lax.dynamic_slice_in_dim(w, (1 - core) * half, half, 0) for w in expert_weights]
        own = [lax.dynamic_slice_in_dim(w, core * half, half, 0) for w in expert_weights]
        expert_block = by_core(jnp.stack(own), to_core(jnp.stack(sent)), 3).reshape(3 * hidden_rows, span)

    cosine, sine = angle_tables(tree_depth[0])
    *found, normed, tokens_low, raw, rot = qkv_call(
        scal, hidden[0], gains, cosine, sine, qkv_pieces, qkv_places, shard, per, chips, columns
    )
    if found:
        gain_one, gain_two, router_t, gain_q, gain_k = found
    key_value = rot[:, inner:]
    kv_x = to_x(key_value)
    kv_other = to_core(key_value)
    kv_all = jnp.concatenate([key_value, kv_other, kv_x, to_core(kv_x)])
    if paired:
        near_x, near_y = exchange(expert_block, expert_block, kv_x, out_far_first)
        forwarded, expert_pieces = [], []
        gate = ()
        for m in range(3):
            rows_of = slice(m * hidden_rows, (m + 1) * hidden_rows)
            forwarded.append((near_y[rows_of, shard:], near_x[rows_of, :shard]))
            far_second, far_first = exchange(*forwarded[-1], *gate)
            gate = (far_first, far_second)
            expert_pieces.append([(expert_block, m), (near_x, m), (near_y, m), (far_first, 0), (far_second, 0)])
        expert_places = five_places(span)
    else:
        gathered = gather_whole(expert_block, 1)
        expert_pieces = [[(gathered, m)] for m in range(3)]
        expert_places = [(0, width, 0)]
    down_pieces, gate_pieces, up_pieces = expert_pieces

    seg = segment[0].reshape(2, 2, rows)
    seg_rel = flip(flip(seg, 0, x), 1, core).reshape(4 * rows)
    position = jnp.arange(4 * rows, dtype=jnp.int32).reshape(2, 2, rows)
    key_pos = flip(flip(position, 0, x), 1, core).reshape(4 * rows)
    first_up = lookup_parent(seg_rel[:rows], parent[0])
    second_up = lookup_parent(first_up, parent[0])
    key_side = jnp.stack([seg_rel, key_pos], 1)
    query_side = jnp.stack([seg_rel[:rows], first_up, second_up, key_pos[:rows]])

    mixed_low, inverse = attend_call(rot, kv_all, key_side, query_side, heads)
    attn_part = project_call(scal, mixed_low, out_pieces, out_places, shard, width)
    attn_add = lax.psum(attn_part, "tensor")

    cot = permute_width(cotangent[0], scal, chips)
    cot_other = to_core(cot)
    grad_act, pair_dy = products_call(cot, cot_other, down_pieces, hidden_rows)
    if paired:
        attn_add = after(attn_add, down_pieces[3][0], down_pieces[4][0])
    resid, moe_low, gates = route_call(tokens_low, attn_add, gain_two, router_t, routes[0])
    moe_other = to_core(moe_low)
    gate_pre, pair_x = products_call(moe_low, moe_other, gate_pieces, hidden_rows)
    gates_t = gates.T
    gates_own = lax.dynamic_slice_in_dim(gates_t, core * half, half, 0)
    gates_sent = lax.dynamic_slice_in_dim(gates_t, (1 - core) * half, half, 0)
    gate_pair = jnp.concatenate([gates_own, to_core(gates_sent)], 1)[:, None, :]

    acts, acts_t, gate_part = experts_call(pair_x, gate_pre, grad_act, gate_pair, up_pieces, hid)
    weights = [gate_pieces, up_pieces]
    part_other = to_core(spread_call(acts_t, (1, 2), 1, weights, expert_places))
    moe_sum = spread_call(acts_t, (1, 2), 0, weights, expert_places, part_other)
    grad_moe_in = lax.psum(moe_sum, "tensor")
    acts, acts_t, gate_part = lax.optimization_barrier((acts, acts_t, gate_part, moe_sum))[:3]
    gate_grads = gate_join_call(scal, *gate_sum_call(gate_part))

    lengths = [span] + [shard] * 6 if paired else [span] * chips
    grad_blocks = weight_grad_call(acts, pair_dy, pair_x, lengths)
    acts_t = after(acts_t, grad_blocks[0])
    grad_moe_in = after(grad_moe_in, grad_blocks[0])
    if paired:
        own_grads, x_first, x_second, y_first, y_second, far_first, far_second = grad_blocks
        far_x, far_y = exchange(far_first, far_second)
        x_first, y_second = exchange(x_first, y_second)
        grad_moe_in = after(grad_moe_in, far_x, far_y)
    out_other = to_core(spread_call(acts_t, (0,), 1, [down_pieces], expert_places))
    out_sum = join_call(spread_call(acts_t, (0,), 0, [down_pieces], expert_places), out_other)
    grad_moe_in = after(grad_moe_in, out_sum)
    out_sum = after(out_sum, grad_moe_in, gate_grads)
    moe_add = lax.psum_scatter(out_sum, "tensor", scatter_dimension=0, tiled=True)

    grad_resid, resid_low, grad_logits, grad_gain_two = route_back_call(
        grad_moe_in, gate_grads, gates, resid, cot, router_t, gain_two
    )

    grad_mixed = project_back_call(scal, after(resid_low, out_sum), out_pieces, out_places, shard, inner)
    query_back, kv_own, kv_sent, kv_mid, grad_gain_q = attend_back_call(
        rot, kv_all, key_side, query_side, grad_mixed, mixed_low, inverse, raw, cosine, sine, gain_q, heads
    )
    output_rows = add_call(after(scal, query_back), resid, moe_add, chips)
    output = lax.all_gather(output_rows, "tensor", axis=0, tiled=True)[None]
    if paired:
        kv_mid = after(kv_mid, x_first, y_second)
    kv_part, kv_on = kv_pass_call(kv_own, after(kv_mid, output_rows), to_core(kv_sent))
    kv_far = to_x(kv_on)
    if paired:
        x_second, y_first = lax.optimization_barrier(met_call(after(x_second, kv_on), far_y, y_first, far_x))
        kv_part = after(kv_part, x_second)
        x_second, y_first = lax.optimization_barrier((to_x(x_second), to_dp(y_first)))
        near_grads = (x_first, y_first, x_second, y_second)
    back_part, grad_gain_one, kv_back, grad_gain_k = qkv_back_call(
        scal, query_back, kv_part, kv_far, raw, cosine, sine, gain_k, tokens_low, qkv_pieces, qkv_places, shard
    )
    grad_normed = lax.psum_scatter(back_part, "tensor", scatter_dimension=0, tiled=True)
    late_resid, late_mixed, late_normed, late_moe = lax.optimization_barrier(
        (resid_low, mixed_low, normed, moe_low, back_part)
    )[:4]
    grad_router_t = dot(grad_logits, late_moe, (0, 0))
    if paired:
        mine, sent = total_call(scal, own_grads, near_grads)
        late_normed = after(late_normed, mine)
        qkv_mine, qkv_sent = rows_grad_call(scal, late_normed, query_back, kv_back, shard)
        out_mine, out_sent = columns_grad_call(scal, late_mixed, late_resid, shard)
        qkv_blocks = cut_call(qkv_mine, to_core(qkv_sent), 0)
        out_blocks = cut_call(out_mine, to_core(out_sent), 1)

        def plane_sum(blocks, axis, lengths):
            own, x_first, x_second, y_first, y_second, far_first, far_second = blocks
            far_x, far_y = exchange(far_first, far_second)
            x_first, y_second = exchange(x_first, y_second)
            x_second, y_first = met_call(x_second, far_y, y_first, far_x)
            x_second, y_first = exchange(x_second, y_first)
            near = (x_first, y_first, x_second, y_second)
            return end_call(own, near, axis, lengths)

        grad_query, grad_key, grad_value = plane_sum(qkv_blocks, 0, [inner, HEAD, HEAD])
        (grad_out_weight,) = plane_sum(out_blocks, 1, [shard])
    else:
        qkv_back = jnp.concatenate([query_back, kv_back], 1)
        sides = [
            (pick_columns(late_normed, scal, shard, o), pick_columns(late_resid, scal, shard, o))
            for o in (False, True)
        ]
        qkv_mine, qkv_sent = (dot(n, qkv_back, (0, 0)) for n, _ in sides)
        out_mine, out_sent = (dot(late_mixed, r, (0, 0)) for _, r in sides)
        qkv_sum = rounded(qkv_mine + to_core(rounded(qkv_sent)).astype(F32))
        out_sum = rounded(out_mine + to_core(rounded(out_sent)).astype(F32))
        grad_qkv = scatter_whole([qkv_sum[r * shard : (r + 1) * shard] for r in range(chips)])
        grad_query, grad_key, grad_value = jnp.split(grad_qkv, [inner, inner + HEAD], 1)
        grad_out_weight = scatter_whole([out_sum[:, r * shard : (r + 1) * shard] for r in range(chips)])
        total = scatter_whole(grad_blocks)
        mine = lax.dynamic_slice_in_dim(total, core * shard, shard, 1)
        sent = rounded(lax.dynamic_slice_in_dim(total, (1 - core) * shard, shard, 1))
    grad_down, grad_gate, grad_up = (
        v.reshape(EXPERTS, hid, shard) for v in lay_call(scal, mine, to_core(sent))
    )
    grad_gate, grad_up = grad_gate.transpose(0, 2, 1), grad_up.transpose(0, 2, 1)

    if paired:
        grad_normed = after(grad_normed, qkv_sent)
    hidden_rows_out = last_call(scal, tokens_low, grad_resid, grad_normed, gain_one, chips)
    grad_hidden = lax.all_gather(hidden_rows_out, "tensor", axis=0, tiled=True)[None]

    share = 1.0 / tensor
    head_rows = jnp.concatenate(
        [grad_gain_q.reshape(2 * chips, per), grad_gain_k.reshape(2 * chips, per)], 1
    )
    head_rows = relative(jnp.pad(head_rows, ((0, 0), (0, shard - 2 * per))).reshape(width))
    table = jnp.concatenate(
        [
            grad_gain_one,
            grad_gain_two * share,
            grad_router_t * share,
            head_rows[None],
            jnp.zeros((5, width), F32),
        ]
    ).reshape(24, chips, 2, shard)
    table_own = lax.dynamic_index_in_dim(table, core, 2, keepdims=False)
    table_sent = lax.dynamic_index_in_dim(table, 1 - core, 2, keepdims=False)
    table = table_own + to_core(table_sent)
    table = table.reshape(24, count, 2, shard)
    table = table[:, :, 0] + to_x(table[:, :, 1])
    if paired:
        table = table[:, 0] + to_dp(table[:, 1])
    else:
        table = lax.psum_scatter(table, "dp", scatter_dimension=1, tiled=False)
    mine = sum_z(table)
    gains = mine[2 + EXPERTS, : 2 * per]

    return (
        output,
        grad_hidden,
        mine[0],
        grad_query,
        grad_key,
        grad_value,
        gains[:per],
        gains[per:],
        grad_out_weight,
        mine[1],
        mine[2 : 2 + EXPERTS].T,
        grad_gate,
        grad_up,
        grad_down,
    )


def solution(mesh):
    plane = ("dp", "ctx")
    in_specs = (
        P("dp", "ctx", None),
        P("dp", "ctx", None),
        P(plane),
        P(plane, "tensor"),
        P(plane, "tensor"),
        P(plane, "tensor"),
        P(plane),
        P(plane),
        P("tensor", plane),
        P(plane),
        P(plane, None),
        P(None, plane, "tensor"),
        P(None, plane, "tensor"),
        P(None, "tensor", plane),
        P("dp", None),
        P("dp", None),
        P("dp", "ctx"),
        P("dp", "ctx", None),
    )
    out_specs = (
        P("dp", "ctx", None),
        P("dp", "ctx", None),
        P(plane),
        P(plane, "tensor"),
        P(plane, "tensor"),
        P(plane, "tensor"),
        P(plane),
        P(plane),
        P("tensor", plane),
        P(plane),
        P(plane, None),
        P(None, plane, "tensor"),
        P(None, plane, "tensor"),
        P(None, "tensor", plane),
    )
    return jax.shard_map(shards, mesh=mesh, in_specs=in_specs, out_specs=out_specs, check_vma=False)
```

```python
import functools
import math

import jax
import jax.numpy as jnp
from jax import lax
from jax.experimental import pallas as pl
from jax.experimental.pallas import tpu as pltpu
from jax.sharding import PartitionSpec as P

HEADS_Q = 32
HEADS_KV = 4
HEAD = 128
TOP = 8
EXPERTS = 16

EPS = 1e-06
THETA = 1000000.0
LOG2E = 1.4426950408889634
HIDE = -1e30

F32 = jnp.float32
BF16 = jnp.bfloat16
VMEM_BYTES = 58 * 1024 * 1024


def rounded(v):
    return v.astype(BF16)


def dot(a, b, contract):
    return lax.dot_general(a, b, ((contract[:1], contract[1:]), ((), ())), preferred_element_type=F32)


def after(value, *others):
    return lax.optimization_barrier((value,) + others)[0]


def to_core(v):
    return lax.ppermute(v, "ctx", [(i, i ^ 1) for i in range(4)])


def to_x(v):
    return lax.ppermute(v, "ctx", [(i, i ^ 2) for i in range(4)])


def to_dp(v):
    return lax.ppermute(v, "dp", [(0, 1), (1, 0)])


def exchange(x_value, y_value, *gate):
    x_value, y_value = after((x_value, y_value), *gate) if gate else lax.optimization_barrier((x_value, y_value))
    return lax.optimization_barrier((to_x(x_value), to_dp(y_value)))


def sum_z(v):
    size = lax.axis_size("tensor")
    one, two, three = (lax.ppermute(v, "tensor", [(i, i ^ k) for i in range(size)]) for k in (1, 2, 3))
    return (v + one) + (two + three)


def place():
    ctx = lax.axis_index("ctx")
    return lax.axis_index("dp"), ctx // 2, ctx % 2


def flips():
    dp, x, _ = place()
    return x + 2 * dp if lax.axis_size("dp") == 2 else x


def flip(v, axis, bit):
    return jnp.where(bit == 0, v, jnp.flip(v, axis))


def relative(v):
    dp, x, _ = place()
    count = lax.axis_size("dp")
    cut = v.reshape(v.shape[:-1] + (count, 2, v.shape[-1] // (2 * count)))
    cut = flip(cut, cut.ndim - 2, x)
    if count == 2:
        cut = flip(cut, cut.ndim - 3, dp)
    return cut.reshape(v.shape)


def halves(v, axis):
    return jnp.split(v, 2, axis)


def gather_whole(block, axis):
    pair = jnp.concatenate([block, to_x(block)], axis)
    return lax.all_gather(pair, "dp", axis=axis, tiled=True)


def scatter_whole(blocks):
    kept = jnp.stack(blocks[0::2]).astype(F32) + to_x(jnp.stack(blocks[1::2])).astype(F32)
    return lax.psum_scatter(rounded(kept), "dp", scatter_dimension=0, tiled=False).astype(F32)


def whole(array):
    dims = len(array.shape)
    return pl.BlockSpec(array.shape, lambda *_: (0,) * dims)


SCALARS = pl.BlockSpec(memory_space=pltpu.SMEM)


TIMES = {
    "permute_kernel": 4.6, "half_kernel": 4, "block_kernel": 6, "qkv_kernel": 11.7,
    "attend_kernel": 16.3, "attend_back_kernel": 30, "project_kernel": 6.6, "project_back_kernel": 6.5,
    "kv_pass_kernel": 2, "qkv_back_kernel": 9.8, "products_kernel": 11.8, "experts_kernel": 20,
    "spread_kernel": 10, "join_kernel": 1, "weight_grad_kernel": 50, "met_kernel": 0.5, "total_kernel": 0.5,
    "lay_kernel": 0.5, "pair_grad_kernel": 0.5, "columns_grad_kernel": 0.5, "cut_kernel": 0.3, "end_kernel": 0.3,
    "route_kernel": 6.3, "route_back_kernel": 8.6, "add_kernel": 2.2, "last_kernel": 6.2,
}


def cost(body):
    name = getattr(body, "func", body).__name__
    return pl.CostEstimate(flops=int(TIMES.get(name, 0.3) * 1e9), bytes_accessed=0, transcendentals=0)


def kernel_call(body, grid, in_specs, out_specs, out_shape, flops, moved, scratch=()):
    return pl.pallas_call(
        body,
        grid=grid,
        in_specs=in_specs,
        out_specs=out_specs,
        out_shape=out_shape,
        scratch_shapes=list(scratch),
        compiler_params=pltpu.CompilerParams(vmem_limit_bytes=VMEM_BYTES),
        cost_estimate=cost(body),
    )


def sds(shape, dtype):
    return jax.ShapeDtypeStruct(shape, dtype)


def piece_starts(scal, places, shard):
    core = scal[1]
    shift = {0: 0, 1: core * shard, 2: (1 - core) * shard}
    return [
        (start if kind == 0 else pl.multiple_of(start + shift[kind], length), length)
        for start, length, kind in places
    ]


def kernel_inverse_rms(v):
    return lax.rsqrt(jnp.mean(v * v, axis=-1, keepdims=True) + EPS)


def permute_kernel(scal, in_ref, out_ref):
    out_ref[...] = in_ref[...]


def permute_width(v, scal, blocks):
    rows, width = v.shape
    span = width // blocks
    return pl.pallas_call(
        permute_kernel,
        grid_spec=pltpu.PrefetchScalarGridSpec(
            num_scalar_prefetch=1,
            grid=(blocks,),
            in_specs=[pl.BlockSpec((rows, span), lambda j, s: (0, j ^ s[0]))],
            out_specs=pl.BlockSpec((rows, span), lambda j, s: (0, j)),
        ),
        out_shape=sds(v.shape, v.dtype),
        cost_estimate=cost(permute_kernel),
    )(scal, v)


def pick_columns(v, scal, shard, other):
    rows, width = v.shape
    count = width // (2 * shard)
    which = 1 - scal[1] if other else scal[1]
    cut = v.reshape(rows, count, 2, shard)
    return lax.dynamic_index_in_dim(cut, which, 2, keepdims=False).reshape(rows, count * shard)


def prefetch_call(body, scal, grid, in_specs, out_specs, out_shape, arrays, scratch=()):
    return pl.pallas_call(
        body,
        grid_spec=pltpu.PrefetchScalarGridSpec(
            num_scalar_prefetch=1,
            grid=grid,
            in_specs=in_specs,
            out_specs=out_specs,
            scratch_shapes=list(scratch),
        ),
        out_shape=out_shape,
        compiler_params=pltpu.CompilerParams(vmem_limit_bytes=VMEM_BYTES),
        cost_estimate=cost(body),
    )(scal, *arrays)


def half_kernel(scal, *refs):
    ins, out = refs[:3], refs[3]
    for m in range(3):

        @pl.when(pl.program_id(0) == m)
        def _():
            out[0] = ins[m][...]


def other_half_call(scal, weights):
    experts, hid, shard = weights[0].shape
    half = experts // 2
    return prefetch_call(
        half_kernel,
        scal,
        (3,),
        [pl.BlockSpec((half, hid, shard), lambda m, s: (1 - s[1], 0, 0))] * 3,
        pl.BlockSpec((1, half, hid, shard), lambda m, s: (m, 0, 0, 0)),
        sds((3, half, hid, shard), BF16),
        weights,
    )


def block_kernel(scal, *refs):
    ins, got, out = refs[:3], refs[3], refs[4]
    shard = got.shape[3]
    rows = out.shape[0]
    other = pl.ds(pl.multiple_of((1 - scal[1]) * shard, shard), shard)
    out[:, other] = got[0].reshape(rows, shard)
    for m in range(3):

        @pl.when(pl.program_id(0) == m)
        def _():
            out[:, pl.ds(pl.multiple_of(scal[1] * shard, shard), shard)] = ins[m][...].reshape(rows, shard)


def block_call(scal, weights, got):
    experts, hid, shard = weights[0].shape
    half = experts // 2
    return prefetch_call(
        block_kernel,
        scal,
        (3,),
        [pl.BlockSpec((half, hid, shard), lambda m, s: (s[1], 0, 0))] * 3
        + [pl.BlockSpec((1, half, hid, shard), lambda m, s: (m, 0, 0, 0))],
        pl.BlockSpec((half * hid, 2 * shard), lambda m, s: (m, 0)),
        sds((3 * half * hid, 2 * shard), BF16),
        [*weights, got],
    )


def read_small(places, shard, per, scal, pieces, gain_one, gain_two, router_t, gain_q, gain_k):
    gain_q[...] = jnp.zeros(gain_q.shape, F32)
    gain_k[...] = jnp.zeros(gain_k.shape, F32)
    lane = lax.broadcasted_iota(jnp.int32, (shard // 2, HEAD), 0)
    target = lax.broadcasted_iota(jnp.int32, (shard // 2, HEAD), 1)
    for (start, length), (fixed, _, kind), ref in zip(piece_starts(scal, places, shard), places, pieces):
        value = ref[...].astype(F32).T
        lanes = pl.ds(start, length)
        router_t[:, lanes] = rounded(value[:EXPERTS])
        gain_one[:, lanes] = value[EXPERTS : EXPERTS + 1]
        gain_two[:, lanes] = value[EXPERTS + 1 : EXPERTS + 2]
        if fixed % shard:
            continue
        half = scal[1] if kind == 1 else 1 - scal[1]
        heads = rounded(value[EXPERTS + 2 : EXPERTS + 3, : shard // 2])
        first = (2 * ((fixed // (2 * shard)) ^ scal[0]) + half) * per
        in_q = (target == first + lane) & (lane < per)
        in_k = (target == first + lane - per) & (lane >= per) & (lane < 2 * per)
        gain_q[...] += dot(heads, jnp.where(in_q, 1.0, 0.0).astype(BF16), (1, 0))
        gain_k[...] += dot(heads, jnp.where(in_k, 1.0, 0.0).astype(BF16), (1, 0))


def qkv_kernel(places, shard, per, blocks, given, scal, hid, cos, sin, *refs):
    n = len(places)
    weights, refs = refs[:n], refs[n:]
    if given:
        gain, gain_q, gain_k, normed, hid_rel, raw, rot = refs
    else:
        smalls, (gain, gain_two, router_t, gain_q, gain_k, normed, hid_rel, raw, rot) = refs[:n], refs[n:]
    step, last = pl.program_id(0), pl.num_programs(0) - 1
    width = hid.shape[1]
    span = width // blocks

    @pl.when(step == 0)
    def _():
        if not given:
            read_small(places, shard, per, scal, smalls, gain, gain_two, router_t, gain_q, gain_k)
        for j in range(blocks):
            source = pl.multiple_of((scal[0] ^ j) * span, span)
            hid_rel[:, j * span : (j + 1) * span] = hid[:, pl.ds(source, span)]
        tokens = hid_rel[...].astype(F32)
        normed[...] = rounded(tokens * kernel_inverse_rms(tokens) * gain[...])

    total = jnp.zeros(raw.shape, F32)
    for (start, length), weight in zip(piece_starts(scal, places, shard), weights):
        total += dot(normed[:, pl.ds(start, length)], weight[...], (1, 0))
    raw[...] = total
    vector = jnp.where(step == last, gain_k[...], gain_q[...])
    for head in range(2):
        cut = total[:, head * HEAD : (head + 1) * HEAD]
        scaled = cut * kernel_inverse_rms(cut) * vector
        turned = scaled * cos[...] + pltpu.roll(scaled, HEAD // 2, 1) * sin[...]
        if head == 1:
            turned = jnp.where(step == last, cut, turned)
        rot[:, head * HEAD : (head + 1) * HEAD] = rounded(turned)


def qkv_call(scal, hid, gains, cos, sin, pieces, places, shard, per, blocks, columns):
    rows, width = hid.shape
    pair = 2 * HEAD
    block = pl.BlockSpec((rows, pair), lambda i: (0, i))
    weights = [pl.BlockSpec((p.shape[0], pair), lambda i: (0, i)) for p in pieces]
    outs = [sds(hid.shape, BF16), sds(hid.shape, BF16), sds((rows, columns), F32), sds((rows, columns), BF16)]
    specs = [whole(hid), whole(hid), block, block]
    if gains:
        more, more_specs = list(gains), [whole(g) for g in gains]
    else:
        more = pieces
        more_specs = [pl.BlockSpec((p.shape[0], HEAD), lambda i: (0, columns // HEAD)) for p in pieces]
        found = [
            sds((1, width), F32),
            sds((1, width), F32),
            sds((EXPERTS, width), BF16),
            sds((1, HEAD), F32),
            sds((1, HEAD), F32),
        ]
        outs, specs = found + outs, [whole(v) for v in found] + specs
    return kernel_call(
        functools.partial(qkv_kernel, places, shard, per, blocks, bool(gains)),
        (columns // pair,),
        [SCALARS, whole(hid), whole(cos), whole(sin)] + weights + more_specs,
        specs,
        outs,
        0,
        0,
    )(scal, hid, cos, sin, *pieces, *more)


def write_bias(bias, key_side, query_side):
    seg = key_side[:, 0:1]
    seen = (seg == query_side[0:1]) | (seg == query_side[1:2]) | (seg == query_side[2:3])
    seen = seen & (key_side[:, 1:2] <= query_side[3:4])
    bias[...] = jnp.where(seen, 0.0, HIDE)


def key_tiles(count):
    tile = next(t for t in (640, 384, 256, 128) if count % t == 0)
    return [(s, tile) for s in range(0, count, tile)]


def attend_kernel(query, keys, values, key_side, query_side, mixed, inverse, bias, values_t):
    @pl.when(pl.program_id(0) == 0)
    def _():
        write_bias(bias, key_side[...], query_side[...])
        values_t[...] = values[...].T

    rows = query.shape[0]
    total = jnp.zeros((HEAD, rows), F32)
    row_sum = jnp.zeros((1, rows), F32)
    factor = LOG2E * HEAD**-0.5
    for start, tile in key_tiles(keys.shape[0]):
        raw = dot(keys[start : start + tile], query[...], (1, 1))
        weight = jnp.exp2(raw * factor + bias[start : start + tile])
        row_sum += jnp.sum(weight, 0, keepdims=True)
        total += dot(values_t[:, start : start + tile], rounded(weight), (1, 0))
    scale = 1.0 / row_sum
    mixed[...] = rounded((total * scale).T)
    inverse[0] = scale


def attend_call(rot, kv_all, key_side, query_side, heads):
    rows, count = rot.shape[0], kv_all.shape[0]
    column = pl.BlockSpec((rows, HEAD), lambda h: (0, h))
    return kernel_call(
        attend_kernel,
        (heads,),
        [
            column,
            pl.BlockSpec((count, HEAD), lambda h: (0, 0)),
            pl.BlockSpec((count, HEAD), lambda h: (0, 1)),
            whole(key_side),
            whole(query_side),
        ],
        [column, pl.BlockSpec((1, 1, rows), lambda h: (h, 0, 0))],
        [sds((rows, heads * HEAD), BF16), sds((heads, 1, rows), F32)],
        4 * heads * rows * count * HEAD,
        4 * rows * heads * HEAD + 4 * count * HEAD,
        [pltpu.VMEM((count, rows), F32), pltpu.VMEM((HEAD, count), BF16)],
    )(rot, kv_all, kv_all, key_side, query_side)


def attend_back_kernel(
    query, keys, values, key_side, query_side, grad, mixed, inverse, raw_query, cos, sin, gain,
    query_back, kv_own, kv_sent, kv_mid, grad_gain, bias, keys_t, grad_kv,
):
    @pl.when(pl.program_id(0) == 0)
    def _():
        write_bias(bias, key_side[...], query_side[...])
        keys_t[...] = keys[...].T
        grad_kv[...] = jnp.zeros(grad_kv.shape, F32)
        grad_gain[...] = jnp.zeros(grad_gain.shape, F32)

    rows = query.shape[0]
    scale = HEAD**-0.5
    factor = LOG2E * scale
    both = grad[...].astype(F32) * mixed[...].astype(F32)
    mean = jnp.sum(both.T, 0, keepdims=True)
    norm = inverse[0]
    total = jnp.zeros((HEAD, rows), F32)
    for start, tile in key_tiles(keys.shape[0]):
        span = slice(start, start + tile)
        raw = dot(keys[span], query[...], (1, 1))
        prob = jnp.exp2(raw * factor + bias[span]) * norm
        grad_prob = dot(values[span], grad[...], (1, 1))
        grad_raw = rounded(prob * (grad_prob - mean))
        total += dot(keys_t[:, span], grad_raw, (1, 0))
        grad_kv[span, :HEAD] += dot(grad_raw, query[...], (1, 0))
        grad_kv[span, HEAD:] += dot(rounded(prob), grad[...], (1, 0))
    turned = total.T * scale
    turned = turned * cos[...] - pltpu.roll(turned, HEAD // 2, 1) * sin[...]
    value = raw_query[...]
    shrink = kernel_inverse_rms(value)
    normal = value * shrink
    grad_gain[...] += jnp.sum(turned * normal, 0, keepdims=True)
    scaled = turned * gain[...]
    middle = jnp.mean(scaled * normal, axis=-1, keepdims=True)
    query_back[...] = rounded(shrink * (scaled - normal * middle))

    @pl.when(pl.program_id(0) == pl.num_programs(0) - 1)
    def _():
        grad_kv[:, :HEAD] = grad_kv[:, :HEAD] * scale
        kv_own[...] = grad_kv[:rows]
        kv_sent[:rows] = rounded(grad_kv[rows : 2 * rows])
        kv_mid[...] = grad_kv[2 * rows : 3 * rows]
        kv_sent[rows:] = rounded(grad_kv[3 * rows :])


def attend_back_call(rot, kv_all, key_side, query_side, grad, mixed, inverse, raw, cos, sin, gain, heads):
    rows, count = rot.shape[0], kv_all.shape[0]
    column = pl.BlockSpec((rows, HEAD), lambda h: (0, h))
    return kernel_call(
        attend_back_kernel,
        (heads,),
        [
            column,
            pl.BlockSpec((count, HEAD), lambda h: (0, 0)),
            pl.BlockSpec((count, HEAD), lambda h: (0, 1)),
            whole(key_side),
            whole(query_side),
            column,
            column,
            pl.BlockSpec((1, 1, rows), lambda h: (h, 0, 0)),
            column,
            whole(cos),
            whole(sin),
            whole(gain),
        ],
        [
            column,
            pl.BlockSpec((rows, 2 * HEAD), lambda h: (0, 0)),
            pl.BlockSpec((2 * rows, 2 * HEAD), lambda h: (0, 0)),
            pl.BlockSpec((rows, 2 * HEAD), lambda h: (0, 0)),
            pl.BlockSpec((1, HEAD), lambda h: (0, 0)),
        ],
        [
            sds((rows, heads * HEAD), BF16),
            sds((rows, 2 * HEAD), F32),
            sds((2 * rows, 2 * HEAD), BF16),
            sds((rows, 2 * HEAD), F32),
            sds((1, HEAD), F32),
        ],
        10 * heads * rows * count * HEAD,
        12 * rows * heads * HEAD + 12 * count * HEAD,
        [
            pltpu.VMEM((count, rows), F32),
            pltpu.VMEM((HEAD, count), BF16),
            pltpu.VMEM((count, 2 * HEAD), F32),
        ],
    )(rot, kv_all, kv_all, key_side, query_side, grad, mixed, inverse, raw, cos, sin, gain)


def project_kernel(places, shard, scal, mixed, *refs):
    out = refs[-1]
    for (start, length), weight in zip(piece_starts(scal, places, shard), refs[:-1]):
        out[:, pl.ds(start, length)] = rounded(dot(mixed[...], weight[...], (1, 0)))


def project_call(scal, mixed, pieces, places, shard, width):
    rows, inner = mixed.shape
    return kernel_call(
        functools.partial(project_kernel, places, shard),
        (1,),
        [SCALARS, whole(mixed)] + [whole(p) for p in pieces],
        pl.BlockSpec((rows, width), lambda i: (0, 0)),
        sds((rows, width), BF16),
        2 * rows * inner * width,
        2 * inner * width + 2 * rows * (inner + width),
    )(scal, mixed, *pieces)


def project_back_kernel(places, shard, scal, grad, *refs):
    out = refs[-1]
    total = jnp.zeros(out.shape, F32)
    for (start, length), weight in zip(piece_starts(scal, places, shard), refs[:-1]):
        total += dot(grad[:, pl.ds(start, length)], weight[...], (1, 1))
    out[...] = rounded(total)


def project_back_call(scal, grad, pieces, places, shard, inner):
    rows, width = grad.shape
    tile = inner // 2
    return kernel_call(
        functools.partial(project_back_kernel, places, shard),
        (2,),
        [SCALARS, whole(grad)] + [pl.BlockSpec((tile, p.shape[1]), lambda i: (i, 0)) for p in pieces],
        pl.BlockSpec((rows, tile), lambda i: (0, i)),
        sds((rows, inner), BF16),
        2 * rows * inner * width,
        2 * inner * width + 2 * rows * (inner + width),
    )(scal, grad, *pieces)


def kv_pass_kernel(own, mid, got, part, sent):
    rows = own.shape[0]
    part[...] = own[...] + got[:rows].astype(F32)
    sent[...] = rounded(mid[...] + got[rows:].astype(F32))


def kv_pass_call(own, mid, got):
    return kernel_call(
        kv_pass_kernel,
        (1,),
        [whole(own), whole(mid), whole(got)],
        [whole(own), whole(own)],
        [sds(own.shape, F32), sds(own.shape, BF16)],
        0,
        0,
    )(own, mid, got)


def qkv_back_kernel(
    places, shard, scal, query_back, kv_part, kv_far, raw_key, cos, sin, gain_k, hid, *refs
):
    weights, (part, grad_gain, kv_back, grad_gain_k) = refs[: len(places)], refs[len(places) :]
    inner = query_back.shape[1]
    total = kv_part[...] + kv_far[...].astype(F32)
    turned = total[:, :HEAD]
    turned = turned * cos[...] - pltpu.roll(turned, HEAD // 2, 1) * sin[...]
    value = raw_key[...]
    shrink = kernel_inverse_rms(value)
    normal = value * shrink
    grad_gain_k[...] = jnp.sum(turned * normal, 0, keepdims=True)
    scaled = turned * gain_k[...]
    middle = jnp.mean(scaled * normal, axis=-1, keepdims=True)
    kv_back[:, :HEAD] = rounded(shrink * (scaled - normal * middle))
    kv_back[:, HEAD:] = rounded(total[:, HEAD:])

    tokens = hid[...].astype(F32)
    shrink = kernel_inverse_rms(tokens)
    for (start, length), weight in zip(piece_starts(scal, places, shard), weights):
        lanes = pl.ds(start, length)
        value = dot(query_back[...], weight[:, :inner], (1, 1))
        value += dot(kv_back[...], weight[:, inner : inner + 2 * HEAD], (1, 1))
        part[:, lanes] = rounded(value)
        normal = hid[:, lanes].astype(F32) * shrink
        grad_gain[:, lanes] = jnp.sum(value * normal, 0, keepdims=True)


def qkv_back_call(scal, query_back, kv_part, kv_far, raw, cos, sin, gain_k, hid, pieces, places, shard):
    rows, width = hid.shape
    inner = query_back.shape[1]
    arrays = (cos, sin, gain_k, hid)
    outs = [sds((rows, width), BF16), sds((1, width), F32), sds((rows, 2 * HEAD), BF16), sds((1, HEAD), F32)]
    return kernel_call(
        functools.partial(qkv_back_kernel, places, shard),
        (1,),
        [SCALARS, whole(query_back), whole(kv_part), whole(kv_far)]
        + [pl.BlockSpec((rows, HEAD), lambda i: (0, inner // HEAD))]
        + [whole(a) for a in arrays]
        + [whole(p) for p in pieces],
        [whole(o) for o in outs],
        outs,
        0,
        0,
    )(scal, query_back, kv_part, kv_far, raw, *arrays, *pieces)


def join_rows(own, other, scratch):
    rows = own.shape[0]

    @pl.when(pl.program_id(0) == 0)
    def _():
        scratch[:rows] = own[...]
        scratch[rows:] = other[...]


def product(weights, rows_ref):
    return dot(jnp.concatenate([w[...] for w in weights], 1), rows_ref[...], (1, 1))


def single(shape):
    dims = len(shape)
    return pl.BlockSpec(shape, lambda *_: (0,) * dims, pipeline_mode=pl.Buffered(1))


def products_kernel(own, other, *refs):
    weights, (out, both, pair) = refs[:-3], refs[-3:]
    join_rows(own, other, both)
    out[...] = product(weights, both)

    @pl.when(pl.program_id(0) == 0)
    def _():
        pair[...] = both[...]


def row_pieces(pieces, tile, hidden):
    step = hidden // tile
    return [pl.BlockSpec((tile, a.shape[1]), lambda i, m=m: (i + m * step, 0)) for a, m in pieces]


def products_call(own, other, pieces, hidden):
    rows, width = own.shape
    tile = hidden // 4
    return kernel_call(
        products_kernel,
        (4,),
        [single(own.shape), single(own.shape)] + row_pieces(pieces, tile, hidden),
        [pl.BlockSpec((tile, 2 * rows), lambda i: (i, 0)), single((2 * rows, width))],
        [sds((hidden, 2 * rows), F32), sds((2 * rows, width), BF16)],
        0,
        0,
        [pltpu.VMEM((2 * rows, width), BF16)],
    )(own, other, *[a for a, _ in pieces])


def experts_kernel(hid, both, gate_ref, grad_act, gates, *refs):
    weights, (acts, acts_t, gate_part) = refs[:-3], refs[-3:]
    gate_pre, up_pre = gate_ref[...], product(weights, both)
    sig = 1.0 / (1.0 + jnp.exp(-gate_pre))
    silu = gate_pre * sig
    act = silu * up_pre
    slope = sig * (1.0 + gate_pre * (1.0 - sig))
    count = gates.shape[0]
    for e in range(count):
        rows = slice(e * hid, (e + 1) * hid)
        gate = gates[e]
        raw = grad_act[rows, :]
        back = gate * raw
        acts[0, rows, :] = rounded(gate * act[rows])
        acts[1, rows, :] = rounded(back * up_pre[rows] * slope[rows])
        acts[2, rows, :] = rounded(back * silu[rows])
        gate_part[e] = jnp.sum(act[rows] * raw, 0, keepdims=True)
    for k in range(3):
        acts_t[k] = acts[k].T


def experts_call(pair, gate_pre, grad_act, gates, pieces, hid):
    both, width = pair.shape
    experts = gates.shape[0]
    per = 2
    tile = per * hid
    hidden = experts * hid
    act = pl.BlockSpec((tile, both), lambda i: (i, 0))
    gate = pl.BlockSpec((per, 1, both), lambda i: (i, 0, 0))
    return kernel_call(
        functools.partial(experts_kernel, hid),
        (experts // per,),
        [single(pair.shape), act, act, gate] + row_pieces(pieces, tile, hidden),
        [
            pl.BlockSpec((3, tile, both), lambda i: (0, i, 0)),
            pl.BlockSpec((3, both, tile), lambda i: (0, 0, i)),
            gate,
        ],
        [sds((3, hidden, both), BF16), sds((3, both, hidden), BF16), sds((experts, 1, both), F32)],
        0,
        0,
    )(pair, gate_pre, grad_act, gates, *[a for a, _ in pieces])


def gate_sum_kernel(first, second, third, fourth, own, sent):
    rows = own.shape[1]
    for e in range(own.shape[0]):
        total = (first[e] + second[e]) + (third[e] + fourth[e])
        own[e : e + 1] = total[:, :rows]
        sent[e : e + 1] = total[:, rows:]


def gate_sum_call(part):
    size = lax.axis_size("tensor")
    there = [lax.ppermute(part, "tensor", [(i, i ^ k) for i in range(size)]) for k in (1, 2, 3)]
    out = sds((part.shape[0], part.shape[2] // 2), F32)
    own, sent = kernel_call(
        gate_sum_kernel, (1,), [whole(part)] * 4, [whole(out)] * 2, [out, out], 0, 0
    )(part, *there)
    return own, to_core(sent)


def gate_join_kernel(scal, own, got, out):
    first = jnp.where(scal[1] == 0, own[...], got[...])
    second = jnp.where(scal[1] == 0, got[...], own[...])
    out[...] = jnp.concatenate([first, second]).T


def gate_join_call(scal, own, got):
    out = sds((own.shape[1], 2 * own.shape[0]), F32)
    return kernel_call(gate_join_kernel, (1,), [SCALARS, whole(own), whole(got)], whole(out), out, 0, 0)(
        scal, own, got
    )


def backward_tiles(places, tile):
    return [(p, k) for p, (_, length, _) in enumerate(places) for k in range(length // tile)]


def spread_kernel(tiles, terms, joined, *refs):
    acts, out = refs[:terms], refs[-1]
    weights = refs[terms + joined : -1]
    n = len(weights) // terms
    step = pl.program_id(0)
    for p in range(n):
        steps = [t for t, (q, _) in enumerate(tiles) if q == p]

        @pl.when((step >= steps[0]) & (step <= steps[-1]))
        def _():
            value = sum(dot(acts[k][0], weights[k * n + p][...], (1, 0)) for k in range(terms))
            if joined:
                value += refs[terms][...].astype(F32)
            out[...] = rounded(value)


def spread_call(acts_t, which, tokens, weights, places, got=None):
    _, both, hidden = acts_t.shape
    rows = both // 2
    width = sum(length for _, length, _ in places)
    tile = 256
    tiles = backward_tiles(places, tile)

    def spec(p, m):
        steps = [t for t, (q, _) in enumerate(tiles) if q == p]
        first, last = steps[0], steps[-1]
        return pl.BlockSpec((hidden, tile), lambda t: (m, jnp.clip(t, first, last) - first))

    out = pl.BlockSpec((rows, tile), lambda t: (0, t))
    return kernel_call(
        functools.partial(spread_kernel, tiles, len(which), got is not None),
        (len(tiles),),
        [
            pl.BlockSpec((1, rows, hidden), lambda t, k=k: (k, tokens, 0), pipeline_mode=pl.Buffered(1))
            for k in which
        ]
        + ([] if got is None else [out])
        + [spec(p, m) for pieces in weights for p, (_, m) in enumerate(pieces)],
        out,
        sds((rows, width), BF16),
        0,
        0,
    )(*[acts_t] * len(which), *([] if got is None else [got]), *[a for pieces in weights for a, _ in pieces])


def join_kernel(own, other, out):
    out[...] = rounded(own[...].astype(F32) + other[...].astype(F32))


def join_call(own, other):
    rows, width = own.shape
    spec = pl.BlockSpec((rows // 3, width), lambda i: (i, 0))
    return kernel_call(join_kernel, (3,), [spec, spec], spec, sds(own.shape, BF16), 0, 0)(own, other)


def weight_grad_kernel(left, first, second, *outs):
    def write(right):
        value = dot(left[0], right[...], (1, 0))
        start = 0
        for out in outs:
            length = out.shape[1]
            out[...] = rounded(value[:, start : start + length])
            start += length

    pl.when(pl.program_id(0) == 0)(lambda: write(first))
    pl.when(pl.program_id(0) > 0)(lambda: write(second))


def weight_grad_call(acts, first, second, lengths):
    _, hidden, both = acts.shape
    tile = hidden // 4
    return kernel_call(
        weight_grad_kernel,
        (3, 4),
        [pl.BlockSpec((1, tile, both), lambda m, i: (m, i, 0)), single(first.shape), single(second.shape)],
        [pl.BlockSpec((tile, n), lambda m, i: (4 * m + i, 0)) for n in lengths],
        [sds((3 * hidden, n), BF16) for n in lengths],
        0,
        0,
    )(acts, first, second)


def met_kernel(a, b, c, d, first, second):
    first[...] = rounded(a[...].astype(F32) + b[...].astype(F32))
    second[...] = rounded(c[...].astype(F32) + d[...].astype(F32))


def met_call(a, b, c, d):
    steps = 6 if a.shape[0] % 96 == 0 else 1
    left = pl.BlockSpec((a.shape[0] // steps, a.shape[1]), lambda i: (i, 0))
    return kernel_call(
        met_kernel,
        (steps,),
        [left] * 4,
        [left] * 2,
        [sds(a.shape, BF16)] * 2,
        0,
        0,
    )(a, b, c, d)


def total_kernel(scal, own, x_first, y_first, x_second, y_second, mine, sent):
    shard = mine.shape[1]
    first = own[:, :shard].astype(F32) + x_first[...].astype(F32) + y_first[...].astype(F32)
    second = own[:, shard:].astype(F32) + x_second[...].astype(F32) + y_second[...].astype(F32)
    core = scal[1]
    mine[...] = jnp.where(core == 0, first, second)
    sent[...] = rounded(jnp.where(core == 0, second, first))


def total_call(scal, own, near):
    rows, span = own.shape
    tile = rows // 12
    half = pl.BlockSpec((tile, span // 2), lambda i: (i, 0))
    return kernel_call(
        total_kernel,
        (12,),
        [SCALARS, pl.BlockSpec((tile, span), lambda i: (i, 0))] + [half] * 4,
        [half] * 2,
        [sds((rows, span // 2), F32), sds((rows, span // 2), BF16)],
        0,
        0,
    )(scal, own, *near)


def lay_kernel(scal, *refs):
    mine, got, outs = refs[:3], refs[3:6], refs[6:]

    @pl.when(pl.program_id(0) == 0)
    def _():
        for m in range(3):
            outs[m][...] = mine[m][...]

    @pl.when(pl.program_id(0) == 1)
    def _():
        for m in range(3):
            outs[m][...] = got[m][...].astype(F32)


def lay_call(scal, mine, got):
    rows, shard = mine.shape
    part = rows // 3
    return prefetch_call(
        lay_kernel,
        scal,
        (2,),
        [pl.BlockSpec((part, shard), lambda i, s, m=m: (m, 0)) for m in range(3)] * 2,
        [pl.BlockSpec((part, shard), lambda i, s: (jnp.where(i == 0, s[1], 1 - s[1]), 0))] * 3,
        [sds((2 * part, shard), F32)] * 3,
        [mine] * 3 + [got] * 3,
    )


def pair_grad_kernel(scal, left_own, left_sent, first, second, own, sent):
    inner = first.shape[1]
    own[:, :inner] = dot(left_own[...], first[...], (0, 0))
    own[:, inner:] = dot(left_own[...], second[...], (0, 0))
    sent[:, :inner] = rounded(dot(left_sent[...], first[...], (0, 0)))
    sent[:, inner:] = rounded(dot(left_sent[...], second[...], (0, 0)))


def rows_grad_call(scal, left, first, second, shard):
    rows, width = left.shape
    columns = first.shape[1] + second.shape[1]
    count = width // (2 * shard)
    return prefetch_call(
        pair_grad_kernel,
        scal,
        (count,),
        [
            pl.BlockSpec((rows, shard), lambda r, s: (0, 2 * r + s[1])),
            pl.BlockSpec((rows, shard), lambda r, s: (0, 2 * r + 1 - s[1])),
            pl.BlockSpec(first.shape, lambda r, s: (0, 0)),
            pl.BlockSpec(second.shape, lambda r, s: (0, 0)),
        ],
        [pl.BlockSpec((shard, columns), lambda r, s: (r, 0))] * 2,
        [sds((count * shard, columns), F32), sds((count * shard, columns), BF16)],
        [left, left, first, second],
    )


def columns_grad_kernel(scal, left, right_own, right_sent, own, sent, left_t):
    @pl.when(pl.program_id(0) == 0)
    def _():
        left_t[...] = left[...].T

    own[...] = dot(left_t[...], right_own[...], (1, 0))
    sent[...] = rounded(dot(left_t[...], right_sent[...], (1, 0)))


def columns_grad_call(scal, left, right, shard):
    rows, inner = left.shape
    count = right.shape[1] // (2 * shard)
    return pl.pallas_call(
        columns_grad_kernel,
        grid_spec=pltpu.PrefetchScalarGridSpec(
            num_scalar_prefetch=1,
            grid=(count,),
            in_specs=[
                pl.BlockSpec((rows, inner), lambda r, s: (0, 0)),
                pl.BlockSpec((rows, shard), lambda r, s: (0, 2 * r + s[1])),
                pl.BlockSpec((rows, shard), lambda r, s: (0, 2 * r + 1 - s[1])),
            ],
            out_specs=[pl.BlockSpec((inner, shard), lambda r, s: (0, r))] * 2,
            scratch_shapes=[pltpu.VMEM((inner, rows), BF16)],
        ),
        out_shape=[sds((inner, count * shard), F32), sds((inner, count * shard), BF16)],
        compiler_params=pltpu.CompilerParams(vmem_limit_bytes=VMEM_BYTES),
        cost_estimate=cost(columns_grad_kernel),
    )(scal, left, right, right)


def cut_kernel(axis, mine, got, *outs):
    value = rounded(mine[...] + got[...].astype(F32))
    start = 0
    for out in outs:
        length = out.shape[axis]
        out[...] = lax.slice_in_dim(value, start, start + length, axis=axis)
        start += length


def cut_call(mine, got, axis):
    eighth = mine.shape[axis] // 8
    shapes = []
    for length in [2 * eighth] + [eighth] * 6:
        shape = list(mine.shape)
        shape[axis] = length
        shapes.append(sds(tuple(shape), BF16))
    return kernel_call(
        functools.partial(cut_kernel, axis),
        (1,),
        [whole(mine), whole(got)],
        [whole(v) for v in shapes],
        shapes,
        0,
        0,
    )(mine, got)


def end_kernel(axis, own, x_first, y_first, x_second, y_second, *outs):
    value = own[...].astype(F32)
    size = x_first.shape[axis]
    first = lax.slice_in_dim(value, 0, size, axis=axis) + x_first[...].astype(F32) + y_first[...].astype(F32)
    second = lax.slice_in_dim(value, size, 2 * size, axis=axis)
    second = second + x_second[...].astype(F32) + y_second[...].astype(F32)
    value = jnp.concatenate([first, second], axis)
    start = 0
    for out in outs:
        length = out.shape[1]
        out[...] = value[:, start : start + length]
        start += length


def end_call(own, near, axis, lengths):
    outs = [sds((own.shape[0], n), F32) for n in lengths]
    return kernel_call(
        functools.partial(end_kernel, axis),
        (1,),
        [whole(own)] + [whole(v) for v in near],
        [whole(v) for v in outs],
        outs,
        0,
        0,
    )(own, *near)


def route_kernel(top_count, hid, attn_add, gain, router_t, routes, resid, moe_low, gates):
    value = hid[...].astype(F32) + attn_add[...].astype(F32)
    resid[...] = value
    moe_low[...] = rounded(value * kernel_inverse_rms(value) * gain[...])
    logits = dot(moe_low[...], router_t[...], (1, 1))
    numbers = lax.broadcasted_iota(jnp.int32, logits.shape, 1)
    chosen = routes[:, 0:1] == numbers
    for k in range(1, top_count):
        chosen = chosen | (routes[:, k : k + 1] == numbers)
    top = jnp.max(jnp.where(chosen, logits, HIDE), -1, keepdims=True)
    lift = jnp.where(chosen, jnp.exp(jnp.where(chosen, logits, top) - top), 0.0)
    gates[...] = lift / jnp.sum(lift, -1, keepdims=True)


def row_specs(arrays, rows, tile):
    return [
        pl.BlockSpec((tile, a.shape[1]), lambda i: (i, 0)) if a.shape[0] == rows else whole(a) for a in arrays
    ]


def route_call(hid, attn_add, gain, router_t, routes):
    rows, width = hid.shape
    tile = rows // 3
    arrays = (hid, attn_add, gain, router_t, routes)
    outs = [sds((rows, width), F32), sds((rows, width), BF16), sds((rows, router_t.shape[0]), F32)]
    return kernel_call(
        functools.partial(route_kernel, routes.shape[1]),
        (3,),
        row_specs(arrays, rows, tile),
        row_specs(outs, rows, tile),
        outs,
        40 * rows * width,
        10 * rows * width,
    )(*arrays)


def route_back_kernel(
    grad_moe, gate_grads, gates, resid, cot, router_t, gain, grad_resid, resid_low, grad_logits, grad_gain
):
    chosen = gates[...]
    part = gate_grads[...]
    middle = jnp.sum(chosen * part, -1, keepdims=True)
    grad_logits[...] = rounded(chosen * (part - middle))
    total = grad_moe[...].astype(F32) + dot(grad_logits[...], router_t[...], (1, 0))
    value = resid[...]
    shrink = kernel_inverse_rms(value)
    normal = value * shrink

    @pl.when(pl.program_id(0) == 0)
    def _():
        grad_gain[...] = jnp.zeros(grad_gain.shape, F32)

    grad_gain[...] += jnp.sum(total * normal, 0, keepdims=True)
    scaled = total * gain[...]
    mean = jnp.mean(scaled * normal, axis=-1, keepdims=True)
    out = cot[...].astype(F32) + shrink * (scaled - normal * mean)
    grad_resid[...] = out
    resid_low[...] = rounded(out)


def route_back_call(grad_moe, gate_grads, gates, resid, cot, router_t, gain):
    rows, width = resid.shape
    tile = rows // 3
    arrays = (grad_moe, gate_grads, gates, resid, cot, router_t, gain)
    outs = [
        sds((rows, width), F32),
        sds((rows, width), BF16),
        sds(gates.shape, BF16),
        sds((1, width), F32),
    ]
    return kernel_call(
        route_back_kernel,
        (3,),
        row_specs(arrays, rows, tile),
        row_specs(outs, rows, tile),
        outs,
        50 * rows * width,
        14 * rows * width,
    )(*arrays)


def to_whole_order(scal, blocks, value, out):
    span = value.shape[1] // blocks
    for j in range(blocks):
        target = pl.multiple_of((scal[0] ^ j) * span, span)
        out[:, pl.ds(target, span)] = value[:, j * span : (j + 1) * span]


def add_kernel(blocks, scal, first, second, out):
    value = rounded(first[...] + second[...].astype(F32))
    to_whole_order(scal, blocks, value, out)


def add_call(scal, resid, part, blocks):
    rows, width = part.shape
    return prefetch_call(
        functools.partial(add_kernel, blocks),
        scal,
        (1,),
        [pl.BlockSpec((rows, width), lambda i, s: (s[2], 0)), pl.BlockSpec((rows, width), lambda i, s: (0, 0))],
        pl.BlockSpec((rows, width), lambda i, s: (0, 0)),
        sds((rows, width), BF16),
        [resid, part],
    )


def last_kernel(blocks, scal, hid, grad_resid, grad_normed, gain, out, wide):
    wide[...] = hid[...].astype(F32)
    rows = out.shape[0]
    tokens = wide[pl.ds(pl.multiple_of(scal[2] * rows, 8), rows)]
    shrink = kernel_inverse_rms(tokens)
    normal = tokens * shrink
    scaled = grad_normed[...].astype(F32) * gain[...]
    middle = jnp.mean(scaled * normal, axis=-1, keepdims=True)
    value = rounded(grad_resid[...] + shrink * (scaled - normal * middle))
    to_whole_order(scal, blocks, value, out)


def last_call(scal, hid, grad_resid, grad_normed, gain, blocks):
    rows, width = grad_normed.shape
    part = pl.BlockSpec((rows, width), lambda i, s: (0, 0))
    return prefetch_call(
        functools.partial(last_kernel, blocks),
        scal,
        (1,),
        [whole(hid), pl.BlockSpec((rows, width), lambda i, s: (s[2], 0)), part, whole(gain)],
        part,
        sds((rows, width), BF16),
        [hid, grad_resid, grad_normed, gain],
        [pltpu.VMEM(hid.shape, F32)],
    )


def angle_tables(positions):
    half_size = HEAD // 2
    frequency = jnp.exp(jnp.arange(half_size, dtype=F32) * (-2.0 * math.log(THETA) / HEAD))
    angles = positions.astype(F32)[..., None] * frequency
    sine = jnp.sin(angles)
    cosine = jnp.cos(angles)
    return jnp.concatenate([cosine, cosine], -1), jnp.concatenate([-sine, sine], -1)


def lookup_parent(segment_ids, parent):
    seg_table = jnp.arange(parent.shape[-1], dtype=jnp.int32)
    return jnp.sum(jnp.where(segment_ids[..., None] == seg_table, parent, 0), -1)


def shards(
    hidden,
    cotangent,
    gain_attn,
    query_weight,
    key_weight,
    value_weight,
    gain_query,
    gain_key,
    out_weight,
    gain_moe,
    router_weight,
    gate_weight,
    up_weight,
    down_weight,
    segment,
    parent,
    tree_depth,
    routes,
):
    _, rows, width = hidden.shape
    dp, x, core = place()
    ctx = lax.axis_index("ctx")
    count = lax.axis_size("dp")
    paired = count == 2
    chips = 2 * count
    tensor = lax.axis_size("tensor")
    heads = HEADS_Q // tensor
    shard = query_weight.shape[0]
    span = 2 * shard
    inner = heads * HEAD
    columns = inner + 2 * HEAD
    half = EXPERTS // 2
    hid = down_weight.shape[1]
    scal = jnp.stack([flips(), core, lax.axis_index("tensor")]).astype(jnp.int32)
    hidden_rows = half * hid

    def by_core(own, other, axis):
        return jnp.where(core == 0, jnp.stack([own, other], axis), jnp.stack([other, own], axis))

    def five_places(size):
        starts = [0, span, 2 * span, 3 * span, 3 * span + size // 2]
        return list(zip(starts, [size, size, size, size // 2, size // 2], [0] * 5))

    def both_cores(own, size):
        return own + [to_core(a) for a in own], [(s, n, k) for k in (1, 2) for s, n, _ in five_places(size)]

    def whole_piece(block, axis):
        own = gather_whole(block, axis)
        cut = own.shape[:axis] + (chips, shard) + own.shape[axis + 1 :]
        full = by_core(own.reshape(cut), to_core(own).reshape(cut), axis + 1)
        return [full.reshape(own.shape[:axis] + (width,) + own.shape[axis + 1 :])], [(0, width, 0)]

    per = gain_query.shape[0]
    heads_column = jnp.pad(jnp.concatenate([gain_query, gain_key]), (0, shard - 2 * per))
    small = [router_weight, gain_attn[:, None], gain_moe[:, None], heads_column[:, None]]
    small.append(jnp.zeros((shard, HEAD - EXPERTS - 3), BF16))
    qkv_shard = jnp.concatenate([query_weight, key_weight, value_weight] + small, 1)
    expert_weights = [down_weight, gate_weight.transpose(0, 2, 1), up_weight.transpose(0, 2, 1)]
    if paired:
        qkv_x, qkv_y = exchange(qkv_shard, qkv_shard)
        far_second, far_first = exchange(halves(qkv_y, 0)[1], halves(qkv_x, 0)[0])
        expert_got = to_core(other_half_call(after(scal, qkv_x), expert_weights))
        expert_block = block_call(scal, expert_weights, expert_got)
        qkv_pieces, qkv_places = both_cores([qkv_shard, qkv_x, qkv_y, far_first, far_second], shard)
        out_x, out_y = exchange(out_weight, out_weight, far_first, far_second)
        out_far_second, out_far_first = exchange(halves(out_y, 1)[1], halves(out_x, 1)[0])
        out_pieces, out_places = both_cores([out_weight, out_x, out_y, out_far_first, out_far_second], shard)
        gains = ()
    else:
        qkv_pieces, qkv_places = whole_piece(qkv_shard, 0)
        small_t = qkv_pieces[0][:, columns:].T
        router_t = small_t[:EXPERTS]
        gain_one, gain_two = (small_t[EXPERTS + i][None].astype(F32) for i in range(2))
        gain_heads = relative(small_t[EXPERTS + 2]).reshape(2 * chips, shard).astype(F32)
        gain_q = gain_heads[:, :per].reshape(1, HEAD)
        gain_k = gain_heads[:, per : 2 * per].reshape(1, HEAD)
        gains = (gain_one, gain_q, gain_k)
        out_pieces, out_places = whole_piece(out_weight, 1)
        sent = [lax.dynamic_slice_in_dim(w, (1 - core) * half, half, 0) for w in expert_weights]
        own = [lax.dynamic_slice_in_dim(w, core * half, half, 0) for w in expert_weights]
        expert_block = by_core(jnp.stack(own), to_core(jnp.stack(sent)), 3).reshape(3 * hidden_rows, span)

    cosine, sine = angle_tables(tree_depth[0])
    *found, normed, tokens_low, raw, rot = qkv_call(
        scal, hidden[0], gains, cosine, sine, qkv_pieces, qkv_places, shard, per, chips, columns
    )
    if found:
        gain_one, gain_two, router_t, gain_q, gain_k = found
    key_value = rot[:, inner:]
    kv_x = to_x(key_value)
    kv_other = to_core(key_value)
    kv_all = jnp.concatenate([key_value, kv_other, kv_x, to_core(kv_x)])
    if paired:
        near_x, near_y = exchange(expert_block, expert_block, kv_x, out_far_first)
        forwarded, expert_pieces = [], []
        gate = ()
        for m in range(3):
            rows_of = slice(m * hidden_rows, (m + 1) * hidden_rows)
            forwarded.append((near_y[rows_of, shard:], near_x[rows_of, :shard]))
            far_second, far_first = exchange(*forwarded[-1], *gate)
            gate = (far_first, far_second)
            expert_pieces.append([(expert_block, m), (near_x, m), (near_y, m), (far_first, 0), (far_second, 0)])
        expert_places = five_places(span)
    else:
        gathered = gather_whole(expert_block, 1)
        expert_pieces = [[(gathered, m)] for m in range(3)]
        expert_places = [(0, width, 0)]
    down_pieces, gate_pieces, up_pieces = expert_pieces

    seg = segment[0].reshape(2, 2, rows)
    seg_rel = flip(flip(seg, 0, x), 1, core).reshape(4 * rows)
    position = jnp.arange(4 * rows, dtype=jnp.int32).reshape(2, 2, rows)
    key_pos = flip(flip(position, 0, x), 1, core).reshape(4 * rows)
    first_up = lookup_parent(seg_rel[:rows], parent[0])
    second_up = lookup_parent(first_up, parent[0])
    key_side = jnp.stack([seg_rel, key_pos], 1)
    query_side = jnp.stack([seg_rel[:rows], first_up, second_up, key_pos[:rows]])

    mixed_low, inverse = attend_call(rot, kv_all, key_side, query_side, heads)
    attn_part = project_call(scal, mixed_low, out_pieces, out_places, shard, width)
    attn_add = lax.psum(attn_part, "tensor")

    cot = permute_width(cotangent[0], scal, chips)
    cot_other = to_core(cot)
    grad_act, pair_dy = products_call(cot, cot_other, down_pieces, hidden_rows)
    if paired:
        attn_add = after(attn_add, down_pieces[3][0], down_pieces[4][0])
    resid, moe_low, gates = route_call(tokens_low, attn_add, gain_two, router_t, routes[0])
    moe_other = to_core(moe_low)
    gate_pre, pair_x = products_call(moe_low, moe_other, gate_pieces, hidden_rows)
    gates_t = gates.T
    gates_own = lax.dynamic_slice_in_dim(gates_t, core * half, half, 0)
    gates_sent = lax.dynamic_slice_in_dim(gates_t, (1 - core) * half, half, 0)
    gate_pair = jnp.concatenate([gates_own, to_core(gates_sent)], 1)[:, None, :]

    acts, acts_t, gate_part = experts_call(pair_x, gate_pre, grad_act, gate_pair, up_pieces, hid)
    weights = [gate_pieces, up_pieces]
    part_other = to_core(spread_call(acts_t, (1, 2), 1, weights, expert_places))
    moe_sum = spread_call(acts_t, (1, 2), 0, weights, expert_places, part_other)
    grad_moe_in = lax.psum(moe_sum, "tensor")
    acts, acts_t, gate_part = lax.optimization_barrier((acts, acts_t, gate_part, moe_sum))[:3]
    gate_grads = gate_join_call(scal, *gate_sum_call(gate_part))

    lengths = [span] + [shard] * 6 if paired else [span] * chips
    grad_blocks = weight_grad_call(acts, pair_dy, pair_x, lengths)
    acts_t = after(acts_t, grad_blocks[0])
    grad_moe_in = after(grad_moe_in, grad_blocks[0])
    if paired:
        own_grads, x_first, x_second, y_first, y_second, far_first, far_second = grad_blocks
        far_x, far_y = exchange(far_first, far_second)
        x_first, y_second = exchange(x_first, y_second)
        grad_moe_in = after(grad_moe_in, far_x, far_y)
    out_other = to_core(spread_call(acts_t, (0,), 1, [down_pieces], expert_places))
    out_sum = join_call(spread_call(acts_t, (0,), 0, [down_pieces], expert_places), out_other)
    grad_moe_in = after(grad_moe_in, out_sum)
    out_sum = after(out_sum, grad_moe_in, gate_grads)
    moe_add = lax.psum_scatter(out_sum, "tensor", scatter_dimension=0, tiled=True)

    grad_resid, resid_low, grad_logits, grad_gain_two = route_back_call(
        grad_moe_in, gate_grads, gates, resid, cot, router_t, gain_two
    )

    grad_mixed = project_back_call(scal, after(resid_low, out_sum), out_pieces, out_places, shard, inner)
    query_back, kv_own, kv_sent, kv_mid, grad_gain_q = attend_back_call(
        rot, kv_all, key_side, query_side, grad_mixed, mixed_low, inverse, raw, cosine, sine, gain_q, heads
    )
    output_rows = add_call(after(scal, query_back), resid, moe_add, chips)
    output = lax.all_gather(output_rows, "tensor", axis=0, tiled=True)[None]
    if paired:
        kv_mid = after(kv_mid, x_first, y_second)
    kv_part, kv_on = kv_pass_call(kv_own, after(kv_mid, output_rows), to_core(kv_sent))
    kv_far = to_x(kv_on)
    if paired:
        x_second, y_first = lax.optimization_barrier(met_call(after(x_second, kv_on), far_y, y_first, far_x))
        kv_part = after(kv_part, x_second)
        x_second, y_first = lax.optimization_barrier((to_x(x_second), to_dp(y_first)))
        near_grads = (x_first, y_first, x_second, y_second)
    back_part, grad_gain_one, kv_back, grad_gain_k = qkv_back_call(
        scal, query_back, kv_part, kv_far, raw, cosine, sine, gain_k, tokens_low, qkv_pieces, qkv_places, shard
    )
    grad_normed = lax.psum_scatter(back_part, "tensor", scatter_dimension=0, tiled=True)
    late_resid, late_mixed, late_normed, late_moe = lax.optimization_barrier(
        (resid_low, mixed_low, normed, moe_low, back_part)
    )[:4]
    grad_router_t = dot(grad_logits, late_moe, (0, 0))
    if paired:
        mine, sent = total_call(scal, own_grads, near_grads)
        late_normed = after(late_normed, mine)
        qkv_mine, qkv_sent = rows_grad_call(scal, late_normed, query_back, kv_back, shard)
        out_mine, out_sent = columns_grad_call(scal, late_mixed, late_resid, shard)
        qkv_blocks = cut_call(qkv_mine, to_core(qkv_sent), 0)
        out_blocks = cut_call(out_mine, to_core(out_sent), 1)

        def plane_sum(blocks, axis, lengths):
            own, x_first, x_second, y_first, y_second, far_first, far_second = blocks
            far_x, far_y = exchange(far_first, far_second)
            x_first, y_second = exchange(x_first, y_second)
            x_second, y_first = met_call(x_second, far_y, y_first, far_x)
            x_second, y_first = exchange(x_second, y_first)
            near = (x_first, y_first, x_second, y_second)
            return end_call(own, near, axis, lengths)

        grad_query, grad_key, grad_value = plane_sum(qkv_blocks, 0, [inner, HEAD, HEAD])
        (grad_out_weight,) = plane_sum(out_blocks, 1, [shard])
    else:
        qkv_back = jnp.concatenate([query_back, kv_back], 1)
        sides = [
            (pick_columns(late_normed, scal, shard, o), pick_columns(late_resid, scal, shard, o))
            for o in (False, True)
        ]
        qkv_mine, qkv_sent = (dot(n, qkv_back, (0, 0)) for n, _ in sides)
        out_mine, out_sent = (dot(late_mixed, r, (0, 0)) for _, r in sides)
        qkv_sum = rounded(qkv_mine + to_core(rounded(qkv_sent)).astype(F32))
        out_sum = rounded(out_mine + to_core(rounded(out_sent)).astype(F32))
        grad_qkv = scatter_whole([qkv_sum[r * shard : (r + 1) * shard] for r in range(chips)])
        grad_query, grad_key, grad_value = jnp.split(grad_qkv, [inner, inner + HEAD], 1)
        grad_out_weight = scatter_whole([out_sum[:, r * shard : (r + 1) * shard] for r in range(chips)])
        total = scatter_whole(grad_blocks)
        mine = lax.dynamic_slice_in_dim(total, core * shard, shard, 1)
        sent = rounded(lax.dynamic_slice_in_dim(total, (1 - core) * shard, shard, 1))
    grad_down, grad_gate, grad_up = (
        v.reshape(EXPERTS, hid, shard) for v in lay_call(scal, mine, to_core(sent))
    )
    grad_gate, grad_up = grad_gate.transpose(0, 2, 1), grad_up.transpose(0, 2, 1)

    if paired:
        grad_normed = after(grad_normed, qkv_sent)
    hidden_rows_out = last_call(scal, tokens_low, grad_resid, grad_normed, gain_one, chips)
    grad_hidden = lax.all_gather(hidden_rows_out, "tensor", axis=0, tiled=True)[None]

    share = 1.0 / tensor
    head_rows = jnp.concatenate(
        [grad_gain_q.reshape(2 * chips, per), grad_gain_k.reshape(2 * chips, per)], 1
    )
    head_rows = relative(jnp.pad(head_rows, ((0, 0), (0, shard - 2 * per))).reshape(width))
    table = jnp.concatenate(
        [
            grad_gain_one,
            grad_gain_two * share,
            grad_router_t * share,
            head_rows[None],
            jnp.zeros((5, width), F32),
        ]
    ).reshape(24, chips, 2, shard)
    table_own = lax.dynamic_index_in_dim(table, core, 2, keepdims=False)
    table_sent = lax.dynamic_index_in_dim(table, 1 - core, 2, keepdims=False)
    table = table_own + to_core(table_sent)
    table = table.reshape(24, count, 2, shard)
    table = table[:, :, 0] + to_x(table[:, :, 1])
    if paired:
        table = table[:, 0] + to_dp(table[:, 1])
    else:
        table = lax.psum_scatter(table, "dp", scatter_dimension=1, tiled=False)
    mine = sum_z(table)
    gains = mine[2 + EXPERTS, : 2 * per]

    return (
        output,
        grad_hidden,
        mine[0],
        grad_query,
        grad_key,
        grad_value,
        gains[:per],
        gains[per:],
        grad_out_weight,
        mine[1],
        mine[2 : 2 + EXPERTS].T,
        grad_gate,
        grad_up,
        grad_down,
    )


def solution(mesh):
    plane = ("dp", "ctx")
    in_specs = (
        P("dp", "ctx", None),
        P("dp", "ctx", None),
        P(plane),
        P(plane, "tensor"),
        P(plane, "tensor"),
        P(plane, "tensor"),
        P(plane),
        P(plane),
        P("tensor", plane),
        P(plane),
        P(plane, None),
        P(None, plane, "tensor"),
        P(None, plane, "tensor"),
        P(None, "tensor", plane),
        P("dp", None),
        P("dp", None),
        P("dp", "ctx"),
        P("dp", "ctx", None),
    )
    out_specs = (
        P("dp", "ctx", None),
        P("dp", "ctx", None),
        P(plane),
        P(plane, "tensor"),
        P(plane, "tensor"),
        P(plane, "tensor"),
        P(plane),
        P(plane),
        P("tensor", plane),
        P(plane),
        P(plane, None),
        P(None, plane, "tensor"),
        P(None, plane, "tensor"),
        P(None, "tensor", plane),
    )
    return jax.shard_map(shards, mesh=mesh, in_specs=in_specs, out_specs=out_specs, check_vma=False)
```
